32 devices in a mesh: ctx: 16 (over z, x, core), fsdp: 2 (over y).
Axes of the slice: x: 2, y: 2, z: 4, core: 2. Of those that a mesh axis runs over, the one named last changes fastest.
Arguments:
- layer_input: bfloat16 [4096, 2, 768], P('ctx', 'fsdp'), may hold values from -6 to 6
- teacher_states: bfloat16 [4096, 2, 768], P('ctx', 'fsdp'), may hold values from -9 to 9
- seq_lengths: int32 [2], P('fsdp'), may hold values from 1024 to 4096, as said below
- query_weight: bfloat16 [768, 768], P('fsdp'), may hold values from -0.21875 to 0.21875
- query_bias: bfloat16 [768], P('fsdp'), may hold values from -3 to 3
- key_weight: bfloat16 [768, 768], P('fsdp'), may hold values from -0.21875 to 0.21875
- value_weight: bfloat16 [768, 768], P('fsdp'), may hold values from -0.21875 to 0.21875
- value_bias: bfloat16 [768], P('fsdp'), may hold values from -0.119628906 to 0.119628906
- out_weight: bfloat16 [768, 768], P('fsdp'), may hold values from -12 to 12
- out_bias: bfloat16 [768], P('fsdp'), may hold values from -3 to 3
- attn_gain: bfloat16 [768], P('fsdp'), may hold values from 0.5 to 1.5
- attn_shift: bfloat16 [768], P('fsdp'), may hold values from -1.796875 to 1.796875
- inner_weight: bfloat16 [768, 3072], P('fsdp'), may hold values from -0.21875 to 0.21875
- inner_bias: bfloat16 [3072], P('fsdp'), may hold values from -3 to 3
- outer_weight: bfloat16 [3072, 768], P('fsdp'), may hold values from -0.109375 to 0.109375
- outer_bias: bfloat16 [768], P('fsdp'), may hold values from -1.796875 to 1.796875
- final_gain: bfloat16 [768], P('fsdp'), may hold values from 0.5 to 1.5
- final_shift: bfloat16 [768], P('fsdp'), may hold values from -1.796875 to 1.796875
Outputs:
- distill_loss: float32 [], replicated
- layer_output: float32 [4096, 2, 768], P('ctx', 'fsdp')
- input_grad: float32 [4096, 2, 768], P('ctx', 'fsdp')
- query_weight_grad: float32 [768, 768], P('fsdp')
- query_bias_grad: float32 [768], P('fsdp')
- key_weight_grad: float32 [768, 768], P('fsdp')
- value_weight_grad: float32 [768, 768], P('fsdp')
- value_bias_grad: float32 [768], P('fsdp')
- out_weight_grad: float32 [768, 768], P('fsdp')
- out_bias_grad: float32 [768], P('fsdp')
- attn_gain_grad: float32 [768], P('fsdp')
- attn_shift_grad: float32 [768], P('fsdp')
- inner_weight_grad: float32 [768, 3072], P('fsdp')
- inner_bias_grad: float32 [3072], P('fsdp')
- outer_weight_grad: float32 [3072, 768], P('fsdp')
- outer_bias_grad: float32 [768], P('fsdp')
- final_gain_grad: float32 [768], P('fsdp')
- final_shift_grad: float32 [768], P('fsdp')
The draws below stay inside these ranges and needn't reach their ends.
Inputs may be any that keep to these rules, and one draw needn't show every extreme that they name: `seq_lengths`: at least one of the 2 sequences has all 4096 tokens valid; in each group of 1 sequence on one index of fsdp, one has more than 3840 valid tokens.
All inputs are finite; a program needn't handle non-finite values.
Results may differ from the reference program's by a relative error of at most 0.013.
Values may be sent and summed in bfloat16 or wider, within the bound.
No kernel may reach another device: no remote copies, remote signals or barrier semaphores. Data moves between devices by JAX's collectives and lax.ppermute only.
A program may use at most 192 MiB of HBM per device.

```python
import math
import jax
import jax.numpy as jnp
from jax import lax

H = 12
FF = 3072
D = 768
SEG = 256
SEQ_GRP = 1
LENGTH = 4096
SEQS = 2


def draw_teacher_states(key, part):
    noise_key = jax.random.fold_in(key, 0)
    position = jnp.arange(LENGTH, dtype=jnp.float32).reshape(LENGTH, 1, 1) / LENGTH
    base = jnp.clip(jax.random.normal(noise_key, (LENGTH, SEQS, D), jnp.float32), -6.0, 6.0)
    return (base * (0.5 + position)).astype(jnp.bfloat16)


def draw_seq_lengths(key, part):
    short_key, full_key, pick_key, near_key, slot_key = jax.random.split(key, 5)
    group_count = SEQS // SEQ_GRP
    shorter = jax.random.randint(short_key, (SEQS,), LENGTH // 4, LENGTH)
    keep_full = jax.random.randint(full_key, (SEQS,), 0, 2) == 1
    near_end = jax.random.randint(near_key, (SEQS,), LENGTH - SEG + 1, LENGTH + 1)
    slot_pick = jax.random.randint(slot_key, (group_count,), 0, SEQ_GRP)
    seq_index = jnp.arange(SEQS, dtype=jnp.int32)
    group_slot = jnp.sum(jnp.where((seq_index // SEQ_GRP)[:, None] == jnp.arange(group_count, dtype=jnp.int32)[None, :], slot_pick[None, :], 0), axis=1)
    reaching = seq_index % SEQ_GRP == group_slot
    chosen = jax.random.randint(pick_key, (1,), 0, SEQS)
    forced = seq_index == chosen
    others = jnp.where(keep_full, LENGTH, shorter)
    return jnp.where(forced, LENGTH, jnp.where(reaching, near_end, others)).astype(jnp.int32)


def shard_levels(own_key, extent, cuts, smallest, high):
    def one(dim, shards_of):
        heights = jax.random.uniform(jax.random.fold_in(jax.random.fold_in(own_key, 6), dim), (shards_of,), jnp.float32, smallest / len(cuts), high / len(cuts))
        return jnp.repeat(jnp.exp(heights), extent[dim] // shards_of).reshape((-1,) + (1,) * (len(extent) - dim - 1))

    gain = one(*cuts[0])
    for cut in cuts[1:]:
        gain = gain * one(*cut)
    return gain


def bell_draw(own_key, shape, spread, most, cuts=(), kind=jnp.bfloat16):
    entries = jax.random.normal(own_key, shape, jnp.float32) * spread
    if len(cuts) > 0:
        entries = shard_levels(own_key, shape, cuts, -0.22, 0.18) * entries
    return jnp.clip(entries, min=-most, max=most).astype(kind)


def setup_inputs(seed: int = 0) -> dict:
    splits = jax.random.split(jax.random.key(seed), 19)
    return {
        "layer_input": bell_draw(splits[0], (LENGTH, SEQS, D), 1.0, 6.0, ((0, 16), (1, 2))),
        "teacher_states": draw_teacher_states(jax.random.fold_in(splits[18], 71), 0),
        "seq_lengths": draw_seq_lengths(jax.random.fold_in(splits[18], 71), 0),
        "query_weight": bell_draw(splits[3], (D, D), D ** -0.5, 0.21875, ((0, 2),)),
        "query_bias": bell_draw(splits[4], (D,), 0.5, 3.0, ((0, 2),)),
        "key_weight": bell_draw(splits[5], (D, D), D ** -0.5, 0.21875, ((0, 2),)),
        "value_weight": bell_draw(splits[6], (D, D), D ** -0.5, 0.21875, ((0, 2),)),
        "value_bias": bell_draw(splits[7], (D,), 0.02, 0.119628906, ((0, 2),)),
        "out_weight": bell_draw(splits[8], (D, D), 2.0, 12.0, ((0, 2),)),
        "out_bias": bell_draw(splits[9], (D,), 0.5, 3.0, ((0, 2),)),
        "attn_gain": jnp.clip(1.0 + 0.1 * jax.random.normal(splits[10], (D,), jnp.float32), 0.5, 1.5).astype(jnp.bfloat16),
        "attn_shift": bell_draw(splits[11], (D,), 0.3, 1.796875, ((0, 2),)),
        "inner_weight": bell_draw(splits[12], (D, FF), D ** -0.5, 0.21875, ((0, 2),)),
        "inner_bias": bell_draw(splits[13], (FF,), 0.5, 3.0, ((0, 2),)),
        "outer_weight": bell_draw(splits[14], (FF, D), FF ** -0.5, 0.109375, ((0, 2),)),
        "outer_bias": bell_draw(splits[15], (D,), 0.3, 1.796875, ((0, 2),)),
        "final_gain": jnp.clip(1.0 + 0.1 * jax.random.normal(splits[16], (D,), jnp.float32), 0.5, 1.5).astype(jnp.bfloat16),
        "final_shift": bell_draw(splits[17], (D,), 0.3, 1.796875, ((0, 2),)),
    }


@jax.custom_vjp
def low(v):
    return lax.optimization_barrier(v.astype(jnp.bfloat16)).astype(jnp.float32)

@jax.custom_vjp
def low_back(v):
    return v

def low_keep(v):
    return (low(v), None)

def low_pass(kept, grad):
    return (grad,)

def back_keep(v):
    return (v, None)

def back_low(kept, grad):
    return (low(grad),)
low.defvjp(low_keep, low_pass)
low_back.defvjp(back_keep, back_low)
norm_eps = 1e-12
log_two = math.log(2.0)
masked_score = -1e+30
highest = lax.Precision.HIGHEST

def layer_norm(hidden, norm_gain, norm_shift):
    centre = hidden - lax.optimization_barrier(jnp.mean(hidden, axis=-1, keepdims=True))
    inverse = lax.rsqrt(lax.optimization_barrier(jnp.mean(centre * centre, axis=-1, keepdims=True)) + norm_eps)
    return centre * inverse * norm_gain + norm_shift

def sequence_terms(params, inputs, targets, length, factor):
    w_query, b_query, w_key, w_value, b_value, w_out, b_out, g_attn, s_attn, w_inner, b_inner, w_outer, b_outer, g_final, s_final = params
    head_size = D // H
    score_scale = 1.0 / (log_two * math.sqrt(head_size))
    queries = low(low_back(jnp.dot(inputs, w_query, precision=highest) + b_query))
    key_proj = low(low_back(jnp.dot(inputs, w_key, precision=highest)))
    value_proj = low(low_back(jnp.dot(inputs, w_value, precision=highest) + b_value))
    key_heads = key_proj.reshape(LENGTH, H, head_size)
    value_heads = value_proj.reshape(LENGTH, H, head_size)
    key_valid = jnp.arange(LENGTH) < length
    block_rows = math.gcd(LENGTH, 512)

    def attend(query_block):
        query_heads = query_block.reshape(block_rows, H, head_size)
        raw_scores = jnp.einsum('qhe,khe->hqk', query_heads, key_heads, precision=highest)
        scores = jnp.where(key_valid, low_back(raw_scores * score_scale), masked_score)
        row_top = jnp.floor(lax.optimization_barrier(jnp.max(scores, axis=-1, keepdims=True)))
        exp_weights = jnp.exp2(scores - row_top)
        row_total = lax.optimization_barrier(jnp.sum(exp_weights, axis=-1))
        numerator = low_back(jnp.einsum('hqk,khe->qhe', low(exp_weights), value_heads, precision=highest))
        context = numerator / jnp.transpose(row_total)[:, :, None]
        return low(low_back(context.reshape(block_rows, D)))
    context = lax.map(jax.checkpoint(attend), queries.reshape(LENGTH // block_rows, block_rows, D)).reshape(LENGTH, D)
    attn_out = low_back(jnp.dot(context, w_out, precision=highest) + b_out)
    normed = layer_norm(inputs + attn_out, g_attn, s_attn)
    hidden_pre = low_back(jnp.dot(low(normed), w_inner, precision=highest) + b_inner)
    activated = low(jax.nn.gelu(hidden_pre, approximate=False))
    branch = low_back(jnp.dot(activated, w_outer, precision=highest) + b_outer)
    output = layer_norm(normed + branch, g_final, s_final)
    valid = (jnp.arange(LENGTH) < length).astype(jnp.float32)[:, None]
    mismatch = output - targets
    squares = jnp.sum(valid * mismatch * mismatch)
    return (squares * factor, (squares, output))

def reference(layer_input, teacher_states, seq_lengths, query_weight, query_bias, key_weight, value_weight, value_bias, out_weight, out_bias, attn_gain, attn_shift, inner_weight, inner_bias, outer_weight, outer_bias, final_gain, final_shift):
    params = tuple((p.astype(jnp.float32) for p in (query_weight, query_bias, key_weight, value_weight, value_bias, out_weight, out_bias, attn_gain, attn_shift, inner_weight, inner_bias, outer_weight, outer_bias, final_gain, final_shift)))
    valid_count = jnp.sum(seq_lengths).astype(jnp.float32)
    factor = LENGTH * SEQS / valid_count
    inputs = jnp.transpose(layer_input, (1, 0, 2)).astype(jnp.float32)
    targets = jnp.transpose(teacher_states, (1, 0, 2)).astype(jnp.float32)

    def one_sequence(grad_sums, scan_items):
        inputs_one, targets_one, length = scan_items

        def loss_of(inputs_in, params_in):
            return sequence_terms(params_in, inputs_in, targets_one, length, factor)
        scaled_loss, pullback, aux_terms = jax.vjp(loss_of, inputs_one, params, has_aux=True)
        grad_input, grad_params = pullback(jnp.ones_like(scaled_loss))
        grad_sums = jax.tree.map(jnp.add, grad_sums, grad_params)
        return (grad_sums, (aux_terms[0], aux_terms[1], grad_input))
    zero_grads = jax.tree.map(jnp.zeros_like, params)
    gradients, (squares, outputs, grad_inputs) = lax.scan(one_sequence, zero_grads, (inputs, targets, seq_lengths))
    distill_loss = jnp.sum(squares) / (D * valid_count)
    return (distill_loss, jnp.transpose(outputs, (1, 0, 2)), jnp.transpose(grad_inputs, (1, 0, 2)), gradients[0], gradients[1], gradients[2], gradients[3], gradients[4], gradients[5], gradients[6], gradients[7], gradients[8], gradients[9], gradients[10], gradients[11], gradients[12], gradients[13], gradients[14])
```

```python
from functools import partial
import math

import jax
import jax.numpy as jnp
from jax import lax
from jax.experimental import pallas as pl
from jax.experimental.pallas import tpu as pltpu
from jax.sharding import PartitionSpec as P

H = 12
head_size = 64
head_splits = 4
norm_eps = 1e-12
log_two = math.log(2.0)
masked_score = -1e30
low_type = jnp.bfloat16
wide_type = jnp.float32
score_scale = 1.0 / (log_two * math.sqrt(head_size))
vmem_bytes = 56 * 1024 * 1024

plain_dims = (((1,), (0,)), ((), ()))
back_dims = (((1,), (1,)), ((), ()))
weight_dims = (((0,), (0,)), ((), ()))


def product(left_op, right_op, dims=plain_dims):
    return lax.dot_general(left_op, right_op, dims, preferred_element_type=wide_type)


def layer_norm(hidden, norm_gain, norm_shift):
    centre = hidden - jnp.mean(hidden, axis=-1, keepdims=True)
    inverse = lax.rsqrt(jnp.mean(centre * centre, axis=-1, keepdims=True) + norm_eps)
    return centre * inverse * norm_gain + norm_shift


def gelu_exact(hidden_pre):
    return jax.nn.gelu(hidden_pre, approximate=False)


def lanes_of(shape):
    return lax.broadcasted_iota(jnp.int32, shape, 1)


def attend_kernel(head_count, key_rows, q_ref, kv_ref, aug_ref, low_ref, wide_ref, stat_ref):
    rows = q_ref.shape[0]
    length = kv_ref.shape[0]
    lane = lanes_of((rows, 128))
    q_aug = jnp.where(lane == 0, 1.0, 0.0).astype(low_type)
    stats = jnp.zeros((rows, 128), wide_type)
    outs = []
    for head in range(head_count):
        cols = pl.ds(head * 128, 128)
        q_ext = jnp.concatenate([q_ref[:, cols], q_aug], axis=1)
        top = None
        for start in range(0, length, key_rows):
            part = pl.ds(start, key_rows)
            kv_ext = jnp.concatenate([kv_ref[part, cols], aug_ref[part, :]], axis=1)
            scores = product(q_ext, kv_ext, back_dims)
            new_top = jnp.floor(jnp.max(scores, axis=1, keepdims=True))
            if top is not None:
                new_top = jnp.maximum(top, new_top)
            weights = jnp.exp2(scores - new_top).astype(low_type)
            part_sum = product(weights, kv_ext)
            if top is None:
                accum = part_sum
            else:
                accum = accum * jnp.exp2(top - new_top) + part_sum
            top = new_top
        total = accum[:, 129:130]
        outs.append(accum[:, :128] / total)
        stats = jnp.where(lane == head, top, stats)
        stats = jnp.where(lane == head_count + head, total, stats)
    tiles = []
    for head in range(0, head_count, 2):
        first = pltpu.roll(outs[head], 64, 1)
        if head + 1 < head_count:
            tiles.append(jnp.where(lane < 64, first, outs[head + 1]))
        else:
            tiles.append(first[:, :64])
    context = jnp.concatenate(tiles, axis=1)
    wide_ref[...] = context
    low_ref[...] = context.astype(low_type)
    stat_ref[...] = stats


def attend(q_pad, kv_all, aug, head_count):
    query_rows = q_pad.shape[0]
    length = kv_all.shape[0]
    tile = 256
    width = head_count * head_size
    whole = lambda i: (0, 0)
    by_tile = lambda i: (i, 0)
    work = query_rows * length * head_count
    return pl.pallas_call(
        partial(attend_kernel, head_count, math.gcd(length, 2048)),
        grid=(query_rows // tile,),
        in_specs=[
            pl.BlockSpec((tile, q_pad.shape[1]), by_tile),
            pl.BlockSpec(kv_all.shape, whole),
            pl.BlockSpec(aug.shape, whole),
        ],
        out_specs=[
            pl.BlockSpec((tile, width), by_tile),
            pl.BlockSpec((tile, width), by_tile),
            pl.BlockSpec((tile, 128), by_tile),
        ],
        out_shape=[
            jax.ShapeDtypeStruct((query_rows, width), low_type),
            jax.ShapeDtypeStruct((query_rows, width), wide_type),
            jax.ShapeDtypeStruct((query_rows, 128), wide_type),
        ],
        cost_estimate=pl.CostEstimate(
            flops=work * 1024, bytes_accessed=8 * 1024 * 1024, transcendentals=work
        ),
        compiler_params=pltpu.CompilerParams(vmem_limit_bytes=vmem_bytes),
    )(q_pad, kv_all, aug)


def split_three(number):
    first = number.astype(low_type).astype(wide_type)
    second = (number - first).astype(low_type).astype(wide_type)
    return first, second, number - first - second


def attend_back_kernel(
    head, head_count, query_part,
    q_ref, stat_ref, grad_ref, context_ref, kv_ref, aug_ref, keys_ref,
    kv_grad_ref, q_grad_ref, q_ext, g_ext,
):
    rows = kv_ref.shape[0]
    query_rows = q_ref.shape[0]

    @pl.when(pl.program_id(0) == 0)
    def _():
        q_grad_ref[...] = jnp.zeros_like(q_grad_ref)
        for start in range(0, query_rows, 256):
            part = pl.ds(start, 256)
            lane = lanes_of((256, 128))
            stats = stat_ref[part, :]
            top = stats[:, head : head + 1]
            total = stats[:, head_count + head : head_count + head + 1]
            begin = head // 2 * 128
            if head % 2 == 0 and head == head_count - 1:
                spare = jnp.zeros((256, 64), wide_type)
                grad = jnp.concatenate([spare, grad_ref[part, begin:].astype(wide_type)], axis=1)
                context = jnp.concatenate([spare, context_ref[part, begin:]], axis=1)
            else:
                grad = grad_ref[part, begin : begin + 128].astype(wide_type)
                context = context_ref[part, begin : begin + 128]
                if head % 2 == 0:
                    grad = pltpu.roll(grad, 64, 1)
                    context = pltpu.roll(context, 64, 1)
            grad = jnp.where(lane >= 64, grad, 0.0)
            delta = jnp.sum(grad * context, axis=1, keepdims=True) / total
            q_more = jnp.where(lane == 0, 1.0, 0.0)
            g_more = jnp.zeros((256, 128), wide_type)
            for place, (of_top, of_delta) in enumerate(zip(split_three(top), split_three(delta))):
                q_more = jnp.where(lane == place + 1, -of_top, q_more)
                g_more = jnp.where(lane == place + 1, -of_delta, g_more)
            q_ext[part, :128] = q_ref[part, :]
            q_ext[part, 128:] = q_more.astype(low_type)
            g_ext[part, :128] = (grad / total).astype(low_type)
            g_ext[part, 128:] = g_more.astype(low_type)

    kv_ext = jnp.concatenate([kv_ref[...], aug_ref[...]], axis=1)
    accum = jnp.zeros((rows, 128), wide_type)
    for start in range(0, query_rows, query_part):
        part = pl.ds(start, query_part)
        q_part = q_ext[part, :]
        g_part = g_ext[part, :]
        weights = jnp.exp2(product(kv_ext, q_part, back_dims))
        along_values = product(kv_ext, g_part, back_dims)
        grad_scores = (weights * along_values).astype(low_type)
        accum = accum + product(weights.astype(low_type), g_part[:, :128])
        accum = accum + product(grad_scores, q_part[:, :128])
        q_grad_ref[:, part] += product(keys_ref[...], grad_scores)
    lane = lanes_of((rows, 128))
    kv_grad_ref[...] = (accum * jnp.where(lane < 64, log_two, 1.0)).astype(low_type)


def attend_back(head, head_count, q_pad, stats, grad_context, context, kv_all, aug, kv_turned):
    query_rows = q_pad.shape[0]
    length = kv_all.shape[0]
    rows = math.gcd(length, 1024)
    width = grad_context.shape[1]
    whole = lambda i: (0, 0)
    work = query_rows * length
    return pl.pallas_call(
        partial(attend_back_kernel, head, head_count, 512),
        grid=(length // rows,),
        in_specs=[
            pl.BlockSpec((query_rows, 128), lambda i: (0, head)),
            pl.BlockSpec((query_rows, 128), whole),
            pl.BlockSpec((query_rows, width), whole),
            pl.BlockSpec((query_rows, width), whole),
            pl.BlockSpec((rows, 128), lambda i: (i, head)),
            pl.BlockSpec((rows, 128), lambda i: (i, 0)),
            pl.BlockSpec((64, rows), lambda i: (2 * head, i)),
        ],
        out_specs=[
            pl.BlockSpec((rows, 128), lambda i: (i, 0)),
            pl.BlockSpec((64, query_rows), whole),
        ],
        out_shape=[
            jax.ShapeDtypeStruct((length, 128), low_type),
            jax.ShapeDtypeStruct((64, query_rows), wide_type),
        ],
        scratch_shapes=[
            pltpu.VMEM((query_rows, 256), low_type),
            pltpu.VMEM((query_rows, 256), low_type),
        ],
        cost_estimate=pl.CostEstimate(
            flops=work * 2560, bytes_accessed=8 * 1024 * 1024, transcendentals=work
        ),
        compiler_params=pltpu.CompilerParams(vmem_limit_bytes=vmem_bytes),
    )(q_pad, stats, grad_context, context, kv_all, aug, kv_turned)


class Layout:
    def __init__(self):
        self.ctx = lax.axis_size("ctx")
        self.fsdp = lax.axis_size("fsdp")
        self.ring = self.ctx // head_splits
        self.group = lax.axis_index("ctx") // self.ring
        self.place = lax.axis_index("ctx") % self.ring
        self.row = lax.axis_index("fsdp")
        self.bits = [1 << k for k in reversed(range(self.ring.bit_length() - 1))]

    def shift(self, block, by):
        pairs = [(i, (i + by * self.ring) % self.ctx) for i in range(self.ctx)]
        return lax.ppermute(block, "ctx", pairs)

    def swap(self, block, bit):
        return lax.ppermute(block, "ctx", [(i, i ^ bit) for i in range(self.ctx)])

    def bit_of(self, bit):
        return (self.place // bit) % 2

    def across(self, block):
        return lax.ppermute(block, "fsdp", [(0, 1), (1, 0)])

    def gather_rows(self, shard):
        rows = shard.shape[0]
        if self.fsdp != 2:
            return lax.all_gather(shard, "fsdp", axis=0, tiled=True)
        half = rows // 2
        core = self.bit_of(1)
        mine = self.across(lax.dynamic_slice_in_dim(shard, core * half, half, 0))
        other = self.swap(mine, 1)
        whole = jnp.zeros((rows * 2,) + shard.shape[1:], shard.dtype)
        far = (1 - self.row) * rows
        whole = lax.dynamic_update_slice_in_dim(whole, shard, self.row * rows, 0)
        whole = lax.dynamic_update_slice_in_dim(whole, mine, far + core * half, 0)
        return lax.dynamic_update_slice_in_dim(whole, other, far + (1 - core) * half, 0)

    def gather_small(self, shard):
        if self.fsdp != 2:
            return lax.all_gather(shard, "fsdp", axis=0, tiled=False)
        other = self.across(shard)
        return jnp.where(
            self.row == 0, jnp.stack([shard, other]), jnp.stack([other, shard])
        )

    def to_far(self, blocks):
        twice = jnp.concatenate([blocks, blocks], axis=0)
        return lax.dynamic_slice_in_dim(twice, self.group, head_splits, 0)

    def to_near(self, blocks):
        twice = jnp.concatenate([blocks, blocks], axis=0)
        return lax.dynamic_slice_in_dim(twice, head_splits - self.group, head_splits, 0)

    def reduce_bit(self, array, bit, axis=0):
        half = array.shape[axis] // 2
        mine = self.bit_of(bit)
        keep = lax.dynamic_slice_in_dim(array, mine * half, half, axis)
        give = lax.dynamic_slice_in_dim(array, (1 - mine) * half, half, axis)
        got = self.swap(give.astype(low_type), bit)
        return keep.astype(wide_type) + got.astype(wide_type)

    def gather_bit(self, array, bit):
        other = self.swap(array, bit)
        return jnp.where(
            self.bit_of(bit) == 0,
            jnp.concatenate([array, other]),
            jnp.concatenate([other, array]),
        )

    def reduce_rows(self, array):
        if self.fsdp != 2:
            summed = lax.psum_scatter(
                array.astype(wide_type), "fsdp", scatter_dimension=0, tiled=True
            )
            return summed[0]
        keep = lax.dynamic_index_in_dim(array, self.row, 0, keepdims=False)
        give = lax.dynamic_index_in_dim(array, 1 - self.row, 0, keepdims=False)
        got = self.across(give.astype(low_type))
        return keep.astype(wide_type) + got.astype(wide_type)


def shards(
    layer_input,
    teacher_states,
    seq_lengths,
    query_weight,
    query_bias,
    key_weight,
    value_weight,
    value_bias,
    out_weight,
    out_bias,
    attn_gain,
    attn_shift,
    inner_weight,
    inner_bias,
    outer_weight,
    outer_bias,
    final_gain,
    final_shift,
):
    at = Layout()
    seg_rows, groups, width = layer_input.shape
    shard_rows = query_weight.shape[0]
    ff_rows = outer_weight.shape[0]
    ff_width = inner_weight.shape[1]
    heads = H // head_splits
    cols = heads * head_size
    tokens = layer_input.reshape(seg_rows, width)

    blocks = [tokens] + [at.shift(tokens, s) for s in range(1, head_splits)]

    def group_cols(weight):
        return lax.dynamic_slice_in_dim(weight, at.group * cols, cols, 1)

    w_qkv = at.gather_small(
        jnp.concatenate(
            [group_cols(query_weight), group_cols(key_weight), group_cols(value_weight)], axis=1
        ).reshape(-1)
    ).reshape(width, 3, heads, head_size)
    vectors = at.gather_small(
        jnp.concatenate(
            [
                query_bias, value_bias, out_bias, attn_gain, attn_shift,
                outer_bias, final_gain, final_shift, inner_bias,
            ]
        )
    ).astype(wide_type)
    vector = lambda k: vectors[:, k * shard_rows : (k + 1) * shard_rows].reshape(-1)
    b_query, b_value, b_out, g_attn, s_attn, b_outer, g_final, s_final = map(vector, range(8))
    b_inner = vectors[:, 8 * shard_rows :].reshape(-1)
    w_out = at.gather_rows(out_weight)
    w_inner = at.gather_rows(inner_weight)
    w_outer = at.gather_rows(outer_weight)
    own_count = jnp.sum(seq_lengths).astype(wide_type)
    if at.fsdp == 2:
        valid_count = own_count + at.across(own_count.reshape(1))[0]
    else:
        valid_count = lax.psum(own_count, "fsdp")

    w_query, w_key, w_value = (w_qkv[:, k] for k in range(3))
    w_pack = jnp.concatenate(
        [
            jnp.pad(w_query, ((0, 0), (0, 0), (0, head_size))).reshape(width, 2 * cols),
            jnp.concatenate([w_key, w_value], axis=2).reshape(width, 2 * cols),
        ],
        axis=1,
    )
    group_bias = lambda b: lax.dynamic_slice_in_dim(b, at.group * cols, cols, 0).reshape(
        heads, head_size
    )
    q_bias = jnp.pad(group_bias(b_query), ((0, 0), (0, head_size))).reshape(-1)
    kv_bias = jnp.pad(group_bias(b_value), ((0, 0), (head_size, 0))).reshape(-1)
    x_line = jnp.concatenate(blocks, axis=0)
    projected = product(x_line, w_pack)
    q_pad = ((projected[:, : 2 * cols] + q_bias) * score_scale).astype(low_type)
    kv_all = (projected[:, 2 * cols :] + kv_bias).astype(low_type)
    codes = [0]
    for bit in at.bits:
        kv_all = jnp.concatenate([kv_all, at.swap(kv_all, bit)], axis=0)
        codes = codes + [code ^ bit for code in codes]
    length = kv_all.shape[0]
    source = jnp.concatenate(
        [
            ((at.group - jnp.arange(head_splits)) % head_splits) * at.ring + (at.place ^ code)
            for code in codes
        ]
    )
    position = (source[:, None] * seg_rows + jnp.arange(seg_rows)[None, :]).reshape(-1, 1)
    lane = lax.broadcasted_iota(jnp.int32, (length, 128), 1)
    mask = jnp.where(position < seq_lengths[0], 0.0, masked_score)
    aug = jnp.where(lane == 0, mask, jnp.where(lane < 4, 1.0, 0.0)).astype(low_type)

    context_low, context_wide, stats = attend(q_pad, kv_all, aug, heads)
    kv_turned = kv_all.T

    line = context_low.reshape(head_splits, seg_rows, cols)
    back = [line[0]] + [at.shift(line[s], -s) for s in range(1, head_splits)]
    context_low = (
        at.to_near(jnp.stack(back)).transpose(1, 0, 2).reshape(seg_rows, width)
    )
    attn_out = product(context_low, w_out) + b_out
    pre_norm = tokens.astype(wide_type) + attn_out
    normed, attn_pull = jax.vjp(layer_norm, pre_norm, g_attn, s_attn)
    normed_low = normed.astype(low_type)
    hidden_pre = product(normed_low, w_inner) + b_inner
    act, gelu_pull = jax.vjp(gelu_exact, hidden_pre)
    act_low = act.astype(low_type)
    branch = product(act_low, w_outer) + b_outer
    output, final_pull = jax.vjp(layer_norm, normed + branch, g_final, s_final)
    target = teacher_states.reshape(seg_rows, width).astype(wide_type)
    own_position = lax.axis_index("ctx") * seg_rows + jnp.arange(seg_rows)[:, None]
    valid_mask = (own_position < seq_lengths[0]).astype(wide_type)
    mismatch = output - target
    total_sq = jnp.sum(valid_mask * mismatch * mismatch)
    token_total = seg_rows * groups * at.ctx * at.fsdp
    grad_out = 2.0 * valid_mask * mismatch * (token_total / valid_count)
    grad_mid, final_gain_grad, final_shift_grad = final_pull(grad_out)
    grad_branch = grad_mid.astype(low_type)
    outer_bias_grad = jnp.sum(grad_branch, axis=0, dtype=wide_type)
    outer_weight_grad = product(act_low, grad_branch, weight_dims)
    grad_hidden = gelu_pull(product(grad_branch, w_outer, back_dims))[0].astype(low_type)
    inner_bias_grad = jnp.sum(grad_hidden, axis=0, dtype=wide_type)
    inner_weight_grad = product(normed_low, grad_hidden, weight_dims)
    grad_normed = grad_mid + product(grad_hidden, w_inner, back_dims)
    grad_sum, attn_gain_grad, attn_shift_grad = attn_pull(grad_normed)
    grad_attn = grad_sum.astype(low_type)
    out_bias_grad = jnp.sum(grad_attn, axis=0, dtype=wide_type)
    out_weight_grad = product(context_low, grad_attn, weight_dims)
    grad_context = product(grad_attn, w_out, back_dims).astype(low_type)

    line = at.to_far(grad_context.reshape(seg_rows, head_splits, cols).transpose(1, 0, 2))
    grad_line = jnp.concatenate(
        [line[0]] + [at.shift(line[s], s) for s in range(1, head_splits)], axis=0
    )
    kv_grads, q_grads = [], []
    for head in range(heads):
        kv_grad, q_grad = attend_back(
            head, heads, q_pad, stats, grad_line, context_wide, kv_all, aug, kv_turned
        )
        for bit in reversed(at.bits):
            half = kv_grad.shape[0] // 2
            got = at.swap(kv_grad[half:], bit)
            kv_grad = (kv_grad[:half].astype(wide_type) + got.astype(wide_type)).astype(low_type)
        kv_grads.append(kv_grad)
        q_grads.append(q_grad)
    q_rows = (jnp.concatenate(q_grads, axis=0).T * 0.125).astype(low_type)
    kv_rows = jnp.stack(kv_grads, axis=1).reshape(-1, heads, 2, head_size)
    rows = jnp.concatenate(
        [q_rows, kv_rows[:, :, 0].reshape(-1, cols), kv_rows[:, :, 1].reshape(-1, cols)], axis=1
    )

    qkv_grad = product(x_line, rows, weight_dims)
    bias_rows = jnp.sum(rows, axis=0, dtype=wide_type)
    line = rows.reshape(head_splits, seg_rows, 3 * cols)
    near = at.to_near(
        jnp.stack([line[0]] + [at.shift(line[s], -s) for s in range(1, head_splits)])
    ).reshape(head_splits, seg_rows, 3, cols)
    all_rows = near.transpose(1, 2, 0, 3).reshape(seg_rows, 3 * width)
    w_all = jnp.concatenate([at.gather_rows(w) for w in (query_weight, key_weight, value_weight)], axis=1)
    input_grad = grad_sum + product(all_rows, w_all, back_dims)

    def spread(weight_rows):
        low = weight_rows.astype(low_type)
        if at.ring > 1:
            low = at.reduce_bit(low, 1, axis=1).astype(low_type)
        kept = at.reduce_rows(low).astype(low_type)
        same_core = [[i for i in range(at.ctx) if i % 2 == c] for c in range(2)]
        part = lax.psum_scatter(
            kept, "ctx", scatter_dimension=0, tiled=True, axis_index_groups=same_core
        )
        full = lax.all_gather(part, "ctx", axis=0, tiled=True, axis_index_groups=same_core)
        return at.gather_bit(full, 1).astype(wide_type)

    outer_weight_grad = spread(outer_weight_grad.reshape(at.fsdp, ff_rows, width))
    inner_weight_grad = spread(inner_weight_grad.reshape(at.fsdp, shard_rows, ff_width))
    out_weight_grad = spread(out_weight_grad.reshape(at.fsdp, shard_rows, width))

    part = qkv_grad.reshape(at.fsdp, shard_rows, 3 * cols)
    for bit in reversed(at.bits):
        part = at.reduce_bit(part, bit, axis=1)
    part = at.reduce_rows(part).astype(low_type)
    from_groups = at.to_near(
        jnp.stack([part] + [at.shift(part, -s) for s in range(1, head_splits)])
    ).transpose(1, 0, 2)
    whole = from_groups
    for bit in at.bits:
        whole = at.gather_bit(whole, bit)
    whole = whole.reshape(shard_rows, head_splits, 3, cols).transpose(0, 2, 1, 3)
    whole = whole.reshape(shard_rows, 3, width).astype(wide_type)

    placed_bias = lax.dynamic_update_slice(
        jnp.zeros((3, width), wide_type), bias_rows.reshape(3, cols), (0, at.group * cols)
    )
    small = jnp.concatenate(
        [
            placed_bias[0], placed_bias[2], out_bias_grad, attn_gain_grad, attn_shift_grad,
            outer_bias_grad, final_gain_grad, final_shift_grad, inner_bias_grad,
            jnp.full((128,), total_sq),
        ]
    )
    small = lax.psum(small, ("ctx", "fsdp"))
    small_part = lambda k: lax.dynamic_slice_in_dim(
        small, k * width + at.row * shard_rows, shard_rows, 0
    )
    (
        query_bias_grad, value_bias_grad, out_bias_grad, attn_gain_grad, attn_shift_grad,
        outer_bias_grad, final_gain_grad, final_shift_grad,
    ) = map(small_part, range(8))
    inner_bias_grad = lax.dynamic_slice_in_dim(small, 8 * width + at.row * ff_rows, ff_rows, 0)
    distill_loss = small[8 * width + ff_width] / (width * valid_count)
    return (
        distill_loss,
        output.reshape(seg_rows, groups, width),
        input_grad.reshape(seg_rows, groups, width),
        whole[:, 0],
        query_bias_grad,
        whole[:, 1],
        whole[:, 2],
        value_bias_grad,
        out_weight_grad,
        out_bias_grad,
        attn_gain_grad,
        attn_shift_grad,
        inner_weight_grad,
        inner_bias_grad,
        outer_weight_grad,
        outer_bias_grad,
        final_gain_grad,
        final_shift_grad,
    )


def solution(mesh):
    states = P("ctx", "fsdp", None)
    matrix = P("fsdp", None)
    vector = P("fsdp")
    placed = (
        states, states, vector,
        matrix, vector, matrix, matrix, vector, matrix, vector, vector, vector,
        matrix, vector, matrix, vector, vector, vector,
    )
    return jax.shard_map(
        shards,
        mesh=mesh,
        in_specs=placed,
        out_specs=(P(), states, states) + placed[3:],
        check_vma=False,
    )
```

```python
from functools import partial
import math

import jax
import jax.numpy as jnp
from jax import lax
from jax.experimental import pallas as pl
from jax.experimental.pallas import tpu as pltpu
from jax.sharding import PartitionSpec as P

H = 12
head_size = 64
head_splits = 4
group_heads = H // head_splits
group_cols = group_heads * head_size
pack_cols = 3 * group_cols
norm_eps = 1e-12
log_two = math.log(2.0)
masked_score = -1e30
low_type = jnp.bfloat16
wide_type = jnp.float32
score_scale = 1.0 / (log_two * math.sqrt(head_size))
some_vmem, most_vmem = 24 << 20, 58 << 20

plain_dims = (((1,), (0,)), ((), ()))
back_dims = (((1,), (1,)), ((), ()))
weight_dims = (((0,), (0,)), ((), ()))

in_smem = pl.BlockSpec(memory_space=pltpu.SMEM)
in_vmem = pl.BlockSpec(memory_space=pltpu.VMEM)
in_any = pl.BlockSpec(memory_space=pl.ANY)


def product(left_op, right_op, dims=plain_dims):
    return lax.dot_general(left_op, right_op, dims, preferred_element_type=wide_type)


def lanes_of(shape):
    return lax.broadcasted_iota(jnp.int32, shape, 1)


def compiled(name, vmem=some_vmem):
    return dict(
        name=name,
        cost_estimate=pl.CostEstimate(flops=1, bytes_accessed=1, transcendentals=0),
        compiler_params=pltpu.CompilerParams(vmem_limit_bytes=vmem),
    )


class Sum:
    def __init__(self, keep, got):
        self.keep, self.got = keep, got

    def close(self):
        return (self.keep.astype(wide_type) + self.got.astype(wide_type)).astype(low_type)


class Order:
    def __init__(self, place):
        self.place, self.last = place, []

    def next(self, *others):
        names = self.last + [(other, "got") for other in others]
        values = [getattr(owner, name) for owner, name in names]
        place, *values = lax.optimization_barrier((self.place, *values))
        for (owner, name), value in zip(names, values):
            setattr(owner, name, value)
        return place

    def did(self, owner, name="keep"):
        self.last = [(owner, name)]


def low_array(*shape):
    return jax.ShapeDtypeStruct(shape, low_type)


def wide_array(*shape):
    return jax.ShapeDtypeStruct(shape, wide_type)


def head_front(tile, head):
    begin = head // 2 * 128
    if begin + 128 <= tile.shape[1]:
        part = tile[:, begin : begin + 128]
        if head % 2:
            part = pltpu.roll(part, 64, 1)
    else:
        part = jnp.concatenate([tile[:, begin:], jnp.zeros_like(tile[:, begin:])], axis=1)
    return jnp.where(lanes_of(part.shape) < 64, part, 0.0)


def head_rear(tile, head):
    begin = head // 2 * 128
    if begin + 128 <= tile.shape[1]:
        part = tile[:, begin : begin + 128]
        if head % 2 == 0:
            part = pltpu.roll(part, 64, 1)
    else:
        part = jnp.concatenate([jnp.zeros_like(tile[:, begin:]), tile[:, begin:]], axis=1)
    return jnp.where(lanes_of(part.shape) >= 64, part, 0.0)


(at_row, at_core, at_x, at_z, at_group, at_ring, at_first, at_length, at_near, at_mine, at_other) = range(11)


def pack_kernel(place_ref, q_ref, k_ref, v_ref, all_ref, own_ref):
    rows = q_ref.shape[0]
    for group in range(head_splits):
        part = pl.ds(group * rows, rows)
        for head in range(group_heads):
            begin = (group * group_heads + head) * head_size
            all_ref[part, head * 128 : head * 128 + 64] = k_ref[:, begin : begin + head_size]
            all_ref[part, head * 128 + 64 : head * 128 + 128] = v_ref[:, begin : begin + head_size]
        all_ref[part, 2 * group_cols :] = q_ref[:, group * group_cols : (group + 1) * group_cols]
    own_ref[...] = all_ref[pl.ds(pl.multiple_of(place_ref[at_group] * rows, rows), rows), :]


def pack_weights(place, query_weight, key_weight, value_weight):
    rows = query_weight.shape[0]
    return pl.pallas_call(
        pack_kernel,
        in_specs=[in_smem] + [in_vmem] * 3,
        out_specs=[in_vmem] * 2,
        out_shape=[low_array(head_splits * rows, pack_cols), low_array(rows, pack_cols)],
        **compiled("pack_weights", most_vmem),
    )(place, query_weight, key_weight, value_weight)


def whole_vector(place_ref, own_ref, other_ref, begin, size):
    own = own_ref[:, begin : begin + size].astype(wide_type)
    other = other_ref[:, begin : begin + size].astype(wide_type)
    first = place_ref[at_near] == 0
    return jnp.concatenate([jnp.where(first, own, other), jnp.where(first, other, own)], axis=1)


def project_kernel(place_ref, x0, x1, x2, x3, own_ref, other_ref, near_ref, far_ref, q_ref, kv_ref):
    half = own_ref.shape[0]
    rows = x0.shape[0]
    near = pl.multiple_of(place_ref[at_near] * half, 128)
    far = pl.multiple_of((1 - place_ref[at_near]) * half, 128)
    kv_cols = 2 * group_cols
    biases = [whole_vector(place_ref, near_ref, far_ref, k * half, half) for k in range(2)]
    q_bias, v_bias = [jnp.zeros((1, group_cols), wide_type)] * 2
    for group in range(head_splits):
        cols = slice(group * group_cols, (group + 1) * group_cols)
        q_bias = jnp.where(place_ref[at_group] == group, biases[0][:, cols], q_bias)
        v_bias = jnp.where(place_ref[at_group] == group, biases[1][:, cols], v_bias)
    kv_bias = []
    for head in range(group_heads):
        kv_bias += [jnp.zeros((1, head_size), wide_type), v_bias[:, head * 64 : head * 64 + 64]]
    bias = jnp.concatenate(kv_bias + [q_bias], axis=1)
    for k, x_ref in enumerate((x0, x1, x2, x3)):
        part = pl.ds(k * rows, rows)
        made = product(x_ref[:, pl.ds(near, half)], own_ref[...])
        made = made + product(x_ref[:, pl.ds(far, half)], other_ref[...]) + bias
        kv_ref[part, :] = made[:, :kv_cols].astype(low_type)
        q_ref[part, :] = (made[:, kv_cols:] * score_scale).astype(low_type)


def project(place, blocks, own, other, vectors):
    rows, width = blocks[0].shape
    line = rows * head_splits
    return pl.pallas_call(
        project_kernel,
        in_specs=[in_smem] + [in_vmem] * 8,
        out_specs=[in_vmem] * 2,
        out_shape=[low_array(line, group_cols), low_array(line, 2 * group_cols)],
        **compiled("project", most_vmem),
    )(place, *blocks, own, other, *vectors)


def attend_kernel(order, resumed, finished, place_ref, q_ref, *refs):
    pieces = len(order)
    kv_refs, aug_ref = refs[:pieces], refs[pieces]
    refs = refs[pieces + 1 :]
    state_ref, out_refs = (refs[0], refs[1:]) if resumed else (None, refs)
    rows = q_ref.shape[0]
    piece_rows = kv_refs[0].shape[0]
    lane = lanes_of((rows, 128))
    q_aug = jnp.where(lane == 0, 1.0, 0.0).astype(low_type)
    stats = jnp.zeros((rows, 128), wide_type)
    q_wide = q_ref[...].astype(wide_type)
    outs = []
    joint = 2 if pieces % 2 == 0 else 1
    for head in range(group_heads):
        cols = pl.ds(head * 128, 128)
        q_ext = jnp.concatenate([head_front(q_wide, head).astype(low_type), q_aug], axis=1)
        top = None
        if resumed:
            accum = state_ref[:, cols]
            total, top = accum[:, 0:1], accum[:, 1:2]
        for first in range(0, pieces, joint):
            kv_ext = jnp.concatenate(
                [
                    jnp.concatenate(
                        [
                            kv_refs[first + k][:, cols],
                            aug_ref[pl.ds(order[first + k] * piece_rows, piece_rows), :],
                        ],
                        axis=1,
                    )
                    for k in range(joint)
                ],
                axis=0,
            )
            scores = product(q_ext, kv_ext, back_dims)
            new_top = jnp.floor(jnp.max(scores, axis=1, keepdims=True))
            if top is not None:
                new_top = jnp.maximum(top, new_top)
            weights = jnp.exp2(scores - new_top).astype(low_type)
            part_sum = product(weights, kv_ext)
            part_total = part_sum[:, 129:130]
            if top is None:
                accum, total = part_sum[:, :128], part_total
            else:
                factor = jnp.exp2(top - new_top)
                accum, total = accum * factor + part_sum[:, :128], total * factor + part_total
            top = new_top
        if finished:
            outs.append(accum / total)
            stats = jnp.where(lane == head, top, stats)
            stats = jnp.where(lane == group_heads + head, total, stats)
        else:
            out_refs[0][:, cols] = jnp.where(lane == 0, total, jnp.where(lane == 1, top, accum))
    if not finished:
        return
    low_refs, wide_ref, stat_ref = out_refs[:head_splits], out_refs[-2], out_refs[-1]
    tiles = []
    for head in range(0, group_heads, 2):
        first = pltpu.roll(outs[head], 64, 1)
        if head + 1 < group_heads:
            tiles.append(jnp.where(lane < 64, first, outs[head + 1]))
        else:
            tiles.append(first[:, :64])
    context = jnp.concatenate(tiles, axis=1)
    wide_ref[...] = context
    stat_ref[...] = stats
    for k, low_ref in enumerate(low_refs):

        @pl.when(pl.program_id(0) == k)
        def _():
            low_ref[...] = context.astype(low_type)


def attend(place, q_line, kv_pieces, order, aug, state, finished):
    line = q_line.shape[0]
    tile = line // head_splits
    whole = lambda i: (0, 0)
    by_tile = lambda i: (i, 0)
    used = [kv_pieces[k] for k in order]
    states = [] if state is None else [state]
    state_cols = 128 * group_heads
    work = line * group_heads * used[0].shape[0] * len(used)
    if finished:
        out_specs = [pl.BlockSpec((tile, group_cols), whole)] * head_splits
        out_specs += [pl.BlockSpec((tile, group_cols), by_tile), pl.BlockSpec((tile, 128), by_tile)]
        out_shape = [low_array(tile, group_cols)] * head_splits
        out_shape += [wide_array(line, group_cols), wide_array(line, 128)]
    else:
        out_specs = pl.BlockSpec((tile, state_cols), by_tile)
        out_shape = wide_array(line, state_cols)
    return pl.pallas_call(
        partial(attend_kernel, order, state is not None, finished),
        grid=(head_splits,),
        in_specs=[in_smem, pl.BlockSpec((tile, group_cols), by_tile)]
        + [pl.BlockSpec(piece.shape, whole) for piece in used]
        + [pl.BlockSpec(aug.shape, whole)]
        + [pl.BlockSpec((tile, state_cols), by_tile) for _ in states],
        out_specs=out_specs,
        out_shape=out_shape,
        **compiled("attend"),
    )(place, q_line, *used, aug, *states)


def split_three(number):
    first = number.astype(low_type).astype(wide_type)
    second = (number - first).astype(low_type).astype(wide_type)
    return first, second, number - first - second


def attend_back_kernel(head, pieces, query_part, place_ref, q_ref, stat_ref, context_ref, g0, g1, g2, g3, *refs):
    kv_refs, aug_ref = refs[:pieces], refs[pieces]
    keep_ref, give_ref, q_grad_ref, kv_all, q_ext, g_ext = refs[pieces + 1 :]
    rows = kv_refs[0].shape[0]
    query_rows = q_ref.shape[0]
    seg_rows = g0.shape[0]
    step = pl.program_id(0)

    @pl.when(step == 0)
    def _():
        q_grad_ref[...] = jnp.zeros_like(q_grad_ref)
        for k, kv_ref in enumerate(kv_refs):
            kv_all[pl.ds(k * rows, rows), :] = kv_ref[...]
        for k, grad_ref in enumerate((g0, g1, g2, g3)):
            part = pl.ds(k * seg_rows, seg_rows)
            lane = lanes_of((seg_rows, 128))
            stats = stat_ref[part, :]
            top = stats[:, head : head + 1]
            total = stats[:, group_heads + head : group_heads + head + 1]
            grad = head_rear(grad_ref[...].astype(wide_type), head)
            context = head_rear(context_ref[part, :], head)
            delta = jnp.sum(grad * context, axis=1, keepdims=True) / total
            q_more = jnp.where(lane == 0, 1.0, 0.0)
            g_more = jnp.zeros((seg_rows, 128), wide_type)
            for place, (of_top, of_delta) in enumerate(zip(split_three(top), split_three(delta))):
                q_more = jnp.where(lane == place + 1, -of_top, q_more)
                g_more = jnp.where(lane == place + 1, -of_delta, g_more)
            q_ext[part, :128] = head_front(q_ref[part, :].astype(wide_type), head).astype(low_type)
            q_ext[part, 128:] = q_more.astype(low_type)
            g_ext[part, :128] = (grad / total).astype(low_type)
            g_ext[part, 128:] = g_more.astype(low_type)

    kv_part = kv_all[pl.ds(pl.multiple_of(step * rows, rows), rows), :]
    kv_ext = jnp.concatenate([kv_part, aug_ref[...]], axis=1)
    keys_turned = jnp.transpose(kv_part)[:64]
    accum = jnp.zeros((rows, 128), wide_type)
    for start in range(0, query_rows, query_part):
        part = pl.ds(start, query_part)
        q_part = q_ext[part, :]
        g_part = g_ext[part, :]
        weights = jnp.exp2(product(kv_ext, q_part, back_dims))
        along_values = product(kv_ext, g_part, back_dims)
        grad_scores = (weights * along_values).astype(low_type)
        accum = accum + product(weights.astype(low_type), g_part[:, :128])
        accum = accum + product(grad_scores, q_part[:, :128])
        q_grad_ref[:, part] += product(keys_turned, grad_scores)
    lane = lanes_of((rows, 128))
    made = (accum * jnp.where(lane < 64, log_two, 1.0)).astype(low_type)

    @pl.when(step < pieces // 2)
    def _():
        keep_ref[...] = made

    @pl.when(step >= pieces // 2)
    def _():
        give_ref[...] = made


def attend_back(place, head, q_line, stats, context, grads, kv_pieces, aug):
    line = q_line.shape[0]
    pieces = len(kv_pieces)
    rows = kv_pieces[0].shape[0]
    half = pieces // 2
    whole = lambda i: (0, 0)
    work = line * rows * pieces
    return pl.pallas_call(
        partial(attend_back_kernel, head, pieces, math.gcd(line, 512)),
        grid=(pieces,),
        in_specs=[
            in_smem,
            pl.BlockSpec(q_line.shape, whole),
            pl.BlockSpec(stats.shape, whole),
            pl.BlockSpec(context.shape, whole),
        ]
        + [pl.BlockSpec(grad.shape, whole) for grad in grads]
        + [pl.BlockSpec((rows, 128), lambda i: (0, head))] * pieces
        + [pl.BlockSpec((rows, 128), lambda i: (i, 0))],
        out_specs=[
            pl.BlockSpec((rows, 128), lambda i: (jnp.minimum(i, half - 1), 0)),
            pl.BlockSpec((rows, 128), lambda i: (jnp.maximum(i - half, 0), 0)),
            pl.BlockSpec((head_size, line), whole),
        ],
        out_shape=[
            low_array(rows * half, 128), low_array(rows * half, 128), wide_array(head_size, line)
        ],
        scratch_shapes=[
            pltpu.VMEM((rows * pieces, 128), low_type),
            pltpu.VMEM((line, 256), low_type),
            pltpu.VMEM((line, 256), low_type),
        ],
        **compiled("attend_back"),
    )(place, q_line, stats, context, *grads, *kv_pieces, aug)


def norm_forward(hidden):
    centre = hidden - jnp.mean(hidden, axis=1, keepdims=True)
    inverse = lax.rsqrt(jnp.mean(centre * centre, axis=1, keepdims=True) + norm_eps)
    return centre * inverse, inverse


def norm_back(grad, normal, inverse):
    along = jnp.mean(grad * normal, axis=1, keepdims=True)
    return inverse * (grad - jnp.mean(grad, axis=1, keepdims=True) - normal * along)


def over_tokens(array):
    return jnp.sum(array, axis=0, keepdims=True)


def mid_kernel(place_ref, factor_ref, x_ref, teacher_ref, c0, c1, c2, c3, near_ref, far_ref, *refs):
    weights = (refs[0:3], refs[3:6], refs[6:9])
    (
        output_ref, sum_ref, d0, d1, d2, d3, act_ref, hidden_ref, normed_ref, branch_ref, attn_ref, small_ref,
        w_out, w_inner, w_outer, slope_ref, sems,
    ) = refs[9:]
    held = (w_out, w_inner, w_outer)
    near, mine = place_ref[at_near], place_ref[at_mine]
    copies = []
    for k in range(3):
        own, half = weights[k][0].shape[0], weights[k][1].shape[0]
        far = (1 - near) * own
        for p, start in enumerate((near * own, far + mine * half, far + (1 - mine) * half)):
            rows = weights[k][p].shape[0]
            target = held[k].at[pl.ds(pl.multiple_of(start, half), rows), :]
            copies.append(pltpu.make_async_copy(weights[k][p], target, sems.at[k * 3 + p]))
            copies[-1].start()
    rows, width = x_ref.shape
    chunks = w_outer.shape[0] // width
    half = width // 2
    vector = lambda k, size: whole_vector(place_ref, near_ref, far_ref, k * half, size)
    b_out, g_attn, s_attn, b_outer, g_final, s_final = (vector(k, half) for k in range(2, 8))
    b_inner = vector(8, w_outer.shape[0] // 2)
    group = place_ref[at_group]
    of_group = lambda k: pl.ds(pl.multiple_of((group ^ k) * group_cols, group_cols), group_cols)

    for copy in copies[0:3]:
        copy.wait()
    hidden = x_ref[...].astype(wide_type) + b_out
    for k, c_ref in enumerate((c0, c1, c2, c3)):
        hidden = hidden + product(c_ref[...], w_out[of_group(k), :])
    attn_normal, attn_inverse = norm_forward(hidden)
    normed = attn_normal * g_attn + s_attn
    normed_low = normed.astype(low_type)
    normed_ref[...] = normed_low
    for copy in copies[3:9]:
        copy.wait()
    branch = normed + b_outer
    for k in range(chunks):
        cols = pl.ds(k * width, width)
        pre = product(normed_low, w_inner[:, cols]) + b_inner[:, k * width : (k + 1) * width]
        bell = 0.5 * (1.0 + lax.erf(pre * math.sqrt(0.5)))
        slope_ref[:, cols] = bell + pre * jnp.exp(-0.5 * pre * pre) * (1.0 / math.sqrt(2.0 * math.pi))
        act = (pre * bell).astype(low_type)
        act_ref[:, cols] = act
        branch = branch + product(act, w_outer[cols, :])
    final_normal, final_inverse = norm_forward(branch)
    output = final_normal * g_final + s_final
    output_ref[...] = output
    token = place_ref[at_first] + lax.broadcasted_iota(jnp.int32, (rows, 1), 0)
    valid = (token < place_ref[at_length]).astype(wide_type)
    mismatch = (output - teacher_ref[...].astype(wide_type)) * valid
    squares = over_tokens(mismatch * mismatch)
    grad_out = mismatch * factor_ref[0]
    final_gain_grad = over_tokens(grad_out * final_normal)
    final_shift_grad = over_tokens(grad_out)
    grad_mid = norm_back(grad_out * g_final, final_normal, final_inverse)
    grad_branch = grad_mid.astype(low_type)
    branch_ref[...] = grad_branch
    outer_bias_grad = over_tokens(grad_branch.astype(wide_type))
    grad_normed = grad_mid
    inner_bias_grad = []
    for k in range(chunks):
        cols = pl.ds(k * width, width)
        grad_act = product(grad_branch, w_outer[cols, :], back_dims)
        grad_hidden = (grad_act * slope_ref[:, cols]).astype(low_type)
        hidden_ref[:, cols] = grad_hidden
        inner_bias_grad.append(over_tokens(grad_hidden.astype(wide_type)))
        grad_normed = grad_normed + product(grad_hidden, w_inner[:, cols], back_dims)
    attn_gain_grad = over_tokens(grad_normed * attn_normal)
    attn_shift_grad = over_tokens(grad_normed)
    grad_sum = norm_back(grad_normed * g_attn, attn_normal, attn_inverse)
    sum_ref[...] = grad_sum
    grad_attn = grad_sum.astype(low_type)
    attn_ref[...] = grad_attn
    out_bias_grad = over_tokens(grad_attn.astype(wide_type))
    for k, d_ref in enumerate((d0, d1, d2, d3)):
        d_ref[...] = product(grad_attn, w_out[of_group(k), :], back_dims).astype(low_type)
    pairs = (
        (final_gain_grad, final_shift_grad),
        (outer_bias_grad, attn_gain_grad),
        (attn_shift_grad, out_bias_grad),
    )
    for side in range(2):
        cols = slice(side * half, side * half + half)
        lines = [jnp.concatenate([a[:, cols], b[:, cols]], axis=1) for a, b in pairs]
        lines += inner_bias_grad[side * 2 : side * 2 + 2] + [squares]
        lines.append(jnp.zeros((8 - len(lines), width), wide_type))
        small_ref[side] = jnp.concatenate(lines, axis=0)


def middle(place, factor, tokens, teacher, contexts, vectors, weights):
    rows, width = tokens.shape
    ff_width = weights[1][0].shape[1]
    pieces = [piece for weight in weights for piece in weight]
    return pl.pallas_call(
        mid_kernel,
        in_specs=[in_smem, in_smem] + [in_vmem] * 8 + [in_any] * 9,
        out_specs=[in_vmem] * 12,
        out_shape=[wide_array(rows, width), wide_array(rows, width)]
        + [low_array(rows, group_cols)] * 4
        + [low_array(rows, ff_width)] * 2
        + [low_array(rows, width)] * 3
        + [wide_array(2, 8, width)],
        scratch_shapes=[
            pltpu.VMEM((width, width), low_type),
            pltpu.VMEM((width, ff_width), low_type),
            pltpu.VMEM((ff_width, width), low_type),
            pltpu.VMEM((rows, ff_width), wide_type),
            pltpu.SemaphoreType.DMA((9,)),
        ],
        **compiled("middle", most_vmem),
    )(place, factor, tokens, teacher, *contexts, *vectors, *pieces)


def weight_kernel(
    place_ref, act_ref, branch_ref, normed_ref, hidden_ref, c0, c1, c2, c3, attn_ref, small_ref,
    give_a, keep_a, give_b, keep_b, out_grad,
):
    width = branch_ref.shape[1]
    half = width // 2
    group = place_ref[at_group]

    @pl.when((pl.program_id(0) == 0) & (pl.program_id(1) == 0))
    def _():
        for k, c_ref in enumerate((c0, c1, c2, c3)):
            part = pl.ds(pl.multiple_of((group ^ k) * group_cols, group_cols), group_cols)
            out_grad[part, :] = product(c_ref[...], attn_ref[...], weight_dims)

    row = place_ref[at_row] ^ pl.program_id(0)
    x = place_ref[at_x] ^ pl.program_id(1)
    for far, a_ref, b_ref in ((1, give_a, give_b), (0, keep_a, keep_b)):
        core = place_ref[at_core] ^ far
        begin = pl.multiple_of(((row * 2 + core) * 2 + x) * half, 128)
        outer = product(
            act_ref[:, pl.ds(begin, half)], branch_ref[...], weight_dims
        ).astype(low_type)
        inner = product(
            normed_ref[:, pl.ds(pl.multiple_of(row * half, 128), half)],
            hidden_ref[:, pl.ds(pl.multiple_of((core * 2 + x) * width, 128), width)],
            weight_dims,
        ).astype(low_type)
        base = row * half + core * (half // 2) + x * (half // 4)
        for z in range(4):
            apart = place_ref[at_z] ^ z
            spot = (apart & 1) * 2 + (apart >> 1)
            rows = slice(z * 96, z * 96 + 96)
            a_ref[0, 0, pl.ds(pl.multiple_of(spot * 96, 32), 96), :] = outer[rows]
            b_ref[0, 0, pl.ds(pl.multiple_of(spot * 128, 128), 96), :] = inner[rows]
            rest = out_grad[pl.ds(pl.multiple_of(base + z * 24, 8), 24), :]
            rest = jnp.concatenate([rest, small_ref[pl.ds(row, 1)][0]], axis=0)
            b_ref[0, 0, pl.ds(pl.multiple_of(spot * 128 + 96, 32), 32), :] = rest.astype(low_type)


def weight_grads(place, act, branch, normed, hidden, contexts, attn, small):
    rows, width = branch.shape
    a_shape, b_shape = (2, 2, width // 2, width), (2, 2, 512, width)
    a_spec = pl.BlockSpec((1, 1) + a_shape[2:], lambda i, j: (i, j, 0, 0))
    b_spec = pl.BlockSpec((1, 1) + b_shape[2:], lambda i, j: (j, i, 0, 0))
    return pl.pallas_call(
        weight_kernel,
        grid=(2, 2),
        in_specs=[in_smem] + [in_vmem] * 10,
        out_specs=[a_spec, a_spec, b_spec, b_spec],
        out_shape=[low_array(*a_shape)] * 2 + [low_array(*b_shape)] * 2,
        scratch_shapes=[pltpu.VMEM((width, width), wide_type)],
        **compiled("weight_grads", most_vmem),
    )(place, act, branch, normed, hidden, *contexts, attn, small)


def add_split_kernel(place_ref, kept_ref, got_ref, keep_ref, give_ref):
    total = kept_ref[...].astype(wide_type) + got_ref[...].astype(wide_type)
    keep_ref[...] = total[0].astype(low_type)
    give_ref[...] = total[1].astype(low_type)


def add_split(place, kept, got):
    cols = kept.shape[-1]
    shape = (2, kept.size // cols // 2, cols)
    tile = math.gcd(shape[1], 512)
    both = pl.BlockSpec((2, tile, cols), lambda i: (0, i, 0))
    one = pl.BlockSpec((tile, cols), lambda i: (i, 0))
    keep, give = pl.pallas_call(
        add_split_kernel,
        grid=(shape[1] // tile,),
        in_specs=[in_smem, both, both],
        out_specs=[one, one],
        out_shape=[low_array(*shape[1:])] * 2,
        **compiled("add_split"),
    )(place, kept.reshape(shape), got.reshape(shape))
    return keep.reshape(kept.shape[1:]), give.reshape(kept.shape[1:])


def unpack_kernel(place_ref, own_ref, got_ref, *out_refs):
    width = own_ref.shape[-1]
    for far, ref in enumerate((own_ref, got_ref)):
        core = place_ref[at_core] ^ far
        for k in range(2):
            x = place_ref[at_x] ^ k
            block = (ref[k, 0, 0] if len(out_refs) == 1 else ref[0, k, 0]).astype(wide_type)
            if len(out_refs) == 1:
                out_refs[0][pl.ds(core, 1), pl.ds(x, 1), 0] = block[None, None]
            else:
                inner_ref, out_ref = out_refs
                inner_ref[:, pl.ds(pl.multiple_of((core * 2 + x) * width, 128), width)] = block[:96]
                out_ref[pl.ds(core, 1), pl.ds(x, 1), 0] = block[None, None, 96:120]


def unpack(place, own, got):
    rows, width = own.shape[3:]
    z_of = lambda i, j, place_ref: place_ref[at_z] ^ (i + 2 * j)
    pieces = lambda count: pl.BlockSpec(
        (2, 2, 1, count, width), lambda i, j, p: (0, 0, z_of(i, j, p), 0, 0)
    )
    whole = pl.BlockSpec((96, 4 * width), lambda i, j, p: (z_of(i, j, p), 0))
    if rows == 96:
        specs, shapes = [pieces(96)], [wide_array(2, 2, 4, 96, width)]
        spec = pl.BlockSpec((2, 1, 1, rows, width), lambda i, j, p: (0, i, j, 0, 0))
    else:
        specs = [whole, pieces(24)]
        spec = pl.BlockSpec((1, 2, 1, rows, width), lambda i, j, p: (i, 0, j, 0, 0))
        shapes = [wide_array(width // 2, 4 * width), wide_array(2, 2, 4, 24, width)]
    return pl.pallas_call(
        unpack_kernel,
        grid_spec=pltpu.PrefetchScalarGridSpec(
            num_scalar_prefetch=1,
            grid=(2, 2),
            in_specs=[spec] * 2,
            out_specs=specs,
        ),
        out_shape=shapes,
        **compiled("unpack"),
    )(place, own, got)


def rows_kernel(heads, place_ref, *refs):
    q_grads, keeps, gots = refs[:heads], refs[heads : 2 * heads], refs[2 * heads : 3 * heads]
    blocks = refs[3 * heads : 3 * heads + 4]
    r0, r1, r2, r3, give_ref, keep_ref, w_grad, all_rows = refs[3 * heads + 4 :]
    rows, width = blocks[0].shape
    kv_cols = 2 * group_cols
    for k, (kept, got) in enumerate(zip(keeps, gots)):
        total = kept[...].astype(wide_type) + got[...].astype(wide_type)
        all_rows[:, k * 128 : k * 128 + 128] = total.astype(low_type)
    turned = jnp.concatenate([q_grad[...] for q_grad in q_grads], axis=0) * 0.125
    all_rows[:, kv_cols:] = jnp.transpose(turned).astype(low_type)
    half = width // 2
    bias = jnp.zeros((1, pack_cols), wide_type)
    for k, r_ref in enumerate((r0, r1, r2, r3)):
        made = all_rows[pl.ds(k * rows, rows), :]
        r_ref[...] = made
        bias = bias + over_tokens(made.astype(wide_type))
        for side in range(2):
            part = product(blocks[k][:, side * half : side * half + half], made, weight_dims)
            if k:
                w_grad[side] += part
            else:
                w_grad[side] = part
    bias = jnp.concatenate([bias, jnp.zeros((15, pack_cols), wide_type)], axis=0)
    for far, piece_ref in ((1, give_ref), (0, keep_ref)):
        core = place_ref[at_core] ^ far
        for i in range(2):
            ring = place_ref[at_ring] ^ i
            start = pl.multiple_of(core * (half // 2) + ring * (half // 4), half // 4)
            for j in range(2):
                row = place_ref[at_row] ^ j
                block = w_grad[pl.ds(row, 1), pl.ds(start, half // 4), :][0]
                piece_ref[i, j] = jnp.concatenate([block, bias], axis=0).astype(low_type)


def project_back(place, q_grads, keeps, gots, blocks):
    heads = len(q_grads)
    rows, width = blocks[0].shape
    pieces = (2, 2, width // 8 + 16, pack_cols)
    return pl.pallas_call(
        partial(rows_kernel, heads),
        in_specs=[in_smem] + [in_vmem] * (3 * heads + 4),
        out_specs=[in_vmem] * 6,
        out_shape=[low_array(rows, pack_cols)] * 4 + [low_array(*pieces)] * 2,
        scratch_shapes=[
            pltpu.VMEM((2, width // 2, pack_cols), wide_type),
            pltpu.VMEM((4 * rows, pack_cols), low_type),
        ],
        **compiled("project_back"),
    )(place, *q_grads, *keeps, *gots, *blocks)


def input_kernel(place_ref, sum_ref, r0, r1, r2, r3, own_ref, mine_ref, other_ref, grad_ref):
    half = own_ref.shape[0] // head_splits
    near = jnp.zeros((sum_ref.shape[0], half), wide_type)
    far = jnp.zeros((sum_ref.shape[0], half), wide_type)
    for k, r_ref in enumerate((r0, r1, r2, r3)):
        group = place_ref[at_group] ^ k
        near = near + product(r_ref[...], own_ref[pl.ds(pl.multiple_of(group * half, half), half), :], back_dims)
        fetched = (group >> 1) == place_ref[at_mine]
        side = pl.ds(pl.multiple_of((group & 1) * half, half), half)
        weight = jnp.where(fetched, mine_ref[side, :], other_ref[side, :])
        far = far + product(r_ref[...], weight, back_dims)
    for part, begin in ((near, place_ref[at_near]), (far, 1 - place_ref[at_near])):
        cols = pl.ds(pl.multiple_of(begin * half, 128), half)
        grad_ref[:, cols] = sum_ref[:, cols] + part


def input_back(place, grad_sum, rows, packs):
    return pl.pallas_call(
        input_kernel,
        in_specs=[in_smem] + [in_vmem] * 8,
        out_specs=in_vmem,
        out_shape=wide_array(*grad_sum.shape),
        **compiled("input_back"),
    )(place, grad_sum, *rows, *packs)


def qkv_unpack_kernel(place_ref, here_ref, there_ref, q_ref, k_ref, v_ref, bias_ref):
    fourth = q_ref.shape[0] // 4
    bias_ref[...] = jnp.zeros_like(bias_ref)
    for own in range(head_splits):

        @pl.when(place_ref[at_group] == own)
        def _():
            for n in range(4):
                piece = there_ref if n // 2 else here_ref
                core = place_ref[at_core] ^ (n // 2)
                ring = place_ref[at_ring] ^ (n % 2)
                part = pl.ds(pl.multiple_of(core * 2 * fourth + ring * fourth, fourth), fourth)
                for k in range(head_splits):
                    first = (own ^ k) * group_cols
                    block = piece[k, n % 2].astype(wide_type)
                    q_ref[part, first : first + group_cols] = block[:fourth, 2 * group_cols :]
                    for h in range(group_heads):
                        begin = first + h * head_size
                        keys = slice(h * 128, h * 128 + 64)
                        values = slice(h * 128 + 64, h * 128 + 128)
                        k_ref[part, begin : begin + head_size] = block[:fourth, keys]
                        v_ref[part, begin : begin + head_size] = block[:fourth, values]
                        if n == 0:
                            bias_ref[1:2, begin : begin + head_size] = block[fourth : fourth + 1, values]
                    if n == 0:
                        bias_ref[0:1, first : first + group_cols] = block[
                            fourth : fourth + 1, 2 * group_cols :
                        ]


def qkv_unpack(place, here, there, width):
    return pl.pallas_call(
        qkv_unpack_kernel,
        in_specs=[in_smem] + [in_vmem] * 2,
        out_specs=[in_vmem] * 4,
        out_shape=[wide_array(width // 2, width)] * 3 + [wide_array(8, width)],
        **compiled("qkv_unpack"),
    )(place, here, there)


class Layout:
    def __init__(self):
        self.ctx = lax.axis_size("ctx")
        self.fsdp = lax.axis_size("fsdp")
        self.me = lax.axis_index("ctx")
        self.row = lax.axis_index("fsdp")
        self.fast = self.ctx == 16 and self.fsdp == 2
        group_bits = (2, 4) if self.fast else (self.ctx // 4, self.ctx // 2)
        bits = [1 << k for k in reversed(range(self.ctx.bit_length() - 1))]
        self.ring_bits = [bit for bit in bits if bit not in group_bits]
        self.group = self.bit(group_bits[0]) + 2 * self.bit(group_bits[1])
        self.group_codes = [0, group_bits[0], group_bits[1], group_bits[0] | group_bits[1]]
        self.ring_codes = [0]
        for bit in self.ring_bits:
            self.ring_codes = self.ring_codes + [code | bit for code in self.ring_codes]

    def bit(self, bit):
        return (self.me // bit) % 2

    def swap(self, block, code):
        return lax.ppermute(block, "ctx", [(i, i ^ code) for i in range(self.ctx)])

    def groups(self, blocks):
        return [blocks[0]] + [self.swap(blocks[k], self.group_codes[k]) for k in range(1, 4)]

    def across(self, block):
        return lax.ppermute(block, "fsdp", [(0, 1), (1, 0)])

    def halves(self, shard):
        if self.fsdp == 2:
            return shard, self.across(shard)
        full = lax.all_gather(shard, "fsdp", axis=0, tiled=True)
        half = full.shape[0] // 2
        return full[:half], full[half:]

    def fetch(self, shard):
        if self.fsdp == 2:
            half = shard.shape[0] // 2
            return shard, self.across(lax.dynamic_slice_in_dim(shard, self.bit(1) * half, half, 0))
        return lax.all_gather(shard, "fsdp", axis=0, tiled=True), None

    def pieces(self, shard, mine):
        if self.fsdp == 2:
            return shard, mine, self.swap(mine, 1)
        half = shard.shape[0] // 2
        return shard[:half], shard[half : half * 3 // 2], shard[half * 3 // 2 :]


def shards(
    layer_input,
    teacher_states,
    seq_lengths,
    query_weight,
    query_bias,
    key_weight,
    value_weight,
    value_bias,
    out_weight,
    out_bias,
    attn_gain,
    attn_shift,
    inner_weight,
    inner_bias,
    outer_weight,
    outer_bias,
    final_gain,
    final_shift,
):
    at = Layout()
    seg_rows, groups, width = layer_input.shape
    shard_rows = query_weight.shape[0]
    ff_rows = outer_weight.shape[0]
    ff_width = inner_weight.shape[1]
    tokens = layer_input.reshape(seg_rows, width)
    teacher = teacher_states.reshape(seg_rows, width)
    two_rows = at.fsdp == 2
    place = jnp.stack(
        [
            at.row, at.bit(1), at.bit(2), at.bit(4) + 2 * at.bit(8), at.group, at.bit(8),
            at.me * seg_rows, seq_lengths[0],
            at.row if two_rows else 0, at.bit(1) if two_rows else 0, 0,
        ]
    ).astype(jnp.int32)

    blocks = at.groups([tokens] * 4)
    all_pack, own_pack = pack_weights(place, query_weight, key_weight, value_weight)
    own_pack, other_pack = at.halves(own_pack)
    vectors = (
        query_bias, value_bias, out_bias, attn_gain, attn_shift,
        outer_bias, final_gain, final_shift, inner_bias,
    )
    if two_rows:
        *vectors, own_pack = lax.optimization_barrier((*vectors, own_pack))
        own_vectors = jnp.concatenate(vectors).reshape(1, -1)
        vectors = (own_vectors, at.across(own_vectors))
    else:
        whole = lambda vector: lax.all_gather(vector, "fsdp", axis=0, tiled=True).reshape(2, -1)
        both = jnp.concatenate([whole(vector) for vector in vectors], axis=1)
        vectors = (both[:1], both[1:])
    own_count = jnp.sum(seq_lengths).astype(wide_type)
    if two_rows:
        valid_count = own_count + at.across(own_count.reshape(1))[0]
    else:
        valid_count = lax.psum(own_count, "fsdp")
    out_weight, inner_weight, outer_weight, other_pack = lax.optimization_barrier(
        (out_weight, inner_weight, outer_weight, other_pack)
    )
    sent = [at.fetch(weight) for weight in (out_weight, inner_weight, outer_weight)]
    q_line, kv_line = project(place, blocks, own_pack, other_pack, vectors)
    valid_count, kv_line = lax.optimization_barrier((valid_count, kv_line))

    source = jnp.stack(
        [at.me ^ (ring | group) for ring in at.ring_codes for group in at.group_codes]
    )
    position = (source[:, None] * seg_rows + jnp.arange(seg_rows)[None, :]).reshape(-1, 1)
    lane = lax.broadcasted_iota(jnp.int32, (position.shape[0], 128), 1)
    mask = jnp.where(position < seq_lengths[0], 0.0, masked_score)
    aug = jnp.where(lane == 0, mask, jnp.where(lane < 4, 1.0, 0.0)).astype(low_type)

    if at.fast:
        near = at.swap(kv_line, 1)
        far = at.swap(kv_line, 8)
        state = attend(place, q_line, [kv_line, None, near], (0, 2), aug, None, False)
        far, state = lax.optimization_barrier((far, state))
        kv_pieces = [kv_line, far, near, at.swap(far, 1)]
        order = (1, 3)
    else:
        kv_pieces = [kv_line]
        for bit in at.ring_bits:
            kv_pieces = kv_pieces + [at.swap(piece, bit) for piece in kv_pieces]
        state, order = None, tuple(range(len(kv_pieces)))
    *context_low, context, stats = attend(place, q_line, kv_pieces, order, aug, state, True)
    sent, context_low, all_pack = lax.optimization_barrier((sent, context_low, all_pack))
    weights = [at.pieces(*weight) for weight in sent]
    contexts = at.groups(context_low)
    if two_rows:
        half = all_pack.shape[0] // 2
        mine_pack = at.across(lax.dynamic_slice_in_dim(all_pack, at.bit(1) * half, half, 0))
    token_total = seg_rows * groups * at.ctx * at.fsdp
    factor = (2.0 * token_total / valid_count).reshape(1)
    output, grad_sum, g0, g1, g2, g3, act, hidden, normed, branch, attn, small = middle(
        place, factor, tokens, teacher, contexts, vectors, weights
    )
    if two_rows:
        mine_pack, g0, g1, g2, g3 = lax.optimization_barrier((mine_pack, g0, g1, g2, g3))
        packs = (all_pack, mine_pack, at.swap(mine_pack, 1))
    else:
        by_row = lax.all_gather(all_pack, "fsdp", axis=0, tiled=False)
        by_row = by_row.reshape(at.fsdp, head_splits, shard_rows, pack_cols)
        whole = by_row.transpose(1, 0, 2, 3).reshape(head_splits, width, pack_cols)
        near, far = whole[:, : width // 2], whole[:, width // 2 :]
        flat = lambda pack: pack.reshape(-1, pack_cols)
        packs = (flat(near), flat(far[:2]), flat(far[2:]))
    grads = at.groups([g0, g1, g2, g3])

    over = lambda bit: lambda block: at.swap(block, bit)
    order = Order(place)

    def add(total, shape, move, *others):
        total.keep, give = add_split(
            order.next(*others), total.keep.reshape(shape), total.got.reshape(shape)
        )
        total.got = move(give)
        order.did(total)

    heads, q_grads = [], []

    def back(*others):
        head = len(heads)
        keep, give, q_grad = attend_back(
            order.next(*others), head, q_line, stats, context, grads, kv_pieces, aug
        )
        heads.append(Sum(keep, at.swap(give, 1)))
        q_grads.append(q_grad)
        order.did(heads[-1])

    def head_add(head, *others):
        for bit in at.ring_bits[-2::-1]:
            add(heads[head], (2, -1, 128), over(bit), *others)

    if at.fast:
        give_a, keep_a, give_b, keep_b = weight_grads(
            place, act, branch, normed, hidden, contexts, attn, small
        )
        give_a, give_b, grads = lax.optimization_barrier((give_a, give_b, grads))
        part_a, part_b = Sum(keep_a, at.swap(give_a, 1)), Sum(keep_b, at.swap(give_b, 1))
        shape_a, shape_b = (2, -1, 96, width), (2, -1, 128, width)
        add(part_a, shape_a, at.across)
        add(part_b, shape_b, over(2))
        back()
        back()
        head_add(0)
        add(part_a, shape_a, over(2))
        add(part_b, shape_b, at.across)
        back()
        head_add(1, heads[0])
        add(part_a, shape_a, over(4))
        add(part_b, shape_b, over(4))
        head_add(2)
        add(part_a, shape_a, over(8))
        add(part_b, shape_b, over(8))
        keeps, gots = [head.keep for head in heads], [head.got for head in heads]
        r0, r1, r2, r3, give, keep = project_back(order.next(), q_grads, keeps, gots, blocks)
        keep, part_a.got, part_b.got = lax.optimization_barrier((keep, part_a.got, part_b.got))
        qkv = Sum(keep, at.swap(give, 1))
        order.did(qkv)
        rows = at.groups([r0, r1, r2, r3])
        own_a = Sum(part_a.close().reshape(96, width), None)
        own_b = Sum(part_b.close().reshape(128, width), None)
        small = own_b.keep[120:].astype(wide_type)
        own_a.got, own_b.got = at.swap(own_a.keep, 8), at.swap(own_b.keep, 8)

        def joined(own, bit):
            own.keep = jnp.stack([own.keep, own.got])
            own.got = at.swap(own.keep, bit)

        qkv_shape = (2, -1, qkv.keep.shape[-2], pack_cols)
        add(qkv, qkv_shape, over(8))
        add(qkv, qkv_shape, at.across, own_a, own_b)
        joined(own_a, 4)
        joined(own_b, 2)
        line = Sum(qkv.got, rows[3])
        input_grad = input_back(order.next(line), grad_sum, rows[:3] + [line.got], packs)
        qkv.got = line.keep
        part = Sum(qkv.close().reshape(qkv_shape[2:]), None)
        part.got = at.swap(part.keep, 8)
        joined(own_a, 2)
        joined(own_b, 4)
        here = at.groups([jnp.stack([part.keep, part.got])] * head_splits)
        here, input_grad = lax.optimization_barrier((here, input_grad))
        here = jnp.stack(here)
        mine = lambda bias, k: lax.dynamic_slice_in_dim(bias[k], at.row * shard_rows, shard_rows, 0)
        side = (small[:3, :shard_rows], small[:3, shard_rows:], small[3:5].reshape(-1), jnp.sum(small[5]))
        side, own_a.got = lax.optimization_barrier((side, own_a.got))
        left, right, inner_bias_grad, total_sq = side
        final_gain_grad, outer_bias_grad, attn_shift_grad = left
        final_shift_grad, attn_gain_grad, out_bias_grad = right
        joined(own_a, 1)
        joined(own_b, 1)
        (outer_weight_grad,) = unpack(place, own_a.keep, own_a.got)
        inner_weight_grad, out_weight_grad = unpack(place, own_b.keep, own_b.got)
        query_weight_grad, key_weight_grad, value_weight_grad, bias = qkv_unpack(
            place, here, at.swap(here, 1), width
        )
        query_bias_grad, value_bias_grad = mine(bias, 0), mine(bias, 1)
        outer_weight_grad = outer_weight_grad.reshape(ff_rows, width)
        out_weight_grad = out_weight_grad.reshape(shard_rows, width)
    else:
        for head in range(group_heads):
            back()
            head_add(head)
        keeps, gots = [head.keep for head in heads], [head.got for head in heads]
        r0, r1, r2, r3, _, _ = project_back(place, q_grads, keeps, gots, blocks)
        rows = at.groups([r0, r1, r2, r3])
        input_grad = input_back(place, grad_sum, rows, packs)
        all_rows = jnp.concatenate([r0, r1, r2, r3])
        line = jnp.concatenate(blocks)

        def summed(partial_sum):
            mine = lax.psum_scatter(partial_sum, "fsdp", scatter_dimension=0, tiled=True)
            return lax.psum(mine, "ctx")

        qkv = product(line, all_rows, weight_dims)
        qkv = jnp.concatenate([qkv, jnp.sum(all_rows, axis=0, dtype=wide_type)[None]])
        qkv = lax.dynamic_update_slice(
            jnp.zeros((width + 1, head_splits, pack_cols), wide_type), qkv[:, None], (0, at.group, 0)
        )
        kv = qkv[:, :, : 2 * group_cols].reshape(width + 1, H, 2, head_size)
        parts = [qkv[:, :, 2 * group_cols :], kv[:, :, 0], kv[:, :, 1]]
        parts = [part.reshape(width + 1, width) for part in parts]
        query_weight_grad, key_weight_grad, value_weight_grad = (
            summed(part[:width]) for part in parts
        )
        outer_weight_grad = summed(product(act, branch, weight_dims))
        inner_weight_grad = summed(product(normed, hidden, weight_dims))
        whole = jnp.zeros((width, width), wide_type)
        for k in range(head_splits):
            whole = lax.dynamic_update_slice_in_dim(
                whole, product(contexts[k], attn, weight_dims), (at.group ^ k) * group_cols, 0
            )
        out_weight_grad = summed(whole)
        sums = small[:, :3].reshape(2, 3, 2, width // 2).transpose(1, 2, 0, 3).reshape(6, width)
        sums = jnp.concatenate(
            [sums, parts[0][width:], parts[2][width:], small[:, 3:5].reshape(4, width), small[0, 5:6]]
        )
        sums = lax.psum(sums, ("ctx", "fsdp"))
        mine = lambda k: lax.dynamic_slice_in_dim(sums[k], at.row * shard_rows, shard_rows, 0)
        (
            final_gain_grad, final_shift_grad, outer_bias_grad, attn_gain_grad, attn_shift_grad,
            out_bias_grad, query_bias_grad, value_bias_grad,
        ) = map(mine, range(8))
        inner_bias_grad = lax.dynamic_slice_in_dim(
            sums[8:12].reshape(-1), at.row * ff_rows, ff_rows, 0
        )
        total_sq = jnp.sum(sums[12])
    distill_loss = total_sq / (width * valid_count)
    return (
        distill_loss,
        output.reshape(seg_rows, groups, width),
        input_grad.reshape(seg_rows, groups, width),
        query_weight_grad,
        query_bias_grad,
        key_weight_grad,
        value_weight_grad,
        value_bias_grad,
        out_weight_grad,
        out_bias_grad,
        attn_gain_grad,
        attn_shift_grad,
        inner_weight_grad,
        inner_bias_grad,
        outer_weight_grad,
        outer_bias_grad,
        final_gain_grad,
        final_shift_grad,
    )


def solution(mesh):
    states = P("ctx", "fsdp", None)
    matrix = P("fsdp", None)
    vector = P("fsdp")
    placed = (
        states, states, vector,
        matrix, vector, matrix, matrix, vector, matrix, vector, vector, vector,
        matrix, vector, matrix, vector, vector, vector,
    )
    return jax.shard_map(
        shards,
        mesh=mesh,
        in_specs=placed,
        out_specs=(P(), states, states) + placed[3:],
        check_vma=False,
    )
```

```python
from functools import partial
import math

import jax
import jax.numpy as jnp
from jax import lax
from jax.experimental import pallas as pl
from jax.experimental.pallas import tpu as pltpu
from jax.sharding import PartitionSpec as P

H = 12
head_size = 64
head_splits = 4
group_heads = H // head_splits
group_cols = group_heads * head_size
pack_cols = 3 * group_cols
padded_cols = 640
norm_eps = 1e-12
log_two = math.log(2.0)
masked_score = -1e30
low_type = jnp.bfloat16
wide_type = jnp.float32
score_scale = 1.0 / (log_two * math.sqrt(head_size))
some_vmem, most_vmem = 24 << 20, 58 << 20

plain_dims = (((1,), (0,)), ((), ()))
back_dims = (((1,), (1,)), ((), ()))
weight_dims = (((0,), (0,)), ((), ()))

in_smem = pl.BlockSpec(memory_space=pltpu.SMEM)
in_vmem = pl.BlockSpec(memory_space=pltpu.VMEM)
in_any = pl.BlockSpec(memory_space=pl.ANY)


def product(left_op, right_op, dims=plain_dims):
    return lax.dot_general(left_op, right_op, dims, preferred_element_type=wide_type)


def lanes_of(shape):
    return lax.broadcasted_iota(jnp.int32, shape, 1)


def compiled(name, vmem=some_vmem):
    return dict(
        name=name,
        cost_estimate=pl.CostEstimate(flops=1, bytes_accessed=1, transcendentals=0),
        compiler_params=pltpu.CompilerParams(vmem_limit_bytes=vmem),
    )


class Sum:
    def __init__(self, keep, got):
        self.keep, self.got = keep, got

    def close(self):
        return (self.keep.astype(wide_type) + self.got.astype(wide_type)).astype(low_type)


class Order:
    def __init__(self, place):
        self.place, self.last = place, []

    def next(self, *others):
        names = self.last + [(other, "got") for other in others]
        values = [getattr(owner, name) for owner, name in names]
        place, *values = lax.optimization_barrier((self.place, *values))
        for (owner, name), value in zip(names, values):
            setattr(owner, name, value)
        return place

    def did(self, owner, name="keep"):
        self.last = [(owner, name)]


def low_array(*shape):
    return jax.ShapeDtypeStruct(shape, low_type)


def wide_array(*shape):
    return jax.ShapeDtypeStruct(shape, wide_type)


def head_front(tile, head):
    begin = head // 2 * 128
    if begin + 128 <= tile.shape[1]:
        part = tile[:, begin : begin + 128]
        if head % 2:
            part = pltpu.roll(part, 64, 1)
    else:
        part = jnp.concatenate([tile[:, begin:], jnp.zeros_like(tile[:, begin:])], axis=1)
    return jnp.where(lanes_of(part.shape) < 64, part, 0.0)


def head_rear(tile, head):
    begin = head // 2 * 128
    if begin + 128 <= tile.shape[1]:
        part = tile[:, begin : begin + 128]
        if head % 2 == 0:
            part = pltpu.roll(part, 64, 1)
    else:
        part = jnp.concatenate([jnp.zeros_like(tile[:, begin:]), tile[:, begin:]], axis=1)
    return jnp.where(lanes_of(part.shape) >= 64, part, 0.0)


(at_row, at_core, at_x, at_z, at_group, at_ring, at_first, at_length, at_near, at_mine, at_other) = range(11)


def pack_kernel(place_ref, q_ref, k_ref, v_ref, all_ref, own_ref):
    rows = q_ref.shape[0]
    for group in range(head_splits):
        part = pl.ds(group * rows, rows)
        for head in range(group_heads):
            begin = (group * group_heads + head) * head_size
            all_ref[part, head * 128 : head * 128 + 64] = k_ref[:, begin : begin + head_size]
            all_ref[part, head * 128 + 64 : head * 128 + 128] = v_ref[:, begin : begin + head_size]
        all_ref[part, 2 * group_cols : pack_cols] = q_ref[:, group * group_cols : (group + 1) * group_cols]
        all_ref[part, pack_cols:] = jnp.zeros((rows, padded_cols - pack_cols), low_type)
    own = pl.ds(pl.multiple_of(place_ref[at_group] * rows, rows), rows)
    own_ref[...] = all_ref[own, :pack_cols]


def pack_weights(place, query_weight, key_weight, value_weight):
    rows = query_weight.shape[0]
    return pl.pallas_call(
        pack_kernel,
        in_specs=[in_smem] + [in_vmem] * 3,
        out_specs=[in_vmem] * 2,
        out_shape=[low_array(head_splits * rows, padded_cols), low_array(rows, pack_cols)],
        **compiled("pack_weights", most_vmem),
    )(place, query_weight, key_weight, value_weight)


def whole_vector(place_ref, own_ref, other_ref, begin, size):
    own = own_ref[:, begin : begin + size].astype(wide_type)
    other = other_ref[:, begin : begin + size].astype(wide_type)
    first = place_ref[at_near] == 0
    return jnp.concatenate([jnp.where(first, own, other), jnp.where(first, other, own)], axis=1)


def ship_kernel(place_ref, out_ref, inner_ref, outer_ref, ship_ref, sems):
    width = out_ref.shape[1]
    copies = []
    start = 0

    def send(ref, cols):
        nonlocal start
        half = ref.shape[0] // 2
        source = ref.at[pl.ds(pl.multiple_of(place_ref[at_mine] * half, half), half), cols]
        copies.append(
            pltpu.make_async_copy(source, ship_ref.at[pl.ds(start, half), :], sems.at[len(copies)])
        )
        copies[-1].start()
        start += half

    send(outer_ref, pl.ds(0, width))
    for k in range(0, inner_ref.shape[1], width):
        send(inner_ref, pl.ds(k, width))
    send(out_ref, pl.ds(0, width))
    for copy in copies:
        copy.wait()


def shipment(place, weights):
    width = weights[0].shape[1]
    chunks = weights[1].shape[1] // width
    rows = (weights[0].shape[0] + weights[1].shape[0] * chunks + weights[2].shape[0]) // 2
    return pl.pallas_call(
        ship_kernel,
        in_specs=[in_smem] + [in_any] * 3,
        out_specs=in_vmem,
        out_shape=low_array(rows, width),
        scratch_shapes=[pltpu.SemaphoreType.DMA((chunks + 2,))],
        **compiled("shipment", most_vmem),
    )(place, *weights)


def project_kernel(place_ref, x0, x1, x2, x3, own_ref, other_ref, near_ref, far_ref, q_ref, kv_ref):
    half = own_ref.shape[0]
    rows = x0.shape[0]
    near = pl.multiple_of(place_ref[at_near] * half, 128)
    far = pl.multiple_of((1 - place_ref[at_near]) * half, 128)
    kv_cols = 2 * group_cols
    biases = [whole_vector(place_ref, near_ref, far_ref, k * half, half) for k in range(2)]
    q_bias, v_bias = [jnp.zeros((1, group_cols), wide_type)] * 2
    for group in range(head_splits):
        cols = slice(group * group_cols, (group + 1) * group_cols)
        q_bias = jnp.where(place_ref[at_group] == group, biases[0][:, cols], q_bias)
        v_bias = jnp.where(place_ref[at_group] == group, biases[1][:, cols], v_bias)
    kv_bias = []
    for head in range(group_heads):
        kv_bias += [jnp.zeros((1, head_size), wide_type), v_bias[:, head * 64 : head * 64 + 64]]
    bias = jnp.concatenate(kv_bias + [q_bias], axis=1)
    for k, x_ref in enumerate((x0, x1, x2, x3)):
        part = pl.ds(k * rows, rows)
        made = product(x_ref[:, pl.ds(near, half)], own_ref[...])
        made = made + product(x_ref[:, pl.ds(far, half)], other_ref[...]) + bias
        kv_ref[part, :] = made[:, :kv_cols].astype(low_type)
        q_ref[part, :] = (made[:, kv_cols:] * score_scale).astype(low_type)


def project(place, blocks, own, other, vectors):
    rows, width = blocks[0].shape
    line = rows * head_splits
    return pl.pallas_call(
        project_kernel,
        in_specs=[in_smem] + [in_vmem] * 8,
        out_specs=[in_vmem] * 2,
        out_shape=[low_array(line, group_cols), low_array(line, 2 * group_cols)],
        **compiled("project", most_vmem),
    )(place, *blocks, own, other, *vectors)


def attend_kernel(starts, resumed, finished, place_ref, q_ref, *refs):
    pieces = len(starts)
    kv_refs, aug_ref = refs[:pieces], refs[pieces]
    refs = refs[pieces + 1 :]
    state_ref, out_refs = (refs[0], refs[1:]) if resumed else (None, refs)
    rows = q_ref.shape[0]
    joints = [[]]
    for k, kv_ref in enumerate(kv_refs):
        if sum(kv_refs[n].shape[0] for n in joints[-1]) + kv_ref.shape[0] > 2048:
            joints.append([])
        joints[-1].append(k)
    lane = lanes_of((rows, 128))
    q_aug = jnp.where(lane == 0, 1.0, 0.0).astype(low_type)
    stats = jnp.zeros((rows, 128), wide_type)
    q_wide = q_ref[...].astype(wide_type)
    outs = []
    for head in range(group_heads):
        cols = pl.ds(head * 128, 128)
        q_ext = jnp.concatenate([head_front(q_wide, head).astype(low_type), q_aug], axis=1)
        top = None
        if resumed:
            accum = state_ref[:, cols]
            total, top = accum[:, 0:1], accum[:, 1:2]
        for joint in joints:
            kv_ext = jnp.concatenate(
                [
                    jnp.concatenate(
                        [kv_refs[k][:, cols], aug_ref[pl.ds(starts[k], kv_refs[k].shape[0]), :]],
                        axis=1,
                    )
                    for k in joint
                ],
                axis=0,
            )
            scores = product(q_ext, kv_ext, back_dims)
            new_top = jnp.floor(jnp.max(scores, axis=1, keepdims=True))
            if top is not None:
                new_top = jnp.maximum(top, new_top)
            weights = jnp.exp2(scores - new_top).astype(low_type)
            part_sum = product(weights, kv_ext)
            part_total = part_sum[:, 129:130]
            if top is None:
                accum, total = part_sum[:, :128], part_total
            else:
                factor = jnp.exp2(top - new_top)
                accum, total = accum * factor + part_sum[:, :128], total * factor + part_total
            top = new_top
        if finished:
            outs.append(accum / total)
            stats = jnp.where(lane == head, top, stats)
            stats = jnp.where(lane == group_heads + head, total, stats)
        else:
            out_refs[0][:, cols] = jnp.where(lane == 0, total, jnp.where(lane == 1, top, accum))
    if not finished:
        return
    low_refs, wide_ref, stat_ref = out_refs[:head_splits], out_refs[-2], out_refs[-1]
    tiles = []
    for head in range(0, group_heads, 2):
        first = pltpu.roll(outs[head], 64, 1)
        if head + 1 < group_heads:
            tiles.append(jnp.where(lane < 64, first, outs[head + 1]))
        else:
            tiles.append(first[:, :64])
    context = jnp.concatenate(tiles, axis=1)
    wide_ref[...] = context
    stat_ref[...] = stats
    for k, low_ref in enumerate(low_refs):

        @pl.when(pl.program_id(0) == k)
        def _():
            low_ref[...] = context.astype(low_type)


def attend(place, q_line, kv_pieces, order, aug, state, finished):
    line = q_line.shape[0]
    tile = line // head_splits
    whole = lambda i: (0, 0)
    by_tile = lambda i: (i, 0)
    sizes = [piece.shape[0] for piece in kv_pieces]
    used = [kv_pieces[k] for k in order]
    starts = [sum(sizes[:k]) for k in order]
    states = [] if state is None else [state]
    state_cols = 128 * group_heads
    work = line * group_heads * used[0].shape[0] * len(used)
    if finished:
        out_specs = [pl.BlockSpec((tile, group_cols), whole)] * head_splits
        out_specs += [pl.BlockSpec((tile, group_cols), by_tile), pl.BlockSpec((tile, 128), by_tile)]
        out_shape = [low_array(tile, group_cols)] * head_splits
        out_shape += [wide_array(line, group_cols), wide_array(line, 128)]
    else:
        out_specs = pl.BlockSpec((tile, state_cols), by_tile)
        out_shape = wide_array(line, state_cols)
    return pl.pallas_call(
        partial(attend_kernel, starts, state is not None, finished),
        grid=(head_splits,),
        in_specs=[in_smem, pl.BlockSpec((tile, group_cols), by_tile)]
        + [pl.BlockSpec(piece.shape, whole) for piece in used]
        + [pl.BlockSpec(aug.shape, whole)]
        + [pl.BlockSpec((tile, state_cols), by_tile) for _ in states],
        out_specs=out_specs,
        out_shape=out_shape,
        **compiled("attend"),
    )(place, q_line, *used, aug, *states)


def split_three(number):
    first = number.astype(low_type).astype(wide_type)
    second = (number - first).astype(low_type).astype(wide_type)
    return first, second, number - first - second


def attend_back_kernel(head, pieces, first, outs, query_part, place_ref, q_ref, stat_ref, context_ref, g0, g1, g2, g3, *refs):
    kv_refs, aug_ref = refs[:pieces], refs[pieces]
    sum_refs = refs[pieces + 1 : pieces + 1 + outs]
    q_grad_ref, kv_all, q_ext, g_ext = refs[pieces + 1 + outs :]
    rows = q_ref.shape[0]
    query_rows = q_ref.shape[0]
    seg_rows = g0.shape[0]
    step = pl.program_id(0)

    @pl.when(step == 0)
    def _():
        q_grad_ref[...] = jnp.zeros_like(q_grad_ref)
        start = 0
        for kv_ref in kv_refs:
            kv_all[pl.ds(start, kv_ref.shape[0]), :] = kv_ref[...]
            start += kv_ref.shape[0]
        for k, grad_ref in enumerate((g0, g1, g2, g3)):
            part = pl.ds(k * seg_rows, seg_rows)
            lane = lanes_of((seg_rows, 128))
            stats = stat_ref[part, :]
            top = stats[:, head : head + 1]
            total = stats[:, group_heads + head : group_heads + head + 1]
            grad = head_rear(grad_ref[...].astype(wide_type), head)
            context = head_rear(context_ref[part, :], head)
            delta = jnp.sum(grad * context, axis=1, keepdims=True) / total
            q_more = jnp.where(lane == 0, 1.0, 0.0)
            g_more = jnp.zeros((seg_rows, 128), wide_type)
            for place, (of_top, of_delta) in enumerate(zip(split_three(top), split_three(delta))):
                q_more = jnp.where(lane == place + 1, -of_top, q_more)
                g_more = jnp.where(lane == place + 1, -of_delta, g_more)
            q_ext[part, :128] = head_front(q_ref[part, :].astype(wide_type), head).astype(low_type)
            q_ext[part, 128:] = q_more.astype(low_type)
            g_ext[part, :128] = (grad / total).astype(low_type)
            g_ext[part, 128:] = g_more.astype(low_type)

    kv_part = kv_all[pl.ds(pl.multiple_of(step * rows, rows), rows), :]
    aug_part = aug_ref[pl.ds(pl.multiple_of(first + step * rows, rows), rows), :]
    kv_ext = jnp.concatenate([kv_part, aug_part], axis=1)
    keys_turned = jnp.transpose(kv_part)[:64]
    accum = jnp.zeros((rows, 128), wide_type)
    for start in range(0, query_rows, query_part):
        part = pl.ds(start, query_part)
        q_part = q_ext[part, :]
        g_part = g_ext[part, :]
        weights = jnp.exp2(product(kv_ext, q_part, back_dims))
        along_values = product(kv_ext, g_part, back_dims)
        grad_scores = (weights * along_values).astype(low_type)
        accum = accum + product(weights.astype(low_type), g_part[:, :128])
        accum = accum + product(grad_scores, q_part[:, :128])
        q_grad_ref[:, part] += product(keys_turned, grad_scores)
    lane = lanes_of((rows, 128))
    made = (accum * jnp.where(lane < 64, log_two, 1.0)).astype(low_type)

    each = kv_all.shape[0] // rows // outs
    for k, sum_ref in enumerate(sum_refs):

        @pl.when(step // each == k)
        def _():
            sum_ref[...] = made


def attend_back(place, head, q_line, stats, context, grads, kv_pieces, order, outs, aug):
    line = q_line.shape[0]
    sizes = [piece.shape[0] for piece in kv_pieces]
    used = [kv_pieces[k] for k in order]
    length = sum(piece.shape[0] for piece in used)
    each = length // line // outs
    whole = lambda i: (0, 0)
    part_of = lambda k: lambda i: (jnp.clip(i - k * each, 0, each - 1), 0)
    *sums, q_grad = pl.pallas_call(
        partial(
            attend_back_kernel, head, len(used), sum(sizes[: order[0]]), outs, math.gcd(line, 512)
        ),
        grid=(length // line,),
        in_specs=[
            in_smem,
            pl.BlockSpec(q_line.shape, whole),
            pl.BlockSpec(stats.shape, whole),
            pl.BlockSpec(context.shape, whole),
        ]
        + [pl.BlockSpec(grad.shape, whole) for grad in grads]
        + [pl.BlockSpec((piece.shape[0], 128), lambda i: (0, head)) for piece in used]
        + [pl.BlockSpec(aug.shape, whole)],
        out_specs=[pl.BlockSpec((line, 128), part_of(k)) for k in range(outs)]
        + [pl.BlockSpec((head_size, line), whole)],
        out_shape=[low_array(line * each, 128)] * outs + [wide_array(head_size, line)],
        scratch_shapes=[
            pltpu.VMEM((length, 128), low_type),
            pltpu.VMEM((line, 256), low_type),
            pltpu.VMEM((line, 256), low_type),
        ],
        **compiled("attend_back"),
    )(place, q_line, stats, context, *grads, *used, aug)
    return sums, q_grad


def add_pairs_kernel(place_ref, *refs):
    out_ref = refs[-1]
    for k in range(out_ref.shape[0]):
        total = refs[2 * k][...].astype(wide_type) + refs[2 * k + 1][...].astype(wide_type)
        out_ref[k] = total.astype(low_type)


def add_pairs(place, *arrays):
    return pl.pallas_call(
        add_pairs_kernel,
        in_specs=[in_smem] + [in_vmem] * len(arrays),
        out_specs=in_vmem,
        out_shape=low_array(len(arrays) // 2, *arrays[0].shape),
        **compiled("add_pairs"),
    )(place, *arrays)


def add_merge_kernel(place_ref, *refs):
    keep_ref, give_ref = refs[-2:]
    start = 0
    for kept, got in ((refs[0], refs[1]), (refs[2], refs[3])):
        total = (kept[...].astype(wide_type) + got[...].astype(wide_type)).astype(low_type)
        rows = kept.shape[2]
        keep_ref[:, start : start + rows, :] = total[0]
        give_ref[:, start : start + rows, :] = total[1]
        start += rows


def add_merge(place, keep_a, got_a, keep_b, got_b):
    shape = (keep_a.shape[1], keep_a.shape[2] + keep_b.shape[2], keep_a.shape[3])
    return pl.pallas_call(
        add_merge_kernel,
        in_specs=[in_smem] + [in_vmem] * 4,
        out_specs=[in_vmem] * 2,
        out_shape=[low_array(*shape)] * 2,
        **compiled("add_merge"),
    )(place, keep_a, got_a, keep_b, got_b)


def norm_forward(hidden):
    centre = hidden - jnp.mean(hidden, axis=1, keepdims=True)
    inverse = lax.rsqrt(jnp.mean(centre * centre, axis=1, keepdims=True) + norm_eps)
    return centre * inverse, inverse


def norm_back(grad, normal, inverse):
    along = jnp.mean(grad * normal, axis=1, keepdims=True)
    return inverse * (grad - jnp.mean(grad, axis=1, keepdims=True) - normal * along)


def over_tokens(array):
    return jnp.sum(array, axis=0, keepdims=True)


def mid_kernel(place_ref, factor_ref, x_ref, teacher_ref, c0, c1, c2, c3, near_ref, far_ref, *refs):
    own_weights, shipments = refs[0:3], refs[3:5]
    (
        output_ref, sum_ref, d0, d1, d2, d3, act_ref, hidden_ref, normed_ref, branch_ref, attn_ref, small_ref,
        w_out, w_inner, w_outer, slope_ref, sems,
    ) = refs[5:]
    held = (w_out, w_inner, w_outer)
    near, mine = place_ref[at_near], place_ref[at_mine]
    copies = []
    width = x_ref.shape[1]

    def fetch(source, k, start, rows, cols=None):
        target = held[k].at[pl.ds(pl.multiple_of(start, rows), rows), :]
        if cols is not None:
            target = held[k].at[pl.ds(pl.multiple_of(start, rows), rows), cols]
        copies.append(pltpu.make_async_copy(source, target, sems.at[len(copies)]))
        copies[-1].start()

    halves = [weight.shape[0] // 2 for weight in own_weights]
    starts = [
        [(1 - near) * 2 * half + core * half for half in halves] for core in (mine, 1 - mine)
    ]
    out_half, inner_half, outer_half = halves
    chunks = own_weights[1].shape[1] // width
    base = outer_half + chunks * inner_half
    fetch(own_weights[0], 0, near * 2 * out_half, 2 * out_half)
    for ship, (out_start, _, _) in zip(shipments, starts):
        fetch(ship.at[pl.ds(base, out_half), :], 0, out_start, out_half)
    fetch(own_weights[1], 1, near * 2 * inner_half, 2 * inner_half)
    fetch(own_weights[2], 2, near * 2 * outer_half, 2 * outer_half)
    for ship, (_, inner_start, outer_start) in zip(shipments, starts):
        for k in range(chunks):
            source = ship.at[pl.ds(outer_half + k * inner_half, inner_half), :]
            fetch(source, 1, inner_start, inner_half, pl.ds(k * width, width))
        fetch(ship.at[pl.ds(0, outer_half), :], 2, outer_start, outer_half)
    rows = x_ref.shape[0]
    half = width // 2
    vector = lambda k, size: whole_vector(place_ref, near_ref, far_ref, k * half, size)
    b_out, g_attn, s_attn, b_outer, g_final, s_final = (vector(k, half) for k in range(2, 8))
    b_inner = vector(8, w_outer.shape[0] // 2)
    group = place_ref[at_group]
    of_group = lambda k: pl.ds(pl.multiple_of((group ^ k) * group_cols, group_cols), group_cols)

    for copy in copies[0:3]:
        copy.wait()
    hidden = x_ref[...].astype(wide_type) + b_out
    for k, c_ref in enumerate((c0, c1, c2, c3)):
        hidden = hidden + product(c_ref[...], w_out[of_group(k), :])
    attn_normal, attn_inverse = norm_forward(hidden)
    normed = attn_normal * g_attn + s_attn
    normed_low = normed.astype(low_type)
    normed_ref[...] = normed_low
    for copy in copies[3:]:
        copy.wait()
    branch = normed + b_outer
    for k in range(chunks):
        cols = pl.ds(k * width, width)
        pre = product(normed_low, w_inner[:, cols]) + b_inner[:, k * width : (k + 1) * width]
        bell = 0.5 * (1.0 + lax.erf(pre * math.sqrt(0.5)))
        slope_ref[:, cols] = bell + pre * jnp.exp(-0.5 * pre * pre) * (1.0 / math.sqrt(2.0 * math.pi))
        act = (pre * bell).astype(low_type)
        act_ref[:, cols] = act
        branch = branch + product(act, w_outer[cols, :])
    final_normal, final_inverse = norm_forward(branch)
    output = final_normal * g_final + s_final
    output_ref[:, 0, :] = output
    token = place_ref[at_first] + lax.broadcasted_iota(jnp.int32, (rows, 1), 0)
    valid = (token < place_ref[at_length]).astype(wide_type)
    mismatch = (output - teacher_ref[...].astype(wide_type)) * valid
    squares = over_tokens(mismatch * mismatch)
    grad_out = mismatch * factor_ref[0]
    final_gain_grad = over_tokens(grad_out * final_normal)
    final_shift_grad = over_tokens(grad_out)
    grad_mid = norm_back(grad_out * g_final, final_normal, final_inverse)
    grad_branch = grad_mid.astype(low_type)
    branch_ref[...] = grad_branch
    outer_bias_grad = over_tokens(grad_branch.astype(wide_type))
    grad_normed = grad_mid
    inner_bias_grad = []
    for k in range(chunks):
        cols = pl.ds(k * width, width)
        grad_act = product(grad_branch, w_outer[cols, :], back_dims)
        grad_hidden = (grad_act * slope_ref[:, cols]).astype(low_type)
        hidden_ref[:, cols] = grad_hidden
        inner_bias_grad.append(over_tokens(grad_hidden.astype(wide_type)))
        grad_normed = grad_normed + product(grad_hidden, w_inner[:, cols], back_dims)
    attn_gain_grad = over_tokens(grad_normed * attn_normal)
    attn_shift_grad = over_tokens(grad_normed)
    grad_sum = norm_back(grad_normed * g_attn, attn_normal, attn_inverse)
    sum_ref[...] = grad_sum
    grad_attn = grad_sum.astype(low_type)
    attn_ref[...] = grad_attn
    out_bias_grad = over_tokens(grad_attn.astype(wide_type))
    for k, d_ref in enumerate((d0, d1, d2, d3)):
        d_ref[...] = product(grad_attn, w_out[of_group(k), :], back_dims).astype(low_type)
    pairs = (
        (final_gain_grad, final_shift_grad),
        (outer_bias_grad, attn_gain_grad),
        (attn_shift_grad, out_bias_grad),
    )
    for side in range(2):
        cols = slice(side * half, side * half + half)
        lines = [jnp.concatenate([a[:, cols], b[:, cols]], axis=1) for a, b in pairs]
        lines += inner_bias_grad[side * 2 : side * 2 + 2] + [squares]
        lines.append(jnp.zeros((8 - len(lines), width), wide_type))
        small_ref[side] = jnp.concatenate(lines, axis=0)


def middle(place, factor, tokens, teacher, contexts, vectors, weights):
    rows, width = tokens.shape
    ff_width = weights[1].shape[1]
    return pl.pallas_call(
        mid_kernel,
        in_specs=[in_smem, in_smem] + [in_vmem] * 8 + [in_any] * 5,
        out_specs=[in_vmem] * 12,
        out_shape=[wide_array(rows, 1, width), wide_array(rows, width)]
        + [low_array(rows, group_cols)] * 4
        + [low_array(rows, ff_width)] * 2
        + [low_array(rows, width)] * 3
        + [wide_array(2, 8, width)],
        scratch_shapes=[
            pltpu.VMEM((width, width), low_type),
            pltpu.VMEM((width, ff_width), low_type),
            pltpu.VMEM((ff_width, width), low_type),
            pltpu.VMEM((rows, ff_width), wide_type),
            pltpu.SemaphoreType.DMA((5 + 2 * (1 + ff_width // width),)),
        ],
        **compiled("middle", most_vmem),
    )(place, factor, tokens, teacher, *contexts, *vectors, *weights)


def weight_kernel(
    place_ref, act_ref, branch_ref, normed_ref, hidden_ref, c0, c1, c2, c3, attn_ref, small_ref,
    give_a, keep_a, give_b, keep_b, out_grad,
):
    width = branch_ref.shape[1]
    half = width // 2
    group = place_ref[at_group]

    @pl.when((pl.program_id(0) == 0) & (pl.program_id(1) == 0))
    def _():
        for k, c_ref in enumerate((c0, c1, c2, c3)):
            part = pl.ds(pl.multiple_of((group ^ k) * group_cols, group_cols), group_cols)
            out_grad[part, :] = product(c_ref[...], attn_ref[...], weight_dims)

    row = place_ref[at_row] ^ pl.program_id(0)
    x = place_ref[at_x] ^ pl.program_id(1)
    for far, a_ref, b_ref in ((1, give_a, give_b), (0, keep_a, keep_b)):
        core = place_ref[at_core] ^ far
        begin = pl.multiple_of(((row * 2 + core) * 2 + x) * half, 128)
        outer = product(
            act_ref[:, pl.ds(begin, half)], branch_ref[...], weight_dims
        ).astype(low_type)
        inner = product(
            normed_ref[:, pl.ds(pl.multiple_of(row * half, 128), half)],
            hidden_ref[:, pl.ds(pl.multiple_of((core * 2 + x) * width, 128), width)],
            weight_dims,
        ).astype(low_type)
        base = row * half + core * (half // 2) + x * (half // 4)
        for z in range(4):
            apart = place_ref[at_z] ^ z
            spot = (apart & 1) * 2 + (apart >> 1)
            rows = slice(z * 96, z * 96 + 96)
            a_ref[0, 0, pl.ds(pl.multiple_of(spot * 96, 32), 96), :] = outer[rows]
            b_ref[0, 0, pl.ds(pl.multiple_of(spot * 128, 128), 96), :] = inner[rows]
            rest = out_grad[pl.ds(pl.multiple_of(base + z * 24, 8), 24), :]
            rest = jnp.concatenate([rest, small_ref[pl.ds(row, 1)][0]], axis=0)
            b_ref[0, 0, pl.ds(pl.multiple_of(spot * 128 + 96, 32), 32), :] = rest.astype(low_type)


def weight_grads(place, act, branch, normed, hidden, contexts, attn, small):
    rows, width = branch.shape
    a_shape, b_shape = (2, 2, width // 2, width), (2, 2, 512, width)
    a_spec = pl.BlockSpec((1, 1) + a_shape[2:], lambda i, j: (i, j, 0, 0))
    b_spec = pl.BlockSpec((1, 1) + b_shape[2:], lambda i, j: (j, i, 0, 0))
    return pl.pallas_call(
        weight_kernel,
        grid=(2, 2),
        in_specs=[in_smem] + [in_vmem] * 10,
        out_specs=[a_spec, a_spec, b_spec, b_spec],
        out_shape=[low_array(*a_shape)] * 2 + [low_array(*b_shape)] * 2,
        scratch_shapes=[pltpu.VMEM((width, width), wide_type)],
        **compiled("weight_grads", most_vmem),
    )(place, act, branch, normed, hidden, *contexts, attn, small)


def add_split_kernel(place_ref, kept_ref, got_ref, keep_ref, give_ref):
    total = kept_ref[...].astype(wide_type) + got_ref[...].astype(wide_type)
    keep_ref[...] = total[0].astype(low_type)
    give_ref[...] = total[1].astype(low_type)


def add_split(place, kept, got):
    cols = kept.shape[-1]
    shape = (2, kept.size // cols // 2, cols)
    tile = math.gcd(shape[1], 512)
    both = pl.BlockSpec((2, tile, cols), lambda i: (0, i, 0))
    one = pl.BlockSpec((tile, cols), lambda i: (i, 0))
    keep, give = pl.pallas_call(
        add_split_kernel,
        grid=(shape[1] // tile,),
        in_specs=[in_smem, both, both],
        out_specs=[one, one],
        out_shape=[low_array(*shape[1:])] * 2,
        **compiled("add_split"),
    )(place, kept.reshape(shape), got.reshape(shape))
    return keep.reshape(kept.shape[1:]), give.reshape(kept.shape[1:])


def unpack_kernel(place_ref, own_ref, got_ref, *refs):
    width = own_ref.shape[-1]
    half = width // 2
    out_refs, wide, sems = refs[:-2], refs[-2], refs[-1]
    copies = []

    def send(source, target):
        copy = pltpu.make_async_copy(source, target, sems.at[len(copies)])
        copy.start()
        copies.append(copy)

    for k in range(16):
        ref = got_ref if k // 8 else own_ref
        core = place_ref[at_core] ^ (k // 8)
        x = place_ref[at_x] ^ (k // 4 % 2)
        z = place_ref[at_z] ^ (k // 2 % 2 + 2 * (k % 2))
        if len(out_refs) == 1:
            wide[k] = ref[k // 4 % 2, k // 2 % 2, k % 2].astype(wide_type)
            start = pl.multiple_of((core * 2 + x) * half + z * 96, 32)
            send(wide.at[k], out_refs[0].at[pl.ds(start, 96), :])
        else:
            inner_ref, out_ref = out_refs
            wide[k] = ref[k // 2 % 2, k // 4 % 2, k % 2].astype(wide_type)
            cols = pl.ds(pl.multiple_of((core * 2 + x) * width, 128), width)
            send(wide.at[k, 0:96], inner_ref.at[pl.ds(pl.multiple_of(z * 96, 32), 96), cols])
            start = pl.multiple_of(core * (half // 2) + x * (half // 4) + z * 24, 8)
            send(wide.at[k, 96:120], out_ref.at[pl.ds(start, 24), :])
    for copy in copies:
        copy.wait()


def unpack(place, own, got):
    rows, width = own.shape[3:]
    if rows == 96:
        shapes = [wide_array(2 * width, width)]
    else:
        shapes = [wide_array(width // 2, 4 * width), wide_array(width // 2, width)]
    return pl.pallas_call(
        unpack_kernel,
        in_specs=[in_smem] + [in_vmem] * 2,
        out_specs=[in_any] * len(shapes),
        out_shape=shapes,
        scratch_shapes=[
            pltpu.VMEM((16, rows, width), wide_type), pltpu.SemaphoreType.DMA((16 * len(shapes),))
        ],
        **compiled("unpack"),
    )(place, own, got)


def rows_kernel(counts, terms, place_ref, *refs):
    heads, used = len(counts), sum(counts)
    q_grads, kv_terms = refs[:used], refs[used : used + sum(terms)]
    refs = refs[used + sum(terms) :]
    blocks = refs[:4]
    r0, r1, r2, r3, give_ref, keep_ref, w_grad, all_rows = refs[4:]
    rows, width = blocks[0].shape
    kv_cols = 2 * group_cols
    for k in range(heads):
        total = 0.0
        for n in range(sum(terms[:k]), sum(terms[: k + 1])):
            term = kv_terms[n]
            total = total + (term[...] if len(term.shape) == 2 else term[k]).astype(wide_type)
        all_rows[:, k * 128 : k * 128 + 128] = total.astype(low_type)
    firsts = [sum(counts[:k]) for k in range(heads)]
    turned = [
        sum((ref[...] for ref in q_grads[first + 1 : first + count]), q_grads[first][...])
        for first, count in zip(firsts, counts)
    ]
    turned = jnp.concatenate(turned, axis=0) * 0.125
    all_rows[:, kv_cols:] = jnp.transpose(turned).astype(low_type)
    half = width // 2
    bias = jnp.zeros((1, pack_cols), wide_type)
    for k, r_ref in enumerate((r0, r1, r2, r3)):
        made = all_rows[pl.ds(k * rows, rows), :]
        r_ref[...] = made
        bias = bias + over_tokens(made.astype(wide_type))
        for side in range(2):
            part = product(blocks[k][:, side * half : side * half + half], made, weight_dims)
            if k:
                w_grad[side] += part
            else:
                w_grad[side] = part
    bias = jnp.concatenate([bias, jnp.zeros((15, pack_cols), wide_type)], axis=0)
    for far, piece_ref in ((1, give_ref), (0, keep_ref)):
        start = pl.multiple_of((place_ref[at_core] ^ far) * (half // 2), half // 2)
        for j in range(2):
            row = place_ref[at_row] ^ j
            block = w_grad[pl.ds(row, 1), pl.ds(start, half // 2), :][0]
            piece_ref[j] = jnp.concatenate([block, bias], axis=0).astype(low_type)


def project_back(place, q_grads, kv_terms, blocks):
    counts = [len(q_grad) for q_grad in q_grads]
    terms = [len(head) for head in kv_terms]
    every = [array for head in q_grads + kv_terms for array in head]
    rows, width = blocks[0].shape
    pieces = (2, width // 4 + 16, pack_cols)
    return pl.pallas_call(
        partial(rows_kernel, counts, terms),
        in_specs=[in_smem] + [in_vmem] * (len(every) + 4),
        out_specs=[in_vmem] * 6,
        out_shape=[low_array(rows, pack_cols)] * 4 + [low_array(*pieces)] * 2,
        scratch_shapes=[
            pltpu.VMEM((2, width // 2, pack_cols), wide_type),
            pltpu.VMEM((4 * rows, pack_cols), low_type),
        ],
        **compiled("project_back"),
    )(place, *every, *blocks)


def input_kernel(place_ref, sum_ref, r0, r1, r2, r3, own_ref, mine_ref, other_ref, grad_ref):
    half = own_ref.shape[0] // head_splits
    near = jnp.zeros((sum_ref.shape[0], half), wide_type)
    far = jnp.zeros((sum_ref.shape[0], half), wide_type)
    for k, r_ref in enumerate((r0, r1, r2, r3)):
        group = place_ref[at_group] ^ k
        near = near + product(r_ref[...], own_ref[pl.ds(pl.multiple_of(group * half, half), half), :pack_cols], back_dims)
        fetched = (group >> 1) == place_ref[at_mine]
        side = pl.ds(pl.multiple_of((group & 1) * half, half), half)
        weight = jnp.where(fetched, mine_ref[side, :pack_cols], other_ref[side, :pack_cols])
        far = far + product(r_ref[...], weight, back_dims)
    for part, begin in ((near, place_ref[at_near]), (far, 1 - place_ref[at_near])):
        cols = pl.ds(pl.multiple_of(begin * half, 128), half)
        grad_ref[:, 0, cols] = sum_ref[:, cols] + part


def input_back(place, grad_sum, rows, packs):
    return pl.pallas_call(
        input_kernel,
        in_specs=[in_smem] + [in_vmem] * 8,
        out_specs=in_vmem,
        out_shape=wide_array(grad_sum.shape[0], 1, grad_sum.shape[1]),
        **compiled("input_back"),
    )(place, grad_sum, *rows, *packs)


def qkv_unpack_kernel(place_ref, here_ref, there_ref, q_ref, k_ref, v_ref, bias_ref):
    side = q_ref.shape[0] // 2
    bias_ref[...] = jnp.zeros_like(bias_ref)
    for own in range(head_splits):

        @pl.when(place_ref[at_group] == own)
        def _():
            for n, piece in enumerate((here_ref, there_ref)):
                part = pl.ds(pl.multiple_of((place_ref[at_core] ^ n) * side, side), side)
                for k in range(head_splits):
                    first = (own ^ k) * group_cols
                    block = piece[k].astype(wide_type)
                    q_ref[part, first : first + group_cols] = block[:side, 2 * group_cols :]
                    for h in range(group_heads):
                        begin = first + h * head_size
                        keys = slice(h * 128, h * 128 + 64)
                        values = slice(h * 128 + 64, h * 128 + 128)
                        k_ref[part, begin : begin + head_size] = block[:side, keys]
                        v_ref[part, begin : begin + head_size] = block[:side, values]
                        if n == 0:
                            bias_ref[1:2, begin : begin + head_size] = block[side : side + 1, values]
                    if n == 0:
                        bias_ref[0:1, first : first + group_cols] = block[
                            side : side + 1, 2 * group_cols :
                        ]


def qkv_unpack(place, here, there, width):
    return pl.pallas_call(
        qkv_unpack_kernel,
        in_specs=[in_smem] + [in_vmem] * 2,
        out_specs=[in_vmem] * 4,
        out_shape=[wide_array(width // 2, width)] * 3 + [wide_array(8, width)],
        **compiled("qkv_unpack"),
    )(place, here, there)


class Layout:
    def __init__(self):
        self.ctx = lax.axis_size("ctx")
        self.fsdp = lax.axis_size("fsdp")
        self.me = lax.axis_index("ctx")
        self.row = lax.axis_index("fsdp")
        self.fast = self.ctx == 16 and self.fsdp == 2
        group_bits = (2, 4) if self.fast else (self.ctx // 4, self.ctx // 2)
        bits = [1 << k for k in reversed(range(self.ctx.bit_length() - 1))]
        self.ring_bits = [bit for bit in bits if bit not in group_bits]
        self.group = self.bit(group_bits[0]) + 2 * self.bit(group_bits[1])
        self.group_codes = [0, group_bits[0], group_bits[1], group_bits[0] | group_bits[1]]
        self.ring_codes = [0]
        for bit in self.ring_bits:
            self.ring_codes = self.ring_codes + [code | bit for code in self.ring_codes]

    def bit(self, bit):
        return (self.me // bit) % 2

    def swap(self, block, code):
        return lax.ppermute(block, "ctx", [(i, i ^ code) for i in range(self.ctx)])

    def groups(self, blocks):
        return [blocks[0]] + [self.swap(blocks[k], self.group_codes[k]) for k in range(1, 4)]

    def across(self, block):
        return lax.ppermute(block, "fsdp", [(0, 1), (1, 0)])

    def halves(self, shard):
        if self.fsdp == 2:
            return shard, self.across(shard)
        full = lax.all_gather(shard, "fsdp", axis=0, tiled=True)
        half = full.shape[0] // 2
        return full[:half], full[half:]


def shards(
    layer_input,
    teacher_states,
    seq_lengths,
    query_weight,
    query_bias,
    key_weight,
    value_weight,
    value_bias,
    out_weight,
    out_bias,
    attn_gain,
    attn_shift,
    inner_weight,
    inner_bias,
    outer_weight,
    outer_bias,
    final_gain,
    final_shift,
):
    at = Layout()
    seg_rows, groups, width = layer_input.shape
    shard_rows = query_weight.shape[0]
    ff_rows = outer_weight.shape[0]
    ff_width = inner_weight.shape[1]
    tokens = layer_input.reshape(seg_rows, width)
    teacher = teacher_states.reshape(seg_rows, width)
    two_rows = at.fsdp == 2
    place = jnp.stack(
        [
            at.row, at.bit(1), at.bit(2), at.bit(4) + 2 * at.bit(8), at.group, at.bit(8),
            at.me * seg_rows, seq_lengths[0],
            at.row if two_rows else 0, at.bit(1), 0,
        ]
    ).astype(jnp.int32)

    blocks = at.groups([tokens] * 4)
    all_pack, own_pack = pack_weights(place, query_weight, key_weight, value_weight)
    own_pack, other_pack = at.halves(own_pack)
    vectors = (
        query_bias, value_bias, out_bias, attn_gain, attn_shift,
        outer_bias, final_gain, final_shift, inner_bias,
    )
    if two_rows:
        *vectors, own_pack = lax.optimization_barrier((*vectors, own_pack))
        own_vectors = jnp.concatenate(vectors).reshape(1, -1)
        vectors = (own_vectors, at.across(own_vectors))
    else:
        whole = lambda vector: lax.all_gather(vector, "fsdp", axis=0, tiled=True).reshape(2, -1)
        both = jnp.concatenate([whole(vector) for vector in vectors], axis=1)
        vectors = (both[:1], both[1:])
    own_count = jnp.sum(seq_lengths).astype(wide_type)
    weights = [out_weight, inner_weight, outer_weight]
    if two_rows:
        ship, other_pack, vectors, blocks = lax.optimization_barrier(
            (shipment(place, weights), other_pack, vectors, blocks)
        )
        ship = at.across(ship)
    q_line, kv_line = project(place, blocks, own_pack, other_pack, vectors)
    if two_rows:
        own_count, kv_line = lax.optimization_barrier((own_count, kv_line))
        valid_count = own_count + at.across(own_count.reshape(1))[0]
    else:
        valid_count = lax.psum(own_count, "fsdp")

    source = jnp.stack(
        [at.me ^ (ring | group) for ring in at.ring_codes for group in at.group_codes]
    )
    position = (source[:, None] * seg_rows + jnp.arange(seg_rows)[None, :]).reshape(-1, 1)
    lane = lax.broadcasted_iota(jnp.int32, (position.shape[0], 128), 1)
    mask = jnp.where(position < seq_lengths[0], 0.0, masked_score)
    aug = jnp.where(lane == 0, mask, jnp.where(lane < 4, 1.0, 0.0)).astype(low_type)

    if at.fast:
        near = at.swap(kv_line, 1)
        far = at.swap(kv_line, 8)
        state = attend(place, q_line, [kv_line, far, near, far], (0, 2), aug, None, False)
        far, state = lax.optimization_barrier((far, state))
        kv_pieces = [kv_line, far, near, at.swap(far, 1)]
        order = (1, 3)
    else:
        kv_pieces = [kv_line]
        for bit in at.ring_bits:
            kv_pieces = kv_pieces + [at.swap(piece, bit) for piece in kv_pieces]
        state, order = None, tuple(range(len(kv_pieces)))
    *context_low, context, stats = attend(place, q_line, kv_pieces, order, aug, state, True)
    if two_rows:
        ship, stats = lax.optimization_barrier((ship, stats))
        weights += [ship, at.swap(ship, 1)]
    else:
        full = [lax.all_gather(weight, "fsdp", axis=0, tiled=True) for weight in weights]
        far = [weight[weight.shape[0] // 2 :] for weight in full]
        weights = [weight[: weight.shape[0] // 2] for weight in full]
        ship = shipment(place, far)
        weights += [ship, at.swap(ship, 1)]
    contexts = at.groups(context_low)
    token_total = seg_rows * groups * at.ctx * at.fsdp
    factor = (2.0 * token_total / valid_count).reshape(1)
    output, grad_sum, g0, g1, g2, g3, act, hidden, normed, branch, attn, small = middle(
        place, factor, tokens, teacher, contexts, vectors, weights
    )
    if two_rows:
        half = all_pack.shape[0] // 2
        mine_pack = lax.dynamic_slice_in_dim(all_pack, at.bit(1) * half, half, 0)
    else:
        by_row = lax.all_gather(all_pack, "fsdp", axis=0, tiled=False)
        by_row = by_row.reshape(at.fsdp, head_splits, shard_rows, padded_cols)
        whole = by_row.transpose(1, 0, 2, 3).reshape(head_splits, width, padded_cols)
        near, far = whole[:, : width // 2], whole[:, width // 2 :]
        flat = lambda pack: pack.reshape(-1, padded_cols)
        mine = lax.dynamic_slice_in_dim(far, at.bit(1) * 2, 2, 0)
        packs = (flat(near), flat(mine), at.swap(flat(mine), 1))
    grads = at.groups([g0, g1, g2, g3])

    over = lambda bit: lambda block: at.swap(block, bit)
    order = Order(place)

    def add(total, shape, move, *others):
        total.keep, give = add_split(
            order.next(*others), total.keep.reshape(shape), total.got.reshape(shape)
        )
        total.got = move(give)
        order.did(total)

    heads, q_grads = [], []

    def back(*others, split=False):
        args = (len(heads), q_line, stats, context, grads, kv_pieces)
        if split:
            give, first = attend_back(order.next(*others), *args, (2, 3), 2, aug)
            far = Sum(give[1], at.swap(give[1], 1))
            own = Sum(give[0], at.swap(give[0], 1))
            order.did(far)
            keep, second = attend_back(order.next(), *args, (0, 1), 2, aug)
            own.keep, far.keep = keep
            q_grads.append([first, second])
        else:
            sums, first = attend_back(order.next(*others), *args, (0, 1, 2, 3), 4, aug)
            own, far = Sum(sums[0], at.swap(sums[2], 1)), Sum(sums[1], at.swap(sums[3], 1))
            q_grads.append([first])
        order.did(far)
        heads.append((own, far))

    def send_far(*used, needs=()):
        pairs = [array for head in used for array in (heads[head][1].keep, heads[head][1].got)]
        sums = add_pairs(order.next(*needs), *pairs)
        total = Sum(sums, at.swap(sums, 8))
        order.did(total)
        return total

    if at.fast:
        give_a, keep_a, give_b, keep_b = weight_grads(
            place, act, branch, normed, hidden, contexts, attn, small
        )
        give_a, give_b, *grads = lax.optimization_barrier((give_a, give_b, *grads))
        part_a, part_b = Sum(keep_a, at.swap(give_a, 1)), Sum(keep_b, at.swap(give_b, 1))
        shape_a, shape_b = (2, -1, 96, width), (2, -1, 128, width)
        add(part_a, shape_a, at.across)
        add(part_b, shape_b, over(2))
        back()
        back()
        add(part_a, shape_a, over(2))
        add(part_b, shape_b, at.across)
        firsts = send_far(0, 1)
        back(split=True)
        place_now = order.next()
        final_shape = lambda shape: (2, 2) + shape[2:]
        keep, give = add_merge(
            place_now,
            part_a.keep.reshape(final_shape(shape_a)),
            part_a.got.reshape(final_shape(shape_a)),
            part_b.keep.reshape(final_shape(shape_b)),
            part_b.got.reshape(final_shape(shape_b)),
        )
        mine_pack, keep = lax.optimization_barrier((mine_pack, keep))
        mine_pack = at.across(mine_pack)
        packs = (all_pack, mine_pack, at.swap(mine_pack, 1))
        both = Sum(keep, at.swap(give, 4))
        order.did(both)
        lasts = send_far(2, needs=(firsts,))
        add(both, (2, 224, width), over(8), lasts)
        kv_terms = []
        for head, (own, _) in enumerate(heads):
            far = firsts.got if head < 2 else lasts.got[0]
            kv_terms.append([own.keep, own.got, far])
        r0, r1, r2, r3, give, keep = project_back(order.next(), q_grads, kv_terms, blocks)
        qkv = Sum(keep, at.swap(give, 1))
        order.did(qkv)
        rows = at.groups([r0, r1, r2, r3])
        both, qkv.got = lax.optimization_barrier((both.close(), qkv.got))
        small = both[216:].astype(wide_type)
        both_got = at.swap(both, 8)

        def joined(own, bit):
            own.keep = jnp.stack([own.keep, own.got])
            own.got = at.swap(own.keep, bit)

        qkv_shape = (2, -1, qkv.keep.shape[-2], pack_cols)
        add(qkv, qkv_shape, at.across)
        qkv = qkv.close().reshape(qkv_shape[2:])
        qkv = Sum(qkv, at.swap(qkv, 8))
        *rows, both_got = lax.optimization_barrier((*rows, both_got))
        own_a, own_b = Sum(both[:96], both_got[:96]), Sum(both[96:], both_got[96:])
        joined(own_a, 4)
        joined(own_b, 2)
        input_grad = input_back(place, grad_sum, rows, packs)
        qkv.got, input_grad = lax.optimization_barrier((qkv.got, input_grad))
        here = at.groups([qkv.close()] * head_splits)
        joined(own_a, 2)
        joined(own_b, 4)
        here = jnp.stack(here)
        mine = lambda bias, k: lax.dynamic_slice_in_dim(bias[k], at.row * shard_rows, shard_rows, 0)
        side = (small[:3, :shard_rows], small[:3, shard_rows:], small[3:5].reshape(-1), jnp.sum(small[5]))
        side, own_a.got = lax.optimization_barrier((side, own_a.got))
        left, right, inner_bias_grad, total_sq = side
        final_gain_grad, outer_bias_grad, attn_shift_grad = left
        final_shift_grad, attn_gain_grad, out_bias_grad = right
        joined(own_a, 1)
        joined(own_b, 1)
        (outer_weight_grad,) = unpack(place, own_a.keep, own_a.got)
        inner_weight_grad, out_weight_grad = unpack(place, own_b.keep, own_b.got)
        query_weight_grad, key_weight_grad, value_weight_grad, bias = qkv_unpack(
            place, here, at.swap(here, 1), width
        )
        query_bias_grad, value_bias_grad = mine(bias, 0), mine(bias, 1)
    else:
        kv_terms = []
        every = tuple(range(len(kv_pieces)))
        for head in range(group_heads):
            (keep, give), q_grad = attend_back(
                place, head, q_line, stats, context, grads, kv_pieces, every, 2, aug
            )
            q_grads.append([q_grad])
            total = Sum(keep, at.swap(give, 1))
            for bit in at.ring_bits[-2::-1]:
                add(total, (2, -1, 128), over(bit))
            kv_terms.append([total.keep, total.got])
        r0, r1, r2, r3, _, _ = project_back(place, q_grads, kv_terms, blocks)
        rows = at.groups([r0, r1, r2, r3])
        input_grad = input_back(place, grad_sum, rows, packs)
        all_rows = jnp.concatenate([r0, r1, r2, r3])
        line = jnp.concatenate(blocks)

        def summed(partial_sum):
            mine = lax.psum_scatter(partial_sum, "fsdp", scatter_dimension=0, tiled=True)
            return lax.psum(mine, "ctx")

        qkv = product(line, all_rows, weight_dims)
        qkv = jnp.concatenate([qkv, jnp.sum(all_rows, axis=0, dtype=wide_type)[None]])
        qkv = lax.dynamic_update_slice(
            jnp.zeros((width + 1, head_splits, pack_cols), wide_type), qkv[:, None], (0, at.group, 0)
        )
        kv = qkv[:, :, : 2 * group_cols].reshape(width + 1, H, 2, head_size)
        parts = [qkv[:, :, 2 * group_cols :], kv[:, :, 0], kv[:, :, 1]]
        parts = [part.reshape(width + 1, width) for part in parts]
        query_weight_grad, key_weight_grad, value_weight_grad = (
            summed(part[:width]) for part in parts
        )
        outer_weight_grad = summed(product(act, branch, weight_dims))
        inner_weight_grad = summed(product(normed, hidden, weight_dims))
        whole = jnp.zeros((width, width), wide_type)
        for k in range(head_splits):
            whole = lax.dynamic_update_slice_in_dim(
                whole, product(contexts[k], attn, weight_dims), (at.group ^ k) * group_cols, 0
            )
        out_weight_grad = summed(whole)
        sums = small[:, :3].reshape(2, 3, 2, width // 2).transpose(1, 2, 0, 3).reshape(6, width)
        sums = jnp.concatenate(
            [sums, parts[0][width:], parts[2][width:], small[:, 3:5].reshape(4, width), small[0, 5:6]]
        )
        sums = lax.psum(sums, ("ctx", "fsdp"))
        mine = lambda k: lax.dynamic_slice_in_dim(sums[k], at.row * shard_rows, shard_rows, 0)
        (
            final_gain_grad, final_shift_grad, outer_bias_grad, attn_gain_grad, attn_shift_grad,
            out_bias_grad, query_bias_grad, value_bias_grad,
        ) = map(mine, range(8))
        inner_bias_grad = lax.dynamic_slice_in_dim(
            sums[8:12].reshape(-1), at.row * ff_rows, ff_rows, 0
        )
        total_sq = jnp.sum(sums[12])
    distill_loss = total_sq / (width * valid_count)
    return (
        distill_loss,
        output.reshape(seg_rows, groups, width),
        input_grad.reshape(seg_rows, groups, width),
        query_weight_grad,
        query_bias_grad,
        key_weight_grad,
        value_weight_grad,
        value_bias_grad,
        out_weight_grad,
        out_bias_grad,
        attn_gain_grad,
        attn_shift_grad,
        inner_weight_grad,
        inner_bias_grad,
        outer_weight_grad,
        outer_bias_grad,
        final_gain_grad,
        final_shift_grad,
    )


def solution(mesh):
    states = P("ctx", "fsdp", None)
    matrix = P("fsdp", None)
    vector = P("fsdp")
    placed = (
        states, states, vector,
        matrix, vector, matrix, matrix, vector, matrix, vector, vector, vector,
        matrix, vector, matrix, vector, vector, vector,
    )
    return jax.shard_map(
        shards,
        mesh=mesh,
        in_specs=placed,
        out_specs=(P(), states, states) + placed[3:],
        check_vma=False,
    )
```

```python
from functools import partial
import math

import jax
import jax.numpy as jnp
from jax import lax
from jax.experimental import pallas as pl
from jax.experimental.pallas import tpu as pltpu
from jax.sharding import PartitionSpec as P

H = 12
head_size = 64
head_splits = 4
group_heads = H // head_splits
group_cols = group_heads * head_size
pack_cols = 3 * group_cols
padded_cols = 640
norm_eps = 1e-12
log_two = math.log(2.0)
masked_score = -1e30
low_type = jnp.bfloat16
wide_type = jnp.float32
score_scale = 1.0 / (log_two * math.sqrt(head_size))
some_vmem, most_vmem = 24 << 20, 58 << 20

plain_dims = (((1,), (0,)), ((), ()))
back_dims = (((1,), (1,)), ((), ()))
weight_dims = (((0,), (0,)), ((), ()))

in_smem = pl.BlockSpec(memory_space=pltpu.SMEM)
in_vmem = pl.BlockSpec(memory_space=pltpu.VMEM)
in_any = pl.BlockSpec(memory_space=pl.ANY)


def product(left_op, right_op, dims=plain_dims):
    return lax.dot_general(left_op, right_op, dims, preferred_element_type=wide_type)


def lanes_of(shape):
    return lax.broadcasted_iota(jnp.int32, shape, 1)


def compiled(name, vmem=some_vmem):
    return dict(
        name=name,
        cost_estimate=pl.CostEstimate(flops=1, bytes_accessed=1, transcendentals=0),
        compiler_params=pltpu.CompilerParams(vmem_limit_bytes=vmem),
    )


class Sum:
    def __init__(self, keep, got):
        self.keep, self.got = keep, got

    def close(self):
        return (self.keep.astype(wide_type) + self.got.astype(wide_type)).astype(low_type)


class Order:
    def __init__(self, place):
        self.place, self.last = place, []

    def next(self, *others):
        names = self.last + [(other, "got") for other in others]
        values = [getattr(owner, name) for owner, name in names]
        place, *values = lax.optimization_barrier((self.place, *values))
        for (owner, name), value in zip(names, values):
            setattr(owner, name, value)
        return place

    def did(self, owner, name="keep"):
        self.last = [(owner, name)]


def low_array(*shape):
    return jax.ShapeDtypeStruct(shape, low_type)


def wide_array(*shape):
    return jax.ShapeDtypeStruct(shape, wide_type)


def head_front(tile, head):
    begin = head // 2 * 128
    if begin + 128 <= tile.shape[1]:
        part = tile[:, begin : begin + 128]
        if head % 2:
            part = pltpu.roll(part, 64, 1)
    else:
        part = jnp.concatenate([tile[:, begin:], jnp.zeros_like(tile[:, begin:])], axis=1)
    return jnp.where(lanes_of(part.shape) < 64, part, 0.0)


def head_rear(tile, head):
    begin = head // 2 * 128
    if begin + 128 <= tile.shape[1]:
        part = tile[:, begin : begin + 128]
        if head % 2 == 0:
            part = pltpu.roll(part, 64, 1)
    else:
        part = jnp.concatenate([jnp.zeros_like(tile[:, begin:]), tile[:, begin:]], axis=1)
    return jnp.where(lanes_of(part.shape) >= 64, part, 0.0)


(at_row, at_core, at_x, at_z, at_group, at_ring, at_first, at_length, at_near, at_mine, at_other) = range(11)


def pack_kernel(place_ref, q_ref, k_ref, v_ref, all_ref, own_ref, half_ref):
    rows = q_ref.shape[0]
    for group in range(head_splits):
        part = pl.ds(group * rows, rows)
        for head in range(group_heads):
            begin = (group * group_heads + head) * head_size
            all_ref[part, head * 128 : head * 128 + 64] = k_ref[:, begin : begin + head_size]
            all_ref[part, head * 128 + 64 : head * 128 + 128] = v_ref[:, begin : begin + head_size]
        all_ref[part, 2 * group_cols : pack_cols] = q_ref[:, group * group_cols : (group + 1) * group_cols]
        all_ref[part, pack_cols:] = jnp.zeros((rows, padded_cols - pack_cols), low_type)
    start = place_ref[at_group] * rows
    own_ref[...] = all_ref[pl.ds(pl.multiple_of(start, rows), rows), :pack_cols]
    start = start + place_ref[at_mine] * (rows // 2)
    half_ref[...] = all_ref[pl.ds(pl.multiple_of(start, rows // 2), rows // 2), :pack_cols]


def pack_weights(place, query_weight, key_weight, value_weight):
    rows = query_weight.shape[0]
    return pl.pallas_call(
        pack_kernel,
        in_specs=[in_smem] + [in_vmem] * 3,
        out_specs=[in_vmem] * 3,
        out_shape=[
            low_array(head_splits * rows, padded_cols),
            low_array(rows, pack_cols),
            low_array(rows // 2, pack_cols),
        ],
        **compiled("pack_weights", most_vmem),
    )(place, query_weight, key_weight, value_weight)


def whole_vector(place_ref, own_ref, other_ref, begin, size):
    own = own_ref[:, begin : begin + size].astype(wide_type)
    other = other_ref[:, begin : begin + size].astype(wide_type)
    first = place_ref[at_near] == 0
    return jnp.concatenate([jnp.where(first, own, other), jnp.where(first, other, own)], axis=1)


def ship_kernel(place_ref, out_ref, inner_ref, outer_ref, ship_ref, sems):
    width = out_ref.shape[1]
    copies = []
    start = 0

    def send(ref, cols):
        nonlocal start
        half = ref.shape[0] // 2
        source = ref.at[pl.ds(pl.multiple_of(place_ref[at_mine] * half, half), half), cols]
        copies.append(
            pltpu.make_async_copy(source, ship_ref.at[pl.ds(start, half), :], sems.at[len(copies)])
        )
        copies[-1].start()
        start += half

    send(outer_ref, pl.ds(0, width))
    for k in range(0, inner_ref.shape[1], width):
        send(inner_ref, pl.ds(k, width))
    send(out_ref, pl.ds(0, width))
    for copy in copies:
        copy.wait()


def shipment(place, weights):
    width = weights[0].shape[1]
    chunks = weights[1].shape[1] // width
    rows = (weights[0].shape[0] + weights[1].shape[0] * chunks + weights[2].shape[0]) // 2
    return pl.pallas_call(
        ship_kernel,
        in_specs=[in_smem] + [in_any] * 3,
        out_specs=in_vmem,
        out_shape=low_array(rows, width),
        scratch_shapes=[pltpu.SemaphoreType.DMA((chunks + 2,))],
        **compiled("shipment", most_vmem),
    )(place, *weights)


def project_kernel(place_ref, x0, x1, x2, x3, own_ref, mine_ref, rest_ref, near_ref, far_ref, q_ref, kv_ref, other_ref):
    half = own_ref.shape[0]
    rows = x0.shape[0]
    near = pl.multiple_of(place_ref[at_near] * half, 128)
    far = pl.multiple_of((1 - place_ref[at_near]) * half, 128)
    kv_cols = 2 * group_cols
    for fetched, core in ((mine_ref, place_ref[at_mine]), (rest_ref, 1 - place_ref[at_mine])):
        other_ref[pl.ds(pl.multiple_of(core * (half // 2), half // 2), half // 2), :] = fetched[...]
    biases = [whole_vector(place_ref, near_ref, far_ref, k * half, half) for k in range(2)]
    q_bias, v_bias = [jnp.zeros((1, group_cols), wide_type)] * 2
    for group in range(head_splits):
        cols = slice(group * group_cols, (group + 1) * group_cols)
        q_bias = jnp.where(place_ref[at_group] == group, biases[0][:, cols], q_bias)
        v_bias = jnp.where(place_ref[at_group] == group, biases[1][:, cols], v_bias)
    kv_bias = []
    for head in range(group_heads):
        kv_bias += [jnp.zeros((1, head_size), wide_type), v_bias[:, head * 64 : head * 64 + 64]]
    bias = jnp.concatenate(kv_bias + [q_bias], axis=1)
    for k, x_ref in enumerate((x0, x1, x2, x3)):
        part = pl.ds(k * rows, rows)
        made = product(x_ref[:, pl.ds(near, half)], own_ref[...])
        made = made + product(x_ref[:, pl.ds(far, half)], other_ref[...]) + bias
        kv_ref[part, :] = made[:, :kv_cols].astype(low_type)
        q_ref[part, :] = (made[:, kv_cols:] * score_scale).astype(low_type)


def project(place, blocks, own, mine, rest, vectors):
    rows, width = blocks[0].shape
    line = rows * head_splits
    return pl.pallas_call(
        project_kernel,
        in_specs=[in_smem] + [in_vmem] * 9,
        out_specs=[in_vmem] * 2,
        out_shape=[low_array(line, group_cols), low_array(line, 2 * group_cols)],
        scratch_shapes=[pltpu.VMEM(own.shape, low_type)],
        **compiled("project", most_vmem),
    )(place, *blocks, own, mine, rest, *vectors)


def attend_kernel(starts, resumed, finished, place_ref, q_ref, *refs):
    pieces = len(starts)
    kv_refs, aug_ref = refs[:pieces], refs[pieces]
    refs = refs[pieces + 1 :]
    state_ref, out_refs = (refs[0], refs[1:]) if resumed else (None, refs)
    rows = q_ref.shape[0]
    joints = [[]]
    for k, kv_ref in enumerate(kv_refs):
        if sum(kv_refs[n].shape[0] for n in joints[-1]) + kv_ref.shape[0] > 2048:
            joints.append([])
        joints[-1].append(k)
    lane = lanes_of((rows, 128))
    q_aug = jnp.where(lane == 0, 1.0, 0.0).astype(low_type)
    stats = jnp.zeros((rows, 128), wide_type)
    q_wide = q_ref[...].astype(wide_type)
    outs = []
    for head in range(group_heads):
        cols = pl.ds(head * 128, 128)
        q_ext = jnp.concatenate([head_front(q_wide, head).astype(low_type), q_aug], axis=1)
        top = None
        if resumed:
            accum = state_ref[:, cols]
            total, top = accum[:, 0:1], accum[:, 1:2]
        for joint in joints:
            kv_ext = jnp.concatenate(
                [
                    jnp.concatenate(
                        [kv_refs[k][:, cols], aug_ref[pl.ds(starts[k], kv_refs[k].shape[0]), :]],
                        axis=1,
                    )
                    for k in joint
                ],
                axis=0,
            )
            scores = product(q_ext, kv_ext, back_dims)
            new_top = jnp.floor(jnp.max(scores, axis=1, keepdims=True))
            if top is not None:
                new_top = jnp.maximum(top, new_top)
            weights = jnp.exp2(scores - new_top).astype(low_type)
            part_sum = product(weights, kv_ext)
            part_total = part_sum[:, 129:130]
            if top is None:
                accum, total = part_sum[:, :128], part_total
            else:
                factor = jnp.exp2(top - new_top)
                accum, total = accum * factor + part_sum[:, :128], total * factor + part_total
            top = new_top
        if finished:
            outs.append(accum / total)
            stats = jnp.where(lane == head, top, stats)
            stats = jnp.where(lane == group_heads + head, total, stats)
        else:
            out_refs[0][:, cols] = jnp.where(lane == 0, total, jnp.where(lane == 1, top, accum))
    if not finished:
        return
    low_refs, wide_ref, stat_ref = out_refs[:head_splits], out_refs[-2], out_refs[-1]
    tiles = []
    for head in range(0, group_heads, 2):
        first = pltpu.roll(outs[head], 64, 1)
        if head + 1 < group_heads:
            tiles.append(jnp.where(lane < 64, first, outs[head + 1]))
        else:
            tiles.append(first[:, :64])
    context = jnp.concatenate(tiles, axis=1)
    wide_ref[...] = context
    stat_ref[...] = stats
    for k, low_ref in enumerate(low_refs):

        @pl.when(pl.program_id(0) == k)
        def _():
            low_ref[...] = context.astype(low_type)


def attend(place, q_line, kv_pieces, order, aug, state, finished):
    line = q_line.shape[0]
    tile = line // head_splits
    whole = lambda i: (0, 0)
    by_tile = lambda i: (i, 0)
    sizes = [piece.shape[0] for piece in kv_pieces]
    used = [kv_pieces[k] for k in order]
    starts = [sum(sizes[:k]) for k in order]
    states = [] if state is None else [state]
    state_cols = 128 * group_heads
    work = line * group_heads * used[0].shape[0] * len(used)
    if finished:
        out_specs = [pl.BlockSpec((tile, group_cols), whole)] * head_splits
        out_specs += [pl.BlockSpec((tile, group_cols), by_tile), pl.BlockSpec((tile, 128), by_tile)]
        out_shape = [low_array(tile, group_cols)] * head_splits
        out_shape += [wide_array(line, group_cols), wide_array(line, 128)]
    else:
        out_specs = pl.BlockSpec((tile, state_cols), by_tile)
        out_shape = wide_array(line, state_cols)
    return pl.pallas_call(
        partial(attend_kernel, starts, state is not None, finished),
        grid=(head_splits,),
        in_specs=[in_smem, pl.BlockSpec((tile, group_cols), by_tile)]
        + [pl.BlockSpec(piece.shape, whole) for piece in used]
        + [pl.BlockSpec(aug.shape, whole)]
        + [pl.BlockSpec((tile, state_cols), by_tile) for _ in states],
        out_specs=out_specs,
        out_shape=out_shape,
        **compiled("attend"),
    )(place, q_line, *used, aug, *states)


def split_three(number):
    first = number.astype(low_type).astype(wide_type)
    second = (number - first).astype(low_type).astype(wide_type)
    return first, second, number - first - second


def attend_back_kernel(head, pieces, first, outs, query_part, place_ref, q_ref, stat_ref, context_ref, g0, g1, g2, g3, *refs):
    kv_refs, aug_ref = refs[:pieces], refs[pieces]
    sum_refs = refs[pieces + 1 : pieces + 1 + outs]
    q_grad_ref, kv_all, q_ext, g_ext = refs[pieces + 1 + outs :]
    rows = q_ref.shape[0]
    query_rows = q_ref.shape[0]
    seg_rows = g0.shape[0]
    step = pl.program_id(0)

    @pl.when(step == 0)
    def _():
        q_grad_ref[...] = jnp.zeros_like(q_grad_ref)
        start = 0
        for kv_ref in kv_refs:
            kv_all[pl.ds(start, kv_ref.shape[0]), :] = kv_ref[...]
            start += kv_ref.shape[0]
        for k, grad_ref in enumerate((g0, g1, g2, g3)):
            part = pl.ds(k * seg_rows, seg_rows)
            lane = lanes_of((seg_rows, 128))
            stats = stat_ref[part, :]
            top = stats[:, head : head + 1]
            total = stats[:, group_heads + head : group_heads + head + 1]
            grad = head_rear(grad_ref[...].astype(wide_type), head)
            context = head_rear(context_ref[part, :], head)
            delta = jnp.sum(grad * context, axis=1, keepdims=True) / total
            q_more = jnp.where(lane == 0, 1.0, 0.0)
            g_more = jnp.zeros((seg_rows, 128), wide_type)
            for place, (of_top, of_delta) in enumerate(zip(split_three(top), split_three(delta))):
                q_more = jnp.where(lane == place + 1, -of_top, q_more)
                g_more = jnp.where(lane == place + 1, -of_delta, g_more)
            q_ext[part, :128] = head_front(q_ref[part, :].astype(wide_type), head).astype(low_type)
            q_ext[part, 128:] = q_more.astype(low_type)
            g_ext[part, :128] = (grad / total).astype(low_type)
            g_ext[part, 128:] = g_more.astype(low_type)

    kv_part = kv_all[pl.ds(pl.multiple_of(step * rows, rows), rows), :]
    aug_part = aug_ref[pl.ds(pl.multiple_of(first + step * rows, rows), rows), :]
    kv_ext = jnp.concatenate([kv_part, aug_part], axis=1)
    keys_turned = jnp.transpose(kv_part)[:64]
    accum = jnp.zeros((rows, 128), wide_type)
    for start in range(0, query_rows, query_part):
        part = pl.ds(start, query_part)
        q_part = q_ext[part, :]
        g_part = g_ext[part, :]
        weights = jnp.exp2(product(kv_ext, q_part, back_dims))
        along_values = product(kv_ext, g_part, back_dims)
        grad_scores = (weights * along_values).astype(low_type)
        accum = accum + product(weights.astype(low_type), g_part[:, :128])
        accum = accum + product(grad_scores, q_part[:, :128])
        q_grad_ref[:, part] += product(keys_turned, grad_scores)
    lane = lanes_of((rows, 128))
    made = (accum * jnp.where(lane < 64, log_two, 1.0)).astype(low_type)

    each = kv_all.shape[0] // rows // outs
    for k, sum_ref in enumerate(sum_refs):

        @pl.when(step // each == k)
        def _():
            sum_ref[...] = made


def attend_back(place, head, q_line, stats, context, grads, kv_pieces, order, outs, aug):
    line = q_line.shape[0]
    sizes = [piece.shape[0] for piece in kv_pieces]
    used = [kv_pieces[k] for k in order]
    length = sum(piece.shape[0] for piece in used)
    each = length // line // outs
    whole = lambda i: (0, 0)
    part_of = lambda k: lambda i: (jnp.clip(i - k * each, 0, each - 1), 0)
    *sums, q_grad = pl.pallas_call(
        partial(
            attend_back_kernel, head, len(used), sum(sizes[: order[0]]), outs, math.gcd(line, 512)
        ),
        grid=(length // line,),
        in_specs=[
            in_smem,
            pl.BlockSpec(q_line.shape, whole),
            pl.BlockSpec(stats.shape, whole),
            pl.BlockSpec(context.shape, whole),
        ]
        + [pl.BlockSpec(grad.shape, whole) for grad in grads]
        + [pl.BlockSpec((piece.shape[0], 128), lambda i: (0, head)) for piece in used]
        + [pl.BlockSpec(aug.shape, whole)],
        out_specs=[pl.BlockSpec((line, 128), part_of(k)) for k in range(outs)]
        + [pl.BlockSpec((head_size, line), whole)],
        out_shape=[low_array(line * each, 128)] * outs + [wide_array(head_size, line)],
        scratch_shapes=[
            pltpu.VMEM((length, 128), low_type),
            pltpu.VMEM((line, 256), low_type),
            pltpu.VMEM((line, 256), low_type),
        ],
        **compiled("attend_back"),
    )(place, q_line, stats, context, *grads, *used, aug)
    return sums, q_grad


def add_pairs_kernel(place_ref, *refs):
    out_ref = refs[-1]
    for k in range(out_ref.shape[0]):
        total = refs[2 * k][...].astype(wide_type) + refs[2 * k + 1][...].astype(wide_type)
        out_ref[k] = total.astype(low_type)


def add_pairs(place, *arrays):
    return pl.pallas_call(
        add_pairs_kernel,
        in_specs=[in_smem] + [in_vmem] * len(arrays),
        out_specs=in_vmem,
        out_shape=low_array(len(arrays) // 2, *arrays[0].shape),
        **compiled("add_pairs"),
    )(place, *arrays)


def add_merge_kernel(place_ref, keep_a, got_a, keep_b, got_b, out_ref):
    start = 0
    for kept, got in ((keep_a, got_a), (keep_b, got_b)):
        rows = kept.shape[1]
        total = kept[...].astype(wide_type) + got[...].astype(wide_type)
        out_ref[:, start : start + rows, :] = total.astype(low_type)
        start += rows


def add_merge(place, keep_a, got_a, keep_b, got_b):
    return pl.pallas_call(
        add_merge_kernel,
        in_specs=[in_smem] + [in_vmem] * 4,
        out_specs=in_vmem,
        out_shape=low_array(2, keep_a.shape[1] + keep_b.shape[1], keep_a.shape[2]),
        **compiled("add_merge"),
    )(place, keep_a, got_a, keep_b, got_b)


def norm_forward(hidden):
    centre = hidden - jnp.mean(hidden, axis=1, keepdims=True)
    inverse = lax.rsqrt(jnp.mean(centre * centre, axis=1, keepdims=True) + norm_eps)
    return centre * inverse, inverse


def norm_back(grad, normal, inverse):
    along = jnp.mean(grad * normal, axis=1, keepdims=True)
    return inverse * (grad - jnp.mean(grad, axis=1, keepdims=True) - normal * along)


def over_tokens(array):
    return jnp.sum(array, axis=0, keepdims=True)


def mid_kernel(place_ref, factor_ref, x_ref, teacher_ref, c0, c1, c2, c3, near_ref, far_ref, *refs):
    own_weights, shipments = refs[0:3], refs[3:5]
    (
        output_ref, sum_ref, d0, d1, d2, d3, act_ref, hidden_ref, normed_ref, branch_ref, attn_ref, small_ref,
        w_out, w_inner, w_outer, slope_ref, sems,
    ) = refs[5:]
    held = (w_out, w_inner, w_outer)
    near, mine = place_ref[at_near], place_ref[at_mine]
    copies = []
    width = x_ref.shape[1]

    def fetch(source, k, start, rows, cols=None):
        target = held[k].at[pl.ds(pl.multiple_of(start, rows), rows), :]
        if cols is not None:
            target = held[k].at[pl.ds(pl.multiple_of(start, rows), rows), cols]
        copies.append(pltpu.make_async_copy(source, target, sems.at[len(copies)]))
        copies[-1].start()

    halves = [weight.shape[0] // 2 for weight in own_weights]
    starts = [
        [(1 - near) * 2 * half + core * half for half in halves] for core in (mine, 1 - mine)
    ]
    out_half, inner_half, outer_half = halves
    chunks = own_weights[1].shape[1] // width
    base = outer_half + chunks * inner_half
    fetch(own_weights[0], 0, near * 2 * out_half, 2 * out_half)
    for ship, (out_start, _, _) in zip(shipments, starts):
        fetch(ship.at[pl.ds(base, out_half), :], 0, out_start, out_half)
    fetch(own_weights[1], 1, near * 2 * inner_half, 2 * inner_half)
    fetch(own_weights[2], 2, near * 2 * outer_half, 2 * outer_half)
    for ship, (_, inner_start, outer_start) in zip(shipments, starts):
        for k in range(chunks):
            source = ship.at[pl.ds(outer_half + k * inner_half, inner_half), :]
            fetch(source, 1, inner_start, inner_half, pl.ds(k * width, width))
        fetch(ship.at[pl.ds(0, outer_half), :], 2, outer_start, outer_half)
    rows = x_ref.shape[0]
    half = width // 2
    vector = lambda k, size: whole_vector(place_ref, near_ref, far_ref, k * half, size)
    b_out, g_attn, s_attn, b_outer, g_final, s_final = (vector(k, half) for k in range(2, 8))
    b_inner = vector(8, w_outer.shape[0] // 2)
    group = place_ref[at_group]
    of_group = lambda k: pl.ds(pl.multiple_of((group ^ k) * group_cols, group_cols), group_cols)

    for copy in copies[0:3]:
        copy.wait()
    hidden = x_ref[...].astype(wide_type) + b_out
    for k, c_ref in enumerate((c0, c1, c2, c3)):
        hidden = hidden + product(c_ref[...], w_out[of_group(k), :])
    attn_normal, attn_inverse = norm_forward(hidden)
    normed = attn_normal * g_attn + s_attn
    normed_low = normed.astype(low_type)
    normed_ref[...] = normed_low
    for copy in copies[3:]:
        copy.wait()
    branch = normed + b_outer
    for k in range(chunks):
        cols = pl.ds(k * width, width)
        pre = product(normed_low, w_inner[:, cols]) + b_inner[:, k * width : (k + 1) * width]
        bell = 0.5 * (1.0 + lax.erf(pre * math.sqrt(0.5)))
        slope_ref[:, cols] = bell + pre * jnp.exp(-0.5 * pre * pre) * (1.0 / math.sqrt(2.0 * math.pi))
        act = (pre * bell).astype(low_type)
        act_ref[:, cols] = act
        branch = branch + product(act, w_outer[cols, :])
    final_normal, final_inverse = norm_forward(branch)
    output = final_normal * g_final + s_final
    output_ref[:, 0, :] = output
    token = place_ref[at_first] + lax.broadcasted_iota(jnp.int32, (rows, 1), 0)
    valid = (token < place_ref[at_length]).astype(wide_type)
    mismatch = (output - teacher_ref[...].astype(wide_type)) * valid
    squares = over_tokens(mismatch * mismatch)
    grad_out = mismatch * factor_ref[0]
    final_gain_grad = over_tokens(grad_out * final_normal)
    final_shift_grad = over_tokens(grad_out)
    grad_mid = norm_back(grad_out * g_final, final_normal, final_inverse)
    grad_branch = grad_mid.astype(low_type)
    branch_ref[...] = grad_branch
    outer_bias_grad = over_tokens(grad_branch.astype(wide_type))
    grad_normed = grad_mid
    inner_bias_grad = []
    for k in range(chunks):
        cols = pl.ds(k * width, width)
        grad_act = product(grad_branch, w_outer[cols, :], back_dims)
        grad_hidden = (grad_act * slope_ref[:, cols]).astype(low_type)
        hidden_ref[:, cols] = grad_hidden
        inner_bias_grad.append(over_tokens(grad_hidden.astype(wide_type)))
        grad_normed = grad_normed + product(grad_hidden, w_inner[:, cols], back_dims)
    attn_gain_grad = over_tokens(grad_normed * attn_normal)
    attn_shift_grad = over_tokens(grad_normed)
    grad_sum = norm_back(grad_normed * g_attn, attn_normal, attn_inverse)
    sum_ref[...] = grad_sum
    grad_attn = grad_sum.astype(low_type)
    attn_ref[...] = grad_attn
    out_bias_grad = over_tokens(grad_attn.astype(wide_type))
    for k, d_ref in enumerate((d0, d1, d2, d3)):
        d_ref[...] = product(grad_attn, w_out[of_group(k), :], back_dims).astype(low_type)
    pairs = (
        (final_gain_grad, final_shift_grad),
        (outer_bias_grad, attn_gain_grad),
        (attn_shift_grad, out_bias_grad),
    )
    for side in range(2):
        cols = slice(side * half, side * half + half)
        lines = [jnp.concatenate([a[:, cols], b[:, cols]], axis=1) for a, b in pairs]
        lines += inner_bias_grad[side * 2 : side * 2 + 2] + [squares]
        lines.append(jnp.zeros((8 - len(lines), width), wide_type))
        small_ref[side] = jnp.concatenate(lines, axis=0)


def middle(place, factor, tokens, teacher, contexts, vectors, weights):
    rows, width = tokens.shape
    ff_width = weights[1].shape[1]
    return pl.pallas_call(
        mid_kernel,
        in_specs=[in_smem, in_smem] + [in_vmem] * 8 + [in_any] * 5,
        out_specs=[in_vmem] * 12,
        out_shape=[wide_array(rows, 1, width), wide_array(rows, width)]
        + [low_array(rows, group_cols)] * 4
        + [low_array(rows, ff_width)] * 2
        + [low_array(rows, width)] * 3
        + [wide_array(2, 8, width)],
        scratch_shapes=[
            pltpu.VMEM((width, width), low_type),
            pltpu.VMEM((width, ff_width), low_type),
            pltpu.VMEM((ff_width, width), low_type),
            pltpu.VMEM((rows, ff_width), wide_type),
            pltpu.SemaphoreType.DMA((5 + 2 * (1 + ff_width // width),)),
        ],
        **compiled("middle", most_vmem),
    )(place, factor, tokens, teacher, *contexts, *vectors, *weights)


def weight_kernel(
    place_ref, act_ref, branch_ref, normed_ref, hidden_ref, c0, c1, c2, c3, attn_ref, small_ref,
    give_a, keep_a, give_b, keep_b, out_grad,
):
    width = branch_ref.shape[1]
    half = width // 2
    group = place_ref[at_group]

    @pl.when((pl.program_id(0) == 0) & (pl.program_id(1) == 0))
    def _():
        for k, c_ref in enumerate((c0, c1, c2, c3)):
            part = pl.ds(pl.multiple_of((group ^ k) * group_cols, group_cols), group_cols)
            out_grad[part, :] = product(c_ref[...], attn_ref[...], weight_dims)

    row = place_ref[at_row] ^ pl.program_id(0)
    x = place_ref[at_x] ^ pl.program_id(1)
    for far, a_ref, b_ref in ((1, give_a, give_b), (0, keep_a, keep_b)):
        core = place_ref[at_core] ^ far
        begin = pl.multiple_of(((row * 2 + core) * 2 + x) * half, 128)
        outer = product(
            act_ref[:, pl.ds(begin, half)], branch_ref[...], weight_dims
        ).astype(low_type)
        inner = product(
            normed_ref[:, pl.ds(pl.multiple_of(row * half, 128), half)],
            hidden_ref[:, pl.ds(pl.multiple_of((core * 2 + x) * width, 128), width)],
            weight_dims,
        ).astype(low_type)
        base = row * half + core * (half // 2) + x * (half // 4)
        for z in range(4):
            apart = place_ref[at_z] ^ z
            low, high = pl.ds(apart & 1, 1), pl.ds(apart >> 1, 1)
            rows = slice(z * 96, z * 96 + 96)
            shaped = lambda block: block[None, None, None, None]
            a_ref[0:1, low, 0:1, high, :, :] = shaped(outer[rows])
            rest = out_grad[pl.ds(pl.multiple_of(base + z * 24, 8), 24), :]
            rest = jnp.concatenate([rest, small_ref[pl.ds(row, 1)][0]], axis=0).astype(low_type)
            b_ref[0:1, 0:1, low, high, :, :] = shaped(jnp.concatenate([inner[rows], rest], axis=0))


def weight_grads(place, act, branch, normed, hidden, contexts, attn, small):
    rows, width = branch.shape
    a_shape, b_shape = (2, 2, 2, 2, 96, width), (2, 2, 2, 2, 128, width)
    a_spec = pl.BlockSpec((1, 2, 1, 2, 96, width), lambda i, j: (i, 0, j, 0, 0, 0))
    b_spec = pl.BlockSpec((1, 1, 2, 2, 128, width), lambda i, j: (j, i, 0, 0, 0, 0))
    return pl.pallas_call(
        weight_kernel,
        grid=(2, 2),
        in_specs=[in_smem] + [in_vmem] * 10,
        out_specs=[a_spec, a_spec, b_spec, b_spec],
        out_shape=[low_array(*a_shape)] * 2 + [low_array(*b_shape)] * 2,
        scratch_shapes=[pltpu.VMEM((width, width), wide_type)],
        **compiled("weight_grads", most_vmem),
    )(place, act, branch, normed, hidden, *contexts, attn, small)


def add_split_kernel(gots, place_ref, kept_ref, *refs):
    got_refs, keep_ref, give_refs = refs[:gots], refs[gots], refs[gots + 1 :]
    got = [got_refs[0][0], got_refs[0][1]] if gots == 1 else [got_ref[...] for got_ref in got_refs]
    total = [
        (kept_ref[k].astype(wide_type) + got[k].astype(wide_type)).astype(low_type) for k in range(2)
    ]
    keep_ref[...] = total[0]
    rows = give_refs[0].shape[0]
    for k, give_ref in enumerate(give_refs):
        give_ref[...] = total[1][k * rows : (k + 1) * rows]


def add_split(place, kept, got, parts=1):
    cols = kept.shape[-1]
    shape = (2, kept.size // cols // 2, cols)
    if isinstance(got, list):
        gots = [array.reshape(shape[1:]) for array in got]
    else:
        gots = [got.reshape(shape)]
    keep, *gives = pl.pallas_call(
        partial(add_split_kernel, len(gots)),
        in_specs=[in_smem] + [in_vmem] * (1 + len(gots)),
        out_specs=[in_vmem] * (1 + parts),
        out_shape=[low_array(*shape[1:])] + [low_array(shape[1] // parts, cols)] * parts,
        **compiled("add_split"),
    )(place, kept.reshape(shape), *gots)
    gives = [give.reshape(kept.shape[1:]) if parts == 1 else give for give in gives]
    return keep.reshape(kept.shape[1:]), gives


def unpack_kernel(place_ref, own_ref, got_ref, *refs):
    width = own_ref.shape[-1]
    half = width // 2
    out_refs, wide, sems = refs[:-2], refs[-2], refs[-1]
    copies = []

    def send(source, target):
        copy = pltpu.make_async_copy(source, target, sems.at[len(copies)])
        copy.start()
        copies.append(copy)

    for k in range(16):
        ref = got_ref if k // 8 else own_ref
        core = place_ref[at_core] ^ (k // 8)
        x = place_ref[at_x] ^ (k // 4 % 2)
        z = place_ref[at_z] ^ (k // 2 % 2 + 2 * (k % 2))
        if len(out_refs) == 1:
            wide[k] = ref[k // 4 % 2, k // 2 % 2, k % 2].astype(wide_type)
            start = pl.multiple_of((core * 2 + x) * half + z * 96, 32)
            send(wide.at[k], out_refs[0].at[pl.ds(start, 96), :])
        else:
            inner_ref, out_ref = out_refs
            wide[k] = ref[k // 2 % 2, k // 4 % 2, k % 2].astype(wide_type)
            cols = pl.ds(pl.multiple_of((core * 2 + x) * width, 128), width)
            send(wide.at[k, 0:96], inner_ref.at[pl.ds(pl.multiple_of(z * 96, 32), 96), cols])
            start = pl.multiple_of(core * (half // 2) + x * (half // 4) + z * 24, 8)
            send(wide.at[k, 96:120], out_ref.at[pl.ds(start, 24), :])
    for copy in copies:
        copy.wait()


def unpack(place, own, got):
    rows, width = own.shape[3:]
    if rows == 96:
        shapes = [wide_array(2 * width, width)]
    else:
        shapes = [wide_array(width // 2, 4 * width), wide_array(width // 2, width)]
    return pl.pallas_call(
        unpack_kernel,
        in_specs=[in_smem] + [in_vmem] * 2,
        out_specs=[in_any] * len(shapes),
        out_shape=shapes,
        scratch_shapes=[
            pltpu.VMEM((16, rows, width), wide_type), pltpu.SemaphoreType.DMA((16 * len(shapes),))
        ],
        **compiled("unpack"),
    )(place, own, got)


def rows_kernel(counts, terms, place_ref, *refs):
    heads, used = len(counts), sum(counts)
    q_grads, kv_terms = refs[:used], refs[used : used + sum(terms)]
    refs = refs[used + sum(terms) :]
    blocks = refs[:4]
    r0, r1, r2, r3, give0, give1, keep0, keep1, w_grad, all_rows = refs[4:]
    rows, width = blocks[0].shape
    kv_cols = 2 * group_cols
    for k in range(heads):
        total = 0.0
        for n in range(sum(terms[:k]), sum(terms[: k + 1])):
            term = kv_terms[n]
            total = total + (term[...] if len(term.shape) == 2 else term[k]).astype(wide_type)
        all_rows[:, k * 128 : k * 128 + 128] = total.astype(low_type)
    firsts = [sum(counts[:k]) for k in range(heads)]
    turned = [
        sum((ref[...] for ref in q_grads[first + 1 : first + count]), q_grads[first][...])
        for first, count in zip(firsts, counts)
    ]
    turned = jnp.concatenate(turned, axis=0) * 0.125
    all_rows[:, kv_cols:] = jnp.transpose(turned).astype(low_type)
    half = width // 2
    bias = jnp.zeros((1, pack_cols), wide_type)
    for k, r_ref in enumerate((r0, r1, r2, r3)):
        made = all_rows[pl.ds(k * rows, rows), :]
        r_ref[...] = made
        bias = bias + over_tokens(made.astype(wide_type))
        for side in range(2):
            part = product(blocks[k][:, side * half : side * half + half], made, weight_dims)
            if k:
                w_grad[side] += part
            else:
                w_grad[side] = part
    bias = jnp.concatenate([bias, jnp.zeros((15, pack_cols), wide_type)], axis=0)
    for far, piece_refs in ((1, (give0, give1)), (0, (keep0, keep1))):
        start = pl.multiple_of((place_ref[at_core] ^ far) * (half // 2), half // 2)
        for j in range(2):
            row = place_ref[at_row] ^ j
            block = w_grad[pl.ds(row, 1), pl.ds(start, half // 2), :][0]
            piece_refs[j][...] = jnp.concatenate([block, bias], axis=0).astype(low_type)


def project_back(place, q_grads, kv_terms, blocks):
    counts = [len(q_grad) for q_grad in q_grads]
    terms = [len(head) for head in kv_terms]
    every = [array for head in q_grads + kv_terms for array in head]
    rows, width = blocks[0].shape
    pieces = (width // 4 + 16, pack_cols)
    return pl.pallas_call(
        partial(rows_kernel, counts, terms),
        in_specs=[in_smem] + [in_vmem] * (len(every) + 4),
        out_specs=[in_vmem] * 8,
        out_shape=[low_array(rows, pack_cols)] * 4 + [low_array(*pieces)] * 4,
        scratch_shapes=[
            pltpu.VMEM((2, width // 2, pack_cols), wide_type),
            pltpu.VMEM((4 * rows, pack_cols), low_type),
        ],
        **compiled("project_back", most_vmem),
    )(place, *every, *blocks)


def input_kernel(place_ref, sum_ref, r0, r1, r2, r3, own_ref, mine_ref, other_ref, grad_ref):
    half = own_ref.shape[0] // head_splits
    near = jnp.zeros((sum_ref.shape[0], half), wide_type)
    far = jnp.zeros((sum_ref.shape[0], half), wide_type)
    for k, r_ref in enumerate((r0, r1, r2, r3)):
        group = place_ref[at_group] ^ k
        near = near + product(r_ref[...], own_ref[pl.ds(pl.multiple_of(group * half, half), half), :pack_cols], back_dims)
        fetched = (group >> 1) == place_ref[at_mine]
        side = pl.ds(pl.multiple_of((group & 1) * half, half), half)
        weight = jnp.where(fetched, mine_ref[side, :pack_cols], other_ref[side, :pack_cols])
        far = far + product(r_ref[...], weight, back_dims)
    for part, begin in ((near, place_ref[at_near]), (far, 1 - place_ref[at_near])):
        cols = pl.ds(pl.multiple_of(begin * half, 128), half)
        grad_ref[:, 0, cols] = sum_ref[:, cols] + part


def input_back(place, grad_sum, rows, packs):
    return pl.pallas_call(
        input_kernel,
        in_specs=[in_smem] + [in_vmem] * 8,
        out_specs=in_vmem,
        out_shape=wide_array(grad_sum.shape[0], 1, grad_sum.shape[1]),
        **compiled("input_back"),
    )(place, grad_sum, *rows, *packs)


def qkv_unpack_kernel(place_ref, here_ref, there_ref, q_ref, k_ref, v_ref, bias_ref):
    side = q_ref.shape[0] // 2
    bias_ref[...] = jnp.zeros_like(bias_ref)
    for own in range(head_splits):

        @pl.when(place_ref[at_group] == own)
        def _():
            for n, piece in enumerate((here_ref, there_ref)):
                part = pl.ds(pl.multiple_of((place_ref[at_core] ^ n) * side, side), side)
                for k in range(head_splits):
                    first = (own ^ k) * group_cols
                    block = piece[k].astype(wide_type)
                    q_ref[part, first : first + group_cols] = block[:side, 2 * group_cols :]
                    for h in range(group_heads):
                        begin = first + h * head_size
                        keys = slice(h * 128, h * 128 + 64)
                        values = slice(h * 128 + 64, h * 128 + 128)
                        k_ref[part, begin : begin + head_size] = block[:side, keys]
                        v_ref[part, begin : begin + head_size] = block[:side, values]
                        if n == 0:
                            bias_ref[1:2, begin : begin + head_size] = block[side : side + 1, values]
                    if n == 0:
                        bias_ref[0:1, first : first + group_cols] = block[
                            side : side + 1, 2 * group_cols :
                        ]


def qkv_unpack(place, here, there, width):
    return pl.pallas_call(
        qkv_unpack_kernel,
        in_specs=[in_smem] + [in_vmem] * 2,
        out_specs=[in_vmem] * 4,
        out_shape=[wide_array(width // 2, width)] * 3 + [wide_array(8, width)],
        **compiled("qkv_unpack"),
    )(place, here, there)


class Layout:
    def __init__(self):
        self.ctx = lax.axis_size("ctx")
        self.fsdp = lax.axis_size("fsdp")
        self.me = lax.axis_index("ctx")
        self.row = lax.axis_index("fsdp")
        self.fast = self.ctx == 16 and self.fsdp == 2
        group_bits = (2, 4) if self.fast else (self.ctx // 4, self.ctx // 2)
        bits = [1 << k for k in reversed(range(self.ctx.bit_length() - 1))]
        self.ring_bits = [bit for bit in bits if bit not in group_bits]
        self.group = self.bit(group_bits[0]) + 2 * self.bit(group_bits[1])
        self.group_codes = [0, group_bits[0], group_bits[1], group_bits[0] | group_bits[1]]
        self.ring_codes = [0]
        for bit in self.ring_bits:
            self.ring_codes = self.ring_codes + [code | bit for code in self.ring_codes]

    def bit(self, bit):
        return (self.me // bit) % 2

    def swap(self, block, code):
        return lax.ppermute(block, "ctx", [(i, i ^ code) for i in range(self.ctx)])

    def groups(self, blocks):
        return [blocks[0]] + [self.swap(blocks[k], self.group_codes[k]) for k in range(1, 4)]

    def across(self, block):
        return lax.ppermute(block, "fsdp", [(0, 1), (1, 0)])


def shards(
    layer_input,
    teacher_states,
    seq_lengths,
    query_weight,
    query_bias,
    key_weight,
    value_weight,
    value_bias,
    out_weight,
    out_bias,
    attn_gain,
    attn_shift,
    inner_weight,
    inner_bias,
    outer_weight,
    outer_bias,
    final_gain,
    final_shift,
):
    at = Layout()
    seg_rows, groups, width = layer_input.shape
    shard_rows = query_weight.shape[0]
    ff_rows = outer_weight.shape[0]
    ff_width = inner_weight.shape[1]
    tokens = layer_input.reshape(seg_rows, width)
    teacher = teacher_states.reshape(seg_rows, width)
    two_rows = at.fsdp == 2
    place = jnp.stack(
        [
            at.row, at.bit(1), at.bit(2), at.bit(4) + 2 * at.bit(8), at.group, at.bit(8),
            at.me * seg_rows, seq_lengths[0],
            at.row if two_rows else 0, at.bit(1), 0,
        ]
    ).astype(jnp.int32)

    blocks = at.groups([tokens] * 4)
    all_pack, own_pack, half_pack = pack_weights(place, query_weight, key_weight, value_weight)
    if two_rows:
        mine_part = at.across(half_pack)
    else:
        full = lax.all_gather(own_pack, "fsdp", axis=0, tiled=True)
        own_pack, far = full[: width // 2], full[width // 2 :]
        mine_part = lax.dynamic_slice_in_dim(far, at.bit(1) * (width // 4), width // 4, 0)
    rest_part = at.swap(mine_part, 1)
    vectors = (
        query_bias, value_bias, out_bias, attn_gain, attn_shift,
        outer_bias, final_gain, final_shift, inner_bias,
    )
    if two_rows:
        *vectors, own_pack = lax.optimization_barrier((*vectors, own_pack))
        own_vectors = jnp.concatenate(vectors).reshape(1, -1)
        vectors = (own_vectors, at.across(own_vectors))
    else:
        whole = lambda vector: lax.all_gather(vector, "fsdp", axis=0, tiled=True).reshape(2, -1)
        both = jnp.concatenate([whole(vector) for vector in vectors], axis=1)
        vectors = (both[:1], both[1:])
    own_count = jnp.sum(seq_lengths).astype(wide_type)
    weights = [out_weight, inner_weight, outer_weight]
    if two_rows:
        valid_count = own_count + at.across(own_count.reshape(1))[0]
        ship, rest_part, vectors, blocks, valid_count = lax.optimization_barrier(
            (shipment(place, weights), rest_part, vectors, blocks, valid_count)
        )
        ship = at.across(ship)
    q_line, kv_line = project(place, blocks, own_pack, mine_part, rest_part, vectors)
    if not two_rows:
        valid_count = lax.psum(own_count, "fsdp")

    source = jnp.stack(
        [at.me ^ (ring | group) for ring in at.ring_codes for group in at.group_codes]
    )
    position = (source[:, None] * seg_rows + jnp.arange(seg_rows)[None, :]).reshape(-1, 1)
    lane = lax.broadcasted_iota(jnp.int32, (position.shape[0], 128), 1)
    mask = jnp.where(position < seq_lengths[0], 0.0, masked_score)
    aug = jnp.where(lane == 0, mask, jnp.where(lane < 4, 1.0, 0.0)).astype(low_type)

    if at.fast:
        near = at.swap(kv_line, 1)
        far = at.swap(kv_line, 8)
        state = attend(place, q_line, [kv_line, far, near, far], (0, 2), aug, None, False)
        far, state = lax.optimization_barrier((far, state))
        kv_pieces = [kv_line, far, near, at.swap(far, 1)]
        order = (1, 3)
    else:
        kv_pieces = [kv_line]
        for bit in at.ring_bits:
            kv_pieces = kv_pieces + [at.swap(piece, bit) for piece in kv_pieces]
        state, order = None, tuple(range(len(kv_pieces)))
    *context_low, context, stats = attend(place, q_line, kv_pieces, order, aug, state, True)
    if two_rows:
        ship, stats = lax.optimization_barrier((ship, stats))
        weights += [ship, at.swap(ship, 1)]
    else:
        full = [lax.all_gather(weight, "fsdp", axis=0, tiled=True) for weight in weights]
        far = [weight[weight.shape[0] // 2 :] for weight in full]
        weights = [weight[: weight.shape[0] // 2] for weight in full]
        ship = shipment(place, far)
        weights += [ship, at.swap(ship, 1)]
    contexts = at.groups(context_low)
    token_total = seg_rows * groups * at.ctx * at.fsdp
    factor = (2.0 * token_total / valid_count).reshape(1)
    output, grad_sum, g0, g1, g2, g3, act, hidden, normed, branch, attn, small = middle(
        place, factor, tokens, teacher, contexts, vectors, weights
    )
    if two_rows:
        half = all_pack.shape[0] // 2
        mine_pack = lax.dynamic_slice_in_dim(all_pack, at.bit(1) * half, half, 0)
    else:
        by_row = lax.all_gather(all_pack, "fsdp", axis=0, tiled=False)
        by_row = by_row.reshape(at.fsdp, head_splits, shard_rows, padded_cols)
        whole = by_row.transpose(1, 0, 2, 3).reshape(head_splits, width, padded_cols)
        near, far = whole[:, : width // 2], whole[:, width // 2 :]
        flat = lambda pack: pack.reshape(-1, padded_cols)
        mine = lax.dynamic_slice_in_dim(far, at.bit(1) * 2, 2, 0)
        packs = (flat(near), flat(mine), at.swap(flat(mine), 1))
    grads = at.groups([g0, g1, g2, g3])

    over = lambda bit: lambda block: at.swap(block, bit)
    order = Order(place)

    def add(total, shape, move, *others, parts=1):
        total.keep, gives = add_split(
            order.next(*others), total.keep.reshape(shape), total.got, parts
        )
        moved = [move(give) for give in gives]
        total.got = moved[0] if parts == 1 else moved
        order.did(total)

    heads, q_grads = [], []

    def back(*others, split=False):
        args = (len(heads), q_line, stats, context, grads, kv_pieces)
        if split:
            give, first = attend_back(order.next(*others), *args, (2, 3), 2, aug)
            far = Sum(give[1], at.swap(give[1], 1))
            own = Sum(give[0], at.swap(give[0], 1))
            order.did(far)
            keep, second = attend_back(order.next(), *args, (0, 1), 2, aug)
            own.keep, far.keep = keep
            q_grads.append([first, second])
        else:
            sums, first = attend_back(order.next(*others), *args, (0, 1, 2, 3), 4, aug)
            own, far = Sum(sums[0], at.swap(sums[2], 1)), Sum(sums[1], at.swap(sums[3], 1))
            q_grads.append([first])
        order.did(far)
        heads.append((own, far))

    def send_far(*used, needs=()):
        pairs = [array for head in used for array in (heads[head][1].keep, heads[head][1].got)]
        sums = add_pairs(order.next(*needs), *pairs)
        total = Sum(sums, at.swap(sums, 8))
        order.did(total)
        return total

    if at.fast:
        give_a, keep_a, give_b, keep_b = weight_grads(
            place, act, branch, normed, hidden, contexts, attn, small
        )
        give_a, give_b, *grads = lax.optimization_barrier((give_a, give_b, *grads))
        part_a, part_b = Sum(keep_a, at.swap(give_a, 1)), Sum(keep_b, at.swap(give_b, 1))
        shape_a, shape_b = (2, -1, 96, width), (2, -1, 128, width)
        def step(move_a, move_b, parts=1):
            add(part_a, shape_a, move_a, parts=parts)
            add(part_b, shape_b, move_b, parts=parts)

        back()
        step(at.across, over(2))
        back()
        firsts = send_far(0, 1)
        back(split=True)
        step(over(4), at.across, 2)
        lasts = send_far(2, needs=(firsts,))
        step(over(2), over(4))
        lay = lambda part, rows: (part.keep.reshape(2, rows, width), part.got.reshape(2, rows, width))
        both = add_merge(order.next(lasts), *lay(part_a, 96), *lay(part_b, 128))
        both, mine_pack = lax.optimization_barrier((both, mine_pack))
        both = Sum(both, at.swap(both, 8))
        mine_pack = at.across(mine_pack)
        packs = (all_pack, mine_pack, at.swap(mine_pack, 1))
        order.did(both)
        fars = [firsts.got, firsts.got, lasts.got[0]]
        kv_terms = [[own.keep, own.got, far] for (own, _), far in zip(heads, fars)]
        r0, r1, r2, r3, give0, give1, keep0, keep1 = project_back(
            order.next(), q_grads, kv_terms, blocks
        )
        qkv = Sum(keep1, at.swap(give1, 1))
        order.did(qkv)
        rows = at.groups([r0, r1, r2, r3])
        got0 = at.swap(give0, 1)
        (onward,) = add_pairs(order.next(), qkv.keep, qkv.got)
        onward = at.across(onward)
        rows, both.got = lax.optimization_barrier((rows, both.got))
        both.got = jnp.concatenate([both.got[1:], both.got[:1]])
        both = both.close()
        small = both[0, 216:].astype(wide_type)
        own_a, own_b = both[:, :96], both[:, 96:]
        own_a, own_b = Sum(own_a, at.swap(own_a, 4)), Sum(own_b, at.swap(own_b, 2))
        qkv = sum(part.astype(wide_type) for part in (keep0, got0, onward)).astype(low_type)
        qkv = Sum(qkv, at.swap(qkv, 8))

        def joined(own, bit):
            own.keep = jnp.stack([own.keep, own.got])
            own.got = at.swap(own.keep, bit)

        joined(own_a, 2)
        joined(own_b, 4)
        input_grad = input_back(place, grad_sum, rows, packs)
        own_b.got, input_grad = lax.optimization_barrier((own_b.got, input_grad))
        here = at.groups([qkv.close()] * head_splits)
        here = jnp.stack(here)
        there = at.swap(here, 1)
        mine = lambda bias, k: lax.dynamic_slice_in_dim(bias[k], at.row * shard_rows, shard_rows, 0)
        side = (small[:3, :shard_rows], small[:3, shard_rows:], small[3:5].reshape(-1), jnp.sum(small[5]))
        side, own_a.got = lax.optimization_barrier((side, own_a.got))
        left, right, inner_bias_grad, total_sq = side
        final_gain_grad, outer_bias_grad, attn_shift_grad = left
        final_shift_grad, attn_gain_grad, out_bias_grad = right
        joined(own_a, 1)
        joined(own_b, 1)
        (outer_weight_grad,) = unpack(place, own_a.keep, own_a.got)
        outer_weight_grad, own_b.got = lax.optimization_barrier((outer_weight_grad, own_b.got))
        inner_weight_grad, out_weight_grad = unpack(place, own_b.keep, own_b.got)
        query_weight_grad, key_weight_grad, value_weight_grad, bias = qkv_unpack(
            place, here, there, width
        )
        query_bias_grad, value_bias_grad = mine(bias, 0), mine(bias, 1)
    else:
        kv_terms = []
        every = tuple(range(len(kv_pieces)))
        for head in range(group_heads):
            (keep, give), q_grad = attend_back(
                place, head, q_line, stats, context, grads, kv_pieces, every, 2, aug
            )
            q_grads.append([q_grad])
            total = Sum(keep, at.swap(give, 1))
            for bit in at.ring_bits[-2::-1]:
                add(total, (2, -1, 128), over(bit))
            kv_terms.append([total.keep, total.got])
        r0, r1, r2, r3, *_ = project_back(place, q_grads, kv_terms, blocks)
        rows = at.groups([r0, r1, r2, r3])
        input_grad = input_back(place, grad_sum, rows, packs)
        all_rows = jnp.concatenate([r0, r1, r2, r3])
        line = jnp.concatenate(blocks)

        def summed(partial_sum):
            mine = lax.psum_scatter(partial_sum, "fsdp", scatter_dimension=0, tiled=True)
            return lax.psum(mine, "ctx")

        qkv = product(line, all_rows, weight_dims)
        qkv = jnp.concatenate([qkv, jnp.sum(all_rows, axis=0, dtype=wide_type)[None]])
        qkv = lax.dynamic_update_slice(
            jnp.zeros((width + 1, head_splits, pack_cols), wide_type), qkv[:, None], (0, at.group, 0)
        )
        kv = qkv[:, :, : 2 * group_cols].reshape(width + 1, H, 2, head_size)
        parts = [qkv[:, :, 2 * group_cols :], kv[:, :, 0], kv[:, :, 1]]
        parts = [part.reshape(width + 1, width) for part in parts]
        query_weight_grad, key_weight_grad, value_weight_grad = (
            summed(part[:width]) for part in parts
        )
        outer_weight_grad = summed(product(act, branch, weight_dims))
        inner_weight_grad = summed(product(normed, hidden, weight_dims))
        whole = jnp.zeros((width, width), wide_type)
        for k in range(head_splits):
            whole = lax.dynamic_update_slice_in_dim(
                whole, product(contexts[k], attn, weight_dims), (at.group ^ k) * group_cols, 0
            )
        out_weight_grad = summed(whole)
        sums = small[:, :3].reshape(2, 3, 2, width // 2).transpose(1, 2, 0, 3).reshape(6, width)
        sums = jnp.concatenate(
            [sums, parts[0][width:], parts[2][width:], small[:, 3:5].reshape(4, width), small[0, 5:6]]
        )
        sums = lax.psum(sums, ("ctx", "fsdp"))
        mine = lambda k: lax.dynamic_slice_in_dim(sums[k], at.row * shard_rows, shard_rows, 0)
        (
            final_gain_grad, final_shift_grad, outer_bias_grad, attn_gain_grad, attn_shift_grad,
            out_bias_grad, query_bias_grad, value_bias_grad,
        ) = map(mine, range(8))
        inner_bias_grad = lax.dynamic_slice_in_dim(
            sums[8:12].reshape(-1), at.row * ff_rows, ff_rows, 0
        )
        total_sq = jnp.sum(sums[12])
    distill_loss = total_sq / (width * valid_count)
    return (
        distill_loss,
        output.reshape(seg_rows, groups, width),
        input_grad.reshape(seg_rows, groups, width),
        query_weight_grad,
        query_bias_grad,
        key_weight_grad,
        value_weight_grad,
        value_bias_grad,
        out_weight_grad,
        out_bias_grad,
        attn_gain_grad,
        attn_shift_grad,
        inner_weight_grad,
        inner_bias_grad,
        outer_weight_grad,
        outer_bias_grad,
        final_gain_grad,
        final_shift_grad,
    )


def solution(mesh):
    states = P("ctx", "fsdp", None)
    matrix = P("fsdp", None)
    vector = P("fsdp")
    placed = (
        states, states, vector,
        matrix, vector, matrix, matrix, vector, matrix, vector, vector, vector,
        matrix, vector, matrix, vector, vector, vector,
    )
    return jax.shard_map(
        shards,
        mesh=mesh,
        in_specs=placed,
        out_specs=(P(), states, states) + placed[3:],
        check_vma=False,
    )
```

```python
from functools import partial
import math

import jax
import jax.numpy as jnp
from jax import lax
from jax.experimental import pallas as pl
from jax.experimental.pallas import tpu as pltpu
from jax.sharding import PartitionSpec as P

H = 12
head_size = 64
head_splits = 4
group_heads = H // head_splits
group_cols = group_heads * head_size
pack_cols = 3 * group_cols
padded_cols = 640
norm_eps = 1e-12
log_two = math.log(2.0)
masked_score = -1e30
low_type = jnp.bfloat16
wide_type = jnp.float32
score_scale = 1.0 / (log_two * math.sqrt(head_size))
some_vmem, most_vmem = 24 << 20, 58 << 20

plain_dims = (((1,), (0,)), ((), ()))
back_dims = (((1,), (1,)), ((), ()))
weight_dims = (((0,), (0,)), ((), ()))

in_smem = pl.BlockSpec(memory_space=pltpu.SMEM)
in_vmem = pl.BlockSpec(memory_space=pltpu.VMEM)
in_any = pl.BlockSpec(memory_space=pl.ANY)


def product(left_op, right_op, dims=plain_dims):
    return lax.dot_general(left_op, right_op, dims, preferred_element_type=wide_type)


def lanes_of(shape):
    return lax.broadcasted_iota(jnp.int32, shape, 1)


def compiled(name, vmem=some_vmem):
    return dict(
        name=name,
        cost_estimate=pl.CostEstimate(flops=1, bytes_accessed=1, transcendentals=0),
        compiler_params=pltpu.CompilerParams(vmem_limit_bytes=vmem),
    )


class Sum:
    def __init__(self, keep, got):
        self.keep, self.got = keep, got

    def close(self):
        return (self.keep.astype(wide_type) + self.got.astype(wide_type)).astype(low_type)


class Order:
    def __init__(self, place):
        self.place, self.last = place, []

    def next(self, *others):
        names = self.last + [(other, "got") for other in others]
        values = [getattr(owner, name) for owner, name in names]
        place, *values = lax.optimization_barrier((self.place, *values))
        for (owner, name), value in zip(names, values):
            setattr(owner, name, value)
        return place

    def did(self, owner, name="keep"):
        self.last = [(owner, name)]


def low_array(*shape):
    return jax.ShapeDtypeStruct(shape, low_type)


def wide_array(*shape):
    return jax.ShapeDtypeStruct(shape, wide_type)


def head_front(tile, head):
    begin = head // 2 * 128
    if begin + 128 <= tile.shape[1]:
        part = tile[:, begin : begin + 128]
        if head % 2:
            part = pltpu.roll(part, 64, 1)
    else:
        part = jnp.concatenate([tile[:, begin:], jnp.zeros_like(tile[:, begin:])], axis=1)
    return jnp.where(lanes_of(part.shape) < 64, part, 0.0)


def head_rear(tile, head):
    begin = head // 2 * 128
    if begin + 128 <= tile.shape[1]:
        part = tile[:, begin : begin + 128]
        if head % 2 == 0:
            part = pltpu.roll(part, 64, 1)
    else:
        part = jnp.concatenate([jnp.zeros_like(tile[:, begin:]), tile[:, begin:]], axis=1)
    return jnp.where(lanes_of(part.shape) >= 64, part, 0.0)


(at_row, at_core, at_x, at_z, at_group, at_ring, at_first, at_length, at_near, at_mine, at_other) = range(11)


def pack_kernel(place_ref, q_ref, k_ref, v_ref, all_ref, own_ref, half_ref):
    rows = q_ref.shape[0]
    for group in range(head_splits):
        part = pl.ds(group * rows, rows)
        for head in range(group_heads):
            begin = (group * group_heads + head) * head_size
            all_ref[part, head * 128 : head * 128 + 64] = k_ref[:, begin : begin + head_size]
            all_ref[part, head * 128 + 64 : head * 128 + 128] = v_ref[:, begin : begin + head_size]
        all_ref[part, 2 * group_cols : pack_cols] = q_ref[:, group * group_cols : (group + 1) * group_cols]
        all_ref[part, pack_cols:] = jnp.zeros((rows, padded_cols - pack_cols), low_type)
    start = place_ref[at_group] * rows
    own_ref[...] = all_ref[pl.ds(pl.multiple_of(start, rows), rows), :pack_cols]
    start = start + place_ref[at_mine] * (rows // 2)
    half_ref[...] = all_ref[pl.ds(pl.multiple_of(start, rows // 2), rows // 2), :pack_cols]


def pack_weights(place, query_weight, key_weight, value_weight):
    rows = query_weight.shape[0]
    return pl.pallas_call(
        pack_kernel,
        in_specs=[in_smem] + [in_vmem] * 3,
        out_specs=[in_vmem] * 3,
        out_shape=[
            low_array(head_splits * rows, padded_cols),
            low_array(rows, pack_cols),
            low_array(rows // 2, pack_cols),
        ],
        **compiled("pack_weights", most_vmem),
    )(place, query_weight, key_weight, value_weight)


def whole_vector(place_ref, own_ref, other_ref, begin, size):
    own = own_ref[:, begin : begin + size].astype(wide_type)
    other = other_ref[:, begin : begin + size].astype(wide_type)
    first = place_ref[at_near] == 0
    return jnp.concatenate([jnp.where(first, own, other), jnp.where(first, other, own)], axis=1)


def ship_kernel(place_ref, out_ref, inner_ref, outer_ref, ship_ref, sems):
    width = out_ref.shape[1]
    copies = []
    start = 0

    def send(ref, cols):
        nonlocal start
        half = ref.shape[0] // 2
        source = ref.at[pl.ds(pl.multiple_of(place_ref[at_mine] * half, half), half), cols]
        copies.append(
            pltpu.make_async_copy(source, ship_ref.at[pl.ds(start, half), :], sems.at[len(copies)])
        )
        copies[-1].start()
        start += half

    send(outer_ref, pl.ds(0, width))
    for k in range(0, inner_ref.shape[1], width):
        send(inner_ref, pl.ds(k, width))
    send(out_ref, pl.ds(0, width))
    for copy in copies:
        copy.wait()


def shipment(place, weights):
    width = weights[0].shape[1]
    chunks = weights[1].shape[1] // width
    rows = (weights[0].shape[0] + weights[1].shape[0] * chunks + weights[2].shape[0]) // 2
    return pl.pallas_call(
        ship_kernel,
        in_specs=[in_smem] + [in_any] * 3,
        out_specs=in_vmem,
        out_shape=low_array(rows, width),
        scratch_shapes=[pltpu.SemaphoreType.DMA((chunks + 2,))],
        **compiled("shipment", most_vmem),
    )(place, *weights)


def project_kernel(place_ref, x0, x1, x2, x3, own_ref, mine_ref, rest_ref, near_ref, far_ref, q_ref, kv_ref, other_ref):
    half = own_ref.shape[0]
    rows = x0.shape[0]
    near = pl.multiple_of(place_ref[at_near] * half, 128)
    far = pl.multiple_of((1 - place_ref[at_near]) * half, 128)
    kv_cols = 2 * group_cols
    for fetched, core in ((mine_ref, place_ref[at_mine]), (rest_ref, 1 - place_ref[at_mine])):
        other_ref[pl.ds(pl.multiple_of(core * (half // 2), half // 2), half // 2), :] = fetched[...]
    biases = [whole_vector(place_ref, near_ref, far_ref, k * half, half) for k in range(2)]
    q_bias, v_bias = [jnp.zeros((1, group_cols), wide_type)] * 2
    for group in range(head_splits):
        cols = slice(group * group_cols, (group + 1) * group_cols)
        q_bias = jnp.where(place_ref[at_group] == group, biases[0][:, cols], q_bias)
        v_bias = jnp.where(place_ref[at_group] == group, biases[1][:, cols], v_bias)
    kv_bias = []
    for head in range(group_heads):
        kv_bias += [jnp.zeros((1, head_size), wide_type), v_bias[:, head * 64 : head * 64 + 64]]
    bias = jnp.concatenate(kv_bias + [q_bias], axis=1)
    for k, x_ref in enumerate((x0, x1, x2, x3)):
        part = pl.ds(k * rows, rows)
        made = product(x_ref[:, pl.ds(near, half)], own_ref[...])
        made = made + product(x_ref[:, pl.ds(far, half)], other_ref[...]) + bias
        kv_ref[part, :] = made[:, :kv_cols].astype(low_type)
        q_ref[part, :] = (made[:, kv_cols:] * score_scale).astype(low_type)


def project(place, blocks, own, mine, rest, vectors):
    rows, width = blocks[0].shape
    line = rows * head_splits
    return pl.pallas_call(
        project_kernel,
        in_specs=[in_smem] + [in_vmem] * 9,
        out_specs=[in_vmem] * 2,
        out_shape=[low_array(line, group_cols), low_array(line, 2 * group_cols)],
        scratch_shapes=[pltpu.VMEM(own.shape, low_type)],
        **compiled("project", most_vmem),
    )(place, *blocks, own, mine, rest, *vectors)


def attend_kernel(starts, resumed, finished, place_ref, q_ref, *refs):
    pieces = len(starts)
    kv_refs, aug_ref = refs[:pieces], refs[pieces]
    refs = refs[pieces + 1 :]
    state_ref, out_refs = (refs[0], refs[1:]) if resumed else (None, refs)
    rows = q_ref.shape[0]
    joints = [[]]
    for k, kv_ref in enumerate(kv_refs):
        if sum(kv_refs[n].shape[0] for n in joints[-1]) + kv_ref.shape[0] > 2048:
            joints.append([])
        joints[-1].append(k)
    lane = lanes_of((rows, 128))
    q_aug = jnp.where(lane == 0, 1.0, 0.0).astype(low_type)
    stats = jnp.zeros((rows, 128), wide_type)
    q_wide = q_ref[...].astype(wide_type)
    outs = []
    for head in range(group_heads):
        cols = pl.ds(head * 128, 128)
        q_ext = jnp.concatenate([head_front(q_wide, head).astype(low_type), q_aug], axis=1)
        top = None
        if resumed:
            accum = state_ref[:, cols]
            total, top = accum[:, 0:1], accum[:, 1:2]
        for joint in joints:
            kv_ext = jnp.concatenate(
                [
                    jnp.concatenate(
                        [kv_refs[k][:, cols], aug_ref[pl.ds(starts[k], kv_refs[k].shape[0]), :]],
                        axis=1,
                    )
                    for k in joint
                ],
                axis=0,
            )
            scores = product(q_ext, kv_ext, back_dims)
            new_top = jnp.floor(jnp.max(scores, axis=1, keepdims=True))
            if top is not None:
                new_top = jnp.maximum(top, new_top)
            weights = jnp.exp2(scores - new_top).astype(low_type)
            part_sum = product(weights, kv_ext)
            part_total = part_sum[:, 129:130]
            if top is None:
                accum, total = part_sum[:, :128], part_total
            else:
                factor = jnp.exp2(top - new_top)
                accum, total = accum * factor + part_sum[:, :128], total * factor + part_total
            top = new_top
        if finished:
            outs.append(accum / total)
            stats = jnp.where(lane == head, top, stats)
            stats = jnp.where(lane == group_heads + head, total, stats)
        else:
            out_refs[0][:, cols] = jnp.where(lane == 0, total, jnp.where(lane == 1, top, accum))
    if not finished:
        return
    low_refs, wide_ref, stat_ref = out_refs[:head_splits], out_refs[-2], out_refs[-1]
    tiles = []
    for head in range(0, group_heads, 2):
        first = pltpu.roll(outs[head], 64, 1)
        if head + 1 < group_heads:
            tiles.append(jnp.where(lane < 64, first, outs[head + 1]))
        else:
            tiles.append(first[:, :64])
    context = jnp.concatenate(tiles, axis=1)
    wide_ref[...] = context
    stat_ref[...] = stats
    for k, low_ref in enumerate(low_refs):

        @pl.when(pl.program_id(0) == k)
        def _():
            low_ref[...] = context.astype(low_type)


def attend(place, q_line, kv_pieces, order, aug, state, finished):
    line = q_line.shape[0]
    tile = line // head_splits
    whole = lambda i: (0, 0)
    by_tile = lambda i: (i, 0)
    sizes = [piece.shape[0] for piece in kv_pieces]
    used = [kv_pieces[k] for k in order]
    starts = [sum(sizes[:k]) for k in order]
    states = [] if state is None else [state]
    state_cols = 128 * group_heads
    work = line * group_heads * used[0].shape[0] * len(used)
    if finished:
        out_specs = [pl.BlockSpec((tile, group_cols), whole)] * head_splits
        out_specs += [pl.BlockSpec((tile, group_cols), by_tile), pl.BlockSpec((tile, 128), by_tile)]
        out_shape = [low_array(tile, group_cols)] * head_splits
        out_shape += [wide_array(line, group_cols), wide_array(line, 128)]
    else:
        out_specs = pl.BlockSpec((tile, state_cols), by_tile)
        out_shape = wide_array(line, state_cols)
    return pl.pallas_call(
        partial(attend_kernel, starts, state is not None, finished),
        grid=(head_splits,),
        in_specs=[in_smem, pl.BlockSpec((tile, group_cols), by_tile)]
        + [pl.BlockSpec(piece.shape, whole) for piece in used]
        + [pl.BlockSpec(aug.shape, whole)]
        + [pl.BlockSpec((tile, state_cols), by_tile) for _ in states],
        out_specs=out_specs,
        out_shape=out_shape,
        **compiled("attend"),
    )(place, q_line, *used, aug, *states)


def split_three(number):
    first = number.astype(low_type).astype(wide_type)
    second = (number - first).astype(low_type).astype(wide_type)
    return first, second, number - first - second


def attend_back_kernel(head, pieces, first, outs, query_part, place_ref, q_ref, stat_ref, context_ref, g0, g1, g2, g3, *refs):
    kv_refs, aug_ref = refs[:pieces], refs[pieces]
    sum_refs = refs[pieces + 1 : pieces + 1 + outs]
    q_grad_ref, kv_all, q_ext, g_ext = refs[pieces + 1 + outs :]
    rows = q_ref.shape[0]
    query_rows = q_ref.shape[0]
    seg_rows = g0.shape[0]
    step = pl.program_id(0)

    @pl.when(step == 0)
    def _():
        q_grad_ref[...] = jnp.zeros_like(q_grad_ref)
        start = 0
        for kv_ref in kv_refs:
            kv_all[pl.ds(start, kv_ref.shape[0]), :] = kv_ref[...]
            start += kv_ref.shape[0]
        for k, grad_ref in enumerate((g0, g1, g2, g3)):
            part = pl.ds(k * seg_rows, seg_rows)
            lane = lanes_of((seg_rows, 128))
            stats = stat_ref[part, :]
            top = stats[:, head : head + 1]
            total = stats[:, group_heads + head : group_heads + head + 1]
            grad = head_rear(grad_ref[...].astype(wide_type), head)
            context = head_rear(context_ref[part, :], head)
            delta = jnp.sum(grad * context, axis=1, keepdims=True) / total
            q_more = jnp.where(lane == 0, 1.0, 0.0)
            g_more = jnp.zeros((seg_rows, 128), wide_type)
            for place, (of_top, of_delta) in enumerate(zip(split_three(top), split_three(delta))):
                q_more = jnp.where(lane == place + 1, -of_top, q_more)
                g_more = jnp.where(lane == place + 1, -of_delta, g_more)
            q_ext[part, :128] = head_front(q_ref[part, :].astype(wide_type), head).astype(low_type)
            q_ext[part, 128:] = q_more.astype(low_type)
            g_ext[part, :128] = (grad / total).astype(low_type)
            g_ext[part, 128:] = g_more.astype(low_type)

    kv_part = kv_all[pl.ds(pl.multiple_of(step * rows, rows), rows), :]
    aug_part = aug_ref[pl.ds(pl.multiple_of(first + step * rows, rows), rows), :]
    kv_ext = jnp.concatenate([kv_part, aug_part], axis=1)
    keys_turned = jnp.transpose(kv_part)[:64]
    accum = jnp.zeros((rows, 128), wide_type)
    for start in range(0, query_rows, query_part):
        part = pl.ds(start, query_part)
        q_part = q_ext[part, :]
        g_part = g_ext[part, :]
        weights = jnp.exp2(product(kv_ext, q_part, back_dims))
        along_values = product(kv_ext, g_part, back_dims)
        grad_scores = (weights * along_values).astype(low_type)
        accum = accum + product(weights.astype(low_type), g_part[:, :128])
        accum = accum + product(grad_scores, q_part[:, :128])
        q_grad_ref[:, part] += product(keys_turned, grad_scores)
    lane = lanes_of((rows, 128))
    made = (accum * jnp.where(lane < 64, log_two, 1.0)).astype(low_type)

    each = kv_all.shape[0] // rows // outs
    for k, sum_ref in enumerate(sum_refs):

        @pl.when(step // each == k)
        def _():
            sum_ref[...] = made


def attend_back(place, head, q_line, stats, context, grads, kv_pieces, order, outs, aug):
    line = q_line.shape[0]
    sizes = [piece.shape[0] for piece in kv_pieces]
    used = [kv_pieces[k] for k in order]
    length = sum(piece.shape[0] for piece in used)
    each = length // line // outs
    whole = lambda i: (0, 0)
    part_of = lambda k: lambda i: (jnp.clip(i - k * each, 0, each - 1), 0)
    *sums, q_grad = pl.pallas_call(
        partial(
            attend_back_kernel, head, len(used), sum(sizes[: order[0]]), outs, math.gcd(line, 512)
        ),
        grid=(length // line,),
        in_specs=[
            in_smem,
            pl.BlockSpec(q_line.shape, whole),
            pl.BlockSpec(stats.shape, whole),
            pl.BlockSpec(context.shape, whole),
        ]
        + [pl.BlockSpec(grad.shape, whole) for grad in grads]
        + [pl.BlockSpec((piece.shape[0], 128), lambda i: (0, head)) for piece in used]
        + [pl.BlockSpec(aug.shape, whole)],
        out_specs=[pl.BlockSpec((line, 128), part_of(k)) for k in range(outs)]
        + [pl.BlockSpec((head_size, line), whole)],
        out_shape=[low_array(line * each, 128)] * outs + [wide_array(head_size, line)],
        scratch_shapes=[
            pltpu.VMEM((length, 128), low_type),
            pltpu.VMEM((line, 256), low_type),
            pltpu.VMEM((line, 256), low_type),
        ],
        **compiled("attend_back"),
    )(place, q_line, stats, context, *grads, *used, aug)
    return sums, q_grad


def add_pairs_kernel(place_ref, *refs):
    out_ref = refs[-1]
    for k in range(out_ref.shape[0]):
        total = refs[2 * k][...].astype(wide_type) + refs[2 * k + 1][...].astype(wide_type)
        out_ref[k] = total.astype(low_type)


def add_pairs(place, *arrays):
    return pl.pallas_call(
        add_pairs_kernel,
        in_specs=[in_smem] + [in_vmem] * len(arrays),
        out_specs=in_vmem,
        out_shape=low_array(len(arrays) // 2, *arrays[0].shape),
        **compiled("add_pairs"),
    )(place, *arrays)


def add_merge_kernel(place_ref, keep_a, got_a, keep_b, got_b, out_ref):
    start = 0
    for kept, got in ((keep_a, got_a), (keep_b, got_b)):
        rows = kept.shape[1]
        total = kept[...].astype(wide_type) + got[...].astype(wide_type)
        out_ref[:, start : start + rows, :] = total.astype(low_type)
        start += rows


def add_merge(place, keep_a, got_a, keep_b, got_b):
    return pl.pallas_call(
        add_merge_kernel,
        in_specs=[in_smem] + [in_vmem] * 4,
        out_specs=in_vmem,
        out_shape=low_array(2, keep_a.shape[1] + keep_b.shape[1], keep_a.shape[2]),
        **compiled("add_merge"),
    )(place, keep_a, got_a, keep_b, got_b)


def norm_forward(hidden):
    centre = hidden - jnp.mean(hidden, axis=1, keepdims=True)
    inverse = lax.rsqrt(jnp.mean(centre * centre, axis=1, keepdims=True) + norm_eps)
    return centre * inverse, inverse


def norm_back(grad, normal, inverse):
    along = jnp.mean(grad * normal, axis=1, keepdims=True)
    return inverse * (grad - jnp.mean(grad, axis=1, keepdims=True) - normal * along)


def over_tokens(array):
    return jnp.sum(array, axis=0, keepdims=True)


def mid_kernel(place_ref, factor_ref, x_ref, teacher_ref, c0, c1, c2, c3, near_ref, far_ref, *refs):
    own_weights, shipments = refs[0:3], refs[3:5]
    (
        output_ref, sum_ref, d0, d1, d2, d3, act_ref, hidden_ref, normed_ref, branch_ref, attn_ref, small_ref,
        w_out, w_inner, w_outer, slope_ref, sems,
    ) = refs[5:]
    held = (w_out, w_inner, w_outer)
    near, mine = place_ref[at_near], place_ref[at_mine]
    copies = []
    width = x_ref.shape[1]

    def fetch(source, k, start, rows, cols=None):
        target = held[k].at[pl.ds(pl.multiple_of(start, rows), rows), :]
        if cols is not None:
            target = held[k].at[pl.ds(pl.multiple_of(start, rows), rows), cols]
        copies.append(pltpu.make_async_copy(source, target, sems.at[len(copies)]))
        copies[-1].start()

    halves = [weight.shape[0] // 2 for weight in own_weights]
    starts = [
        [(1 - near) * 2 * half + core * half for half in halves] for core in (mine, 1 - mine)
    ]
    out_half, inner_half, outer_half = halves
    chunks = own_weights[1].shape[1] // width
    base = outer_half + chunks * inner_half
    fetch(own_weights[0], 0, near * 2 * out_half, 2 * out_half)
    for ship, (out_start, _, _) in zip(shipments, starts):
        fetch(ship.at[pl.ds(base, out_half), :], 0, out_start, out_half)
    fetch(own_weights[1], 1, near * 2 * inner_half, 2 * inner_half)
    fetch(own_weights[2], 2, near * 2 * outer_half, 2 * outer_half)
    for ship, (_, inner_start, outer_start) in zip(shipments, starts):
        for k in range(chunks):
            source = ship.at[pl.ds(outer_half + k * inner_half, inner_half), :]
            fetch(source, 1, inner_start, inner_half, pl.ds(k * width, width))
        fetch(ship.at[pl.ds(0, outer_half), :], 2, outer_start, outer_half)
    rows = x_ref.shape[0]
    half = width // 2
    vector = lambda k, size: whole_vector(place_ref, near_ref, far_ref, k * half, size)
    b_out, g_attn, s_attn, b_outer, g_final, s_final = (vector(k, half) for k in range(2, 8))
    b_inner = vector(8, w_outer.shape[0] // 2)
    group = place_ref[at_group]
    of_group = lambda k: pl.ds(pl.multiple_of((group ^ k) * group_cols, group_cols), group_cols)

    for copy in copies[0:3]:
        copy.wait()
    hidden = x_ref[...].astype(wide_type) + b_out
    for k, c_ref in enumerate((c0, c1, c2, c3)):
        hidden = hidden + product(c_ref[...], w_out[of_group(k), :])
    attn_normal, attn_inverse = norm_forward(hidden)
    normed = attn_normal * g_attn + s_attn
    normed_low = normed.astype(low_type)
    normed_ref[...] = normed_low
    for copy in copies[3:]:
        copy.wait()
    branch = normed + b_outer
    for k in range(chunks):
        cols = pl.ds(k * width, width)
        pre = product(normed_low, w_inner[:, cols]) + b_inner[:, k * width : (k + 1) * width]
        bell = 0.5 * (1.0 + lax.erf(pre * math.sqrt(0.5)))
        slope_ref[:, cols] = bell + pre * jnp.exp(-0.5 * pre * pre) * (1.0 / math.sqrt(2.0 * math.pi))
        act = (pre * bell).astype(low_type)
        act_ref[:, cols] = act
        branch = branch + product(act, w_outer[cols, :])
    final_normal, final_inverse = norm_forward(branch)
    output = final_normal * g_final + s_final
    output_ref[:, 0, :] = output
    token = place_ref[at_first] + lax.broadcasted_iota(jnp.int32, (rows, 1), 0)
    valid = (token < place_ref[at_length]).astype(wide_type)
    mismatch = (output - teacher_ref[...].astype(wide_type)) * valid
    squares = over_tokens(mismatch * mismatch)
    grad_out = mismatch * factor_ref[0]
    final_gain_grad = over_tokens(grad_out * final_normal)
    final_shift_grad = over_tokens(grad_out)
    grad_mid = norm_back(grad_out * g_final, final_normal, final_inverse)
    grad_branch = grad_mid.astype(low_type)
    branch_ref[...] = grad_branch
    outer_bias_grad = over_tokens(grad_branch.astype(wide_type))
    grad_normed = grad_mid
    inner_bias_grad = []
    for k in range(chunks):
        cols = pl.ds(k * width, width)
        grad_act = product(grad_branch, w_outer[cols, :], back_dims)
        grad_hidden = (grad_act * slope_ref[:, cols]).astype(low_type)
        hidden_ref[:, cols] = grad_hidden
        inner_bias_grad.append(over_tokens(grad_hidden.astype(wide_type)))
        grad_normed = grad_normed + product(grad_hidden, w_inner[:, cols], back_dims)
    attn_gain_grad = over_tokens(grad_normed * attn_normal)
    attn_shift_grad = over_tokens(grad_normed)
    grad_sum = norm_back(grad_normed * g_attn, attn_normal, attn_inverse)
    sum_ref[...] = grad_sum
    grad_attn = grad_sum.astype(low_type)
    attn_ref[...] = grad_attn
    out_bias_grad = over_tokens(grad_attn.astype(wide_type))
    for k, d_ref in enumerate((d0, d1, d2, d3)):
        d_ref[...] = product(grad_attn, w_out[of_group(k), :], back_dims).astype(low_type)
    pairs = (
        (final_gain_grad, final_shift_grad),
        (outer_bias_grad, attn_gain_grad),
        (attn_shift_grad, out_bias_grad),
    )
    for side in range(2):
        cols = slice(side * half, side * half + half)
        lines = [jnp.concatenate([a[:, cols], b[:, cols]], axis=1) for a, b in pairs]
        lines += inner_bias_grad[side * 2 : side * 2 + 2] + [squares]
        lines.append(jnp.zeros((8 - len(lines), width), wide_type))
        small_ref[side] = jnp.concatenate(lines, axis=0)


def middle(place, factor, tokens, teacher, contexts, vectors, weights):
    rows, width = tokens.shape
    ff_width = weights[1].shape[1]
    return pl.pallas_call(
        mid_kernel,
        in_specs=[in_smem, in_smem] + [in_vmem] * 8 + [in_any] * 5,
        out_specs=[in_vmem] * 12,
        out_shape=[wide_array(rows, 1, width), wide_array(rows, width)]
        + [low_array(rows, group_cols)] * 4
        + [low_array(rows, ff_width)] * 2
        + [low_array(rows, width)] * 3
        + [wide_array(2, 8, width)],
        scratch_shapes=[
            pltpu.VMEM((width, width), low_type),
            pltpu.VMEM((width, ff_width), low_type),
            pltpu.VMEM((ff_width, width), low_type),
            pltpu.VMEM((rows, ff_width), wide_type),
            pltpu.SemaphoreType.DMA((5 + 2 * (1 + ff_width // width),)),
        ],
        **compiled("middle", most_vmem),
    )(place, factor, tokens, teacher, *contexts, *vectors, *weights)


def weight_kernel(
    place_ref, act_ref, branch_ref, normed_ref, hidden_ref, c0, c1, c2, c3, attn_ref, small_ref,
    give_a, keep_a, give_b, keep_b, out_grad,
):
    width = branch_ref.shape[1]
    half = width // 2
    group = place_ref[at_group]

    @pl.when((pl.program_id(0) == 0) & (pl.program_id(1) == 0))
    def _():
        for k, c_ref in enumerate((c0, c1, c2, c3)):
            part = pl.ds(pl.multiple_of((group ^ k) * group_cols, group_cols), group_cols)
            out_grad[part, :] = product(c_ref[...], attn_ref[...], weight_dims)

    row = place_ref[at_row] ^ pl.program_id(0)
    x = place_ref[at_x] ^ pl.program_id(1)
    for far, a_ref, b_ref in ((1, give_a, give_b), (0, keep_a, keep_b)):
        core = place_ref[at_core] ^ far
        begin = pl.multiple_of(((row * 2 + core) * 2 + x) * half, 128)
        outer = product(
            act_ref[:, pl.ds(begin, half)], branch_ref[...], weight_dims
        ).astype(low_type)
        inner = product(
            normed_ref[:, pl.ds(pl.multiple_of(row * half, 128), half)],
            hidden_ref[:, pl.ds(pl.multiple_of((core * 2 + x) * width, 128), width)],
            weight_dims,
        ).astype(low_type)
        base = row * half + core * (half // 2) + x * (half // 4)
        for z in range(4):
            apart = place_ref[at_z] ^ z
            low, high = pl.ds(apart & 1, 1), pl.ds(apart >> 1, 1)
            rows = slice(z * 96, z * 96 + 96)
            shaped = lambda block: block[None, None, None, None]
            a_ref[0:1, low, 0:1, high, :, :] = shaped(outer[rows])
            rest = out_grad[pl.ds(pl.multiple_of(base + z * 24, 8), 24), :]
            rest = jnp.concatenate([rest, small_ref[pl.ds(row, 1)][0]], axis=0).astype(low_type)
            b_ref[0:1, 0:1, low, high, :, :] = shaped(jnp.concatenate([inner[rows], rest], axis=0))


def weight_grads(place, act, branch, normed, hidden, contexts, attn, small):
    rows, width = branch.shape
    a_shape, b_shape = (2, 2, 2, 2, 96, width), (2, 2, 2, 2, 128, width)
    a_spec = pl.BlockSpec((1, 2, 1, 2, 96, width), lambda i, j: (i, 0, j, 0, 0, 0))
    b_spec = pl.BlockSpec((1, 1, 2, 2, 128, width), lambda i, j: (j, i, 0, 0, 0, 0))
    return pl.pallas_call(
        weight_kernel,
        grid=(2, 2),
        in_specs=[in_smem] + [in_vmem] * 10,
        out_specs=[a_spec, a_spec, b_spec, b_spec],
        out_shape=[low_array(*a_shape)] * 2 + [low_array(*b_shape)] * 2,
        scratch_shapes=[pltpu.VMEM((width, width), wide_type)],
        **compiled("weight_grads", most_vmem),
    )(place, act, branch, normed, hidden, *contexts, attn, small)


def add_split_kernel(gots, place_ref, kept_ref, *refs):
    got_refs, keep_ref, give_refs = refs[:gots], refs[gots], refs[gots + 1 :]
    got = [got_refs[0][0], got_refs[0][1]] if gots == 1 else [got_ref[...] for got_ref in got_refs]
    total = [
        (kept_ref[k].astype(wide_type) + got[k].astype(wide_type)).astype(low_type) for k in range(2)
    ]
    keep_ref[...] = total[0]
    rows = give_refs[0].shape[0]
    for k, give_ref in enumerate(give_refs):
        give_ref[...] = total[1][k * rows : (k + 1) * rows]


def add_split(place, kept, got, parts=1):
    cols = kept.shape[-1]
    shape = (2, kept.size // cols // 2, cols)
    if isinstance(got, list):
        gots = [array.reshape(shape[1:]) for array in got]
    else:
        gots = [got.reshape(shape)]
    keep, *gives = pl.pallas_call(
        partial(add_split_kernel, len(gots)),
        in_specs=[in_smem] + [in_vmem] * (1 + len(gots)),
        out_specs=[in_vmem] * (1 + parts),
        out_shape=[low_array(*shape[1:])] + [low_array(shape[1] // parts, cols)] * parts,
        **compiled("add_split"),
    )(place, kept.reshape(shape), *gots)
    gives = [give.reshape(kept.shape[1:]) if parts == 1 else give for give in gives]
    return keep.reshape(kept.shape[1:]), gives


def unpack_kernel(
    place_ref, own_a, got_a, own_b, got_b, outer_ref, inner_ref, out_ref, wide_a, wide_b, sems
):
    width = own_a.shape[-1]
    half = width // 2
    copies = []

    def send(source, target):
        copy = pltpu.make_async_copy(source, target, sems.at[len(copies)])
        copy.start()
        copies.append(copy)

    for k in range(16):
        core = place_ref[at_core] ^ (k // 8)
        x = place_ref[at_x] ^ (k // 4 % 2)
        z = place_ref[at_z] ^ (k // 2 % 2 + 2 * (k % 2))
        a_ref, b_ref = (got_a, got_b) if k // 8 else (own_a, own_b)
        wide_a[k] = a_ref[k // 4 % 2, k // 2 % 2, k % 2].astype(wide_type)
        start = pl.multiple_of((core * 2 + x) * half + z * 96, 32)
        send(wide_a.at[k], outer_ref.at[pl.ds(start, 96), :])
        wide_b[k] = b_ref[k // 2 % 2, k // 4 % 2, k % 2].astype(wide_type)
        cols = pl.ds(pl.multiple_of((core * 2 + x) * width, 128), width)
        send(wide_b.at[k, 0:96], inner_ref.at[pl.ds(pl.multiple_of(z * 96, 32), 96), cols])
        start = pl.multiple_of(core * (half // 2) + x * (half // 4) + z * 24, 8)
        send(wide_b.at[k, 96:120], out_ref.at[pl.ds(start, 24), :])
    for copy in copies:
        copy.wait()


def unpack(place, own_a, got_a, own_b, got_b):
    width = own_a.shape[-1]
    return pl.pallas_call(
        unpack_kernel,
        in_specs=[in_smem] + [in_vmem] * 4,
        out_specs=[in_any] * 3,
        out_shape=[
            wide_array(2 * width, width), wide_array(width // 2, 4 * width), wide_array(width // 2, width)
        ],
        scratch_shapes=[
            pltpu.VMEM((16, own_a.shape[-2], width), wide_type),
            pltpu.VMEM((16, own_b.shape[-2], width), wide_type),
            pltpu.SemaphoreType.DMA((48,)),
        ],
        **compiled("unpack"),
    )(place, own_a, got_a, own_b, got_b)


def rows_kernel(counts, terms, place_ref, *refs):
    heads, used = len(counts), sum(counts)
    q_grads, kv_terms = refs[:used], refs[used : used + sum(terms)]
    refs = refs[used + sum(terms) :]
    blocks = refs[:4]
    r0, r1, r2, r3, give0, give1, keep0, keep1, w_grad, all_rows = refs[4:]
    rows, width = blocks[0].shape
    kv_cols = 2 * group_cols
    for k in range(heads):
        total = 0.0
        for n in range(sum(terms[:k]), sum(terms[: k + 1])):
            term = kv_terms[n]
            total = total + (term[...] if len(term.shape) == 2 else term[k]).astype(wide_type)
        all_rows[:, k * 128 : k * 128 + 128] = total.astype(low_type)
    firsts = [sum(counts[:k]) for k in range(heads)]
    turned = [
        sum((ref[...] for ref in q_grads[first + 1 : first + count]), q_grads[first][...])
        for first, count in zip(firsts, counts)
    ]
    turned = jnp.concatenate(turned, axis=0) * 0.125
    all_rows[:, kv_cols:] = jnp.transpose(turned).astype(low_type)
    half = width // 2
    bias = jnp.zeros((1, pack_cols), wide_type)
    for k, r_ref in enumerate((r0, r1, r2, r3)):
        made = all_rows[pl.ds(k * rows, rows), :]
        r_ref[...] = made
        bias = bias + over_tokens(made.astype(wide_type))
        for side in range(2):
            part = product(blocks[k][:, side * half : side * half + half], made, weight_dims)
            if k:
                w_grad[side] += part
            else:
                w_grad[side] = part
    bias = jnp.concatenate([bias, jnp.zeros((15, pack_cols), wide_type)], axis=0)
    for far, piece_refs in ((1, (give0, give1)), (0, (keep0, keep1))):
        start = pl.multiple_of((place_ref[at_core] ^ far) * (half // 2), half // 2)
        for j in range(2):
            row = place_ref[at_row] ^ j
            block = w_grad[pl.ds(row, 1), pl.ds(start, half // 2), :][0]
            piece_refs[j][...] = jnp.concatenate([block, bias], axis=0).astype(low_type)


def project_back(place, q_grads, kv_terms, blocks):
    counts = [len(q_grad) for q_grad in q_grads]
    terms = [len(head) for head in kv_terms]
    every = [array for head in q_grads + kv_terms for array in head]
    rows, width = blocks[0].shape
    pieces = (width // 4 + 16, pack_cols)
    return pl.pallas_call(
        partial(rows_kernel, counts, terms),
        in_specs=[in_smem] + [in_vmem] * (len(every) + 4),
        out_specs=[in_vmem] * 8,
        out_shape=[low_array(rows, pack_cols)] * 4 + [low_array(*pieces)] * 4,
        scratch_shapes=[
            pltpu.VMEM((2, width // 2, pack_cols), wide_type),
            pltpu.VMEM((4 * rows, pack_cols), low_type),
        ],
        **compiled("project_back", most_vmem),
    )(place, *every, *blocks)


def input_kernel(place_ref, sum_ref, r0, r1, r2, r3, own_ref, mine_ref, other_ref, grad_ref):
    half = own_ref.shape[0] // head_splits
    near = jnp.zeros((sum_ref.shape[0], half), wide_type)
    far = jnp.zeros((sum_ref.shape[0], half), wide_type)
    for k, r_ref in enumerate((r0, r1, r2, r3)):
        group = place_ref[at_group] ^ k
        near = near + product(r_ref[...], own_ref[pl.ds(pl.multiple_of(group * half, half), half), :pack_cols], back_dims)
        fetched = (group >> 1) == place_ref[at_mine]
        side = pl.ds(pl.multiple_of((group & 1) * half, half), half)
        weight = jnp.where(fetched, mine_ref[side, :pack_cols], other_ref[side, :pack_cols])
        far = far + product(r_ref[...], weight, back_dims)
    for part, begin in ((near, place_ref[at_near]), (far, 1 - place_ref[at_near])):
        cols = pl.ds(pl.multiple_of(begin * half, 128), half)
        grad_ref[:, 0, cols] = sum_ref[:, cols] + part


def input_back(place, grad_sum, rows, packs):
    return pl.pallas_call(
        input_kernel,
        in_specs=[in_smem] + [in_vmem] * 8,
        out_specs=in_vmem,
        out_shape=wide_array(grad_sum.shape[0], 1, grad_sum.shape[1]),
        **compiled("input_back"),
    )(place, grad_sum, *rows, *packs)


def qkv_unpack_kernel(place_ref, here_ref, there_ref, q_ref, k_ref, v_ref, bias_ref):
    side = q_ref.shape[0] // 2
    bias_ref[...] = jnp.zeros_like(bias_ref)
    for own in range(head_splits):

        @pl.when(place_ref[at_group] == own)
        def _():
            for n, piece in enumerate((here_ref, there_ref)):
                part = pl.ds(pl.multiple_of((place_ref[at_core] ^ n) * side, side), side)
                for k in range(head_splits):
                    first = (own ^ k) * group_cols
                    block = piece[k].astype(wide_type)
                    q_ref[part, first : first + group_cols] = block[:side, 2 * group_cols :]
                    for h in range(group_heads):
                        begin = first + h * head_size
                        keys = slice(h * 128, h * 128 + 64)
                        values = slice(h * 128 + 64, h * 128 + 128)
                        k_ref[part, begin : begin + head_size] = block[:side, keys]
                        v_ref[part, begin : begin + head_size] = block[:side, values]
                        if n == 0:
                            bias_ref[1:2, begin : begin + head_size] = block[side : side + 1, values]
                    if n == 0:
                        bias_ref[0:1, first : first + group_cols] = block[
                            side : side + 1, 2 * group_cols :
                        ]


def qkv_unpack(place, here, there, width):
    return pl.pallas_call(
        qkv_unpack_kernel,
        in_specs=[in_smem] + [in_vmem] * 2,
        out_specs=[in_vmem] * 4,
        out_shape=[wide_array(width // 2, width)] * 3 + [wide_array(8, width)],
        **compiled("qkv_unpack"),
    )(place, here, there)


class Layout:
    def __init__(self):
        self.ctx = lax.axis_size("ctx")
        self.fsdp = lax.axis_size("fsdp")
        self.me = lax.axis_index("ctx")
        self.row = lax.axis_index("fsdp")
        self.fast = self.ctx == 16 and self.fsdp == 2
        group_bits = (2, 4) if self.fast else (self.ctx // 4, self.ctx // 2)
        bits = [1 << k for k in reversed(range(self.ctx.bit_length() - 1))]
        self.ring_bits = [bit for bit in bits if bit not in group_bits]
        self.group = self.bit(group_bits[0]) + 2 * self.bit(group_bits[1])
        self.group_codes = [0, group_bits[0], group_bits[1], group_bits[0] | group_bits[1]]
        self.ring_codes = [0]
        for bit in self.ring_bits:
            self.ring_codes = self.ring_codes + [code | bit for code in self.ring_codes]

    def bit(self, bit):
        return (self.me // bit) % 2

    def swap(self, block, code):
        return lax.ppermute(block, "ctx", [(i, i ^ code) for i in range(self.ctx)])

    def groups(self, blocks):
        return [blocks[0]] + [self.swap(blocks[k], self.group_codes[k]) for k in range(1, 4)]

    def across(self, block):
        return lax.ppermute(block, "fsdp", [(0, 1), (1, 0)])


def shards(
    layer_input,
    teacher_states,
    seq_lengths,
    query_weight,
    query_bias,
    key_weight,
    value_weight,
    value_bias,
    out_weight,
    out_bias,
    attn_gain,
    attn_shift,
    inner_weight,
    inner_bias,
    outer_weight,
    outer_bias,
    final_gain,
    final_shift,
):
    at = Layout()
    seg_rows, groups, width = layer_input.shape
    shard_rows = query_weight.shape[0]
    ff_rows = outer_weight.shape[0]
    ff_width = inner_weight.shape[1]
    tokens = layer_input.reshape(seg_rows, width)
    teacher = teacher_states.reshape(seg_rows, width)
    two_rows = at.fsdp == 2
    place = jnp.stack(
        [
            at.row, at.bit(1), at.bit(2), at.bit(4) + 2 * at.bit(8), at.group, at.bit(8),
            at.me * seg_rows, seq_lengths[0],
            at.row if two_rows else 0, at.bit(1), 0,
        ]
    ).astype(jnp.int32)

    blocks = at.groups([tokens] * 4)
    all_pack, own_pack, half_pack = pack_weights(place, query_weight, key_weight, value_weight)
    if two_rows:
        mine_part = at.across(half_pack)
    else:
        full = lax.all_gather(own_pack, "fsdp", axis=0, tiled=True)
        own_pack, far = full[: width // 2], full[width // 2 :]
        mine_part = lax.dynamic_slice_in_dim(far, at.bit(1) * (width // 4), width // 4, 0)
    rest_part = at.swap(mine_part, 1)
    vectors = (
        query_bias, value_bias, out_bias, attn_gain, attn_shift,
        outer_bias, final_gain, final_shift, inner_bias,
    )
    if two_rows:
        *vectors, own_pack = lax.optimization_barrier((*vectors, own_pack))
        own_vectors = jnp.concatenate(vectors).reshape(1, -1)
        vectors = (own_vectors, at.across(own_vectors))
    else:
        whole = lambda vector: lax.all_gather(vector, "fsdp", axis=0, tiled=True).reshape(2, -1)
        both = jnp.concatenate([whole(vector) for vector in vectors], axis=1)
        vectors = (both[:1], both[1:])
    own_count = jnp.sum(seq_lengths).astype(wide_type)
    weights = [out_weight, inner_weight, outer_weight]
    if two_rows:
        valid_count = own_count + at.across(own_count.reshape(1))[0]
        ship, rest_part, vectors, blocks, valid_count = lax.optimization_barrier(
            (shipment(place, weights), rest_part, vectors, blocks, valid_count)
        )
        ship = at.across(ship)
    q_line, kv_line = project(place, blocks, own_pack, mine_part, rest_part, vectors)
    if not two_rows:
        valid_count = lax.psum(own_count, "fsdp")

    source = jnp.stack(
        [at.me ^ (ring | group) for ring in at.ring_codes for group in at.group_codes]
    )
    position = (source[:, None] * seg_rows + jnp.arange(seg_rows)[None, :]).reshape(-1, 1)
    lane = lax.broadcasted_iota(jnp.int32, (position.shape[0], 128), 1)
    mask = jnp.where(position < seq_lengths[0], 0.0, masked_score)
    aug = jnp.where(lane == 0, mask, jnp.where(lane < 4, 1.0, 0.0)).astype(low_type)

    if at.fast:
        near = at.swap(kv_line, 1)
        far = at.swap(kv_line, 8)
        state = attend(place, q_line, [kv_line, far, near, far], (0, 2), aug, None, False)
        far, state = lax.optimization_barrier((far, state))
        kv_pieces = [kv_line, far, near, at.swap(far, 1)]
        order = (1, 3)
    else:
        kv_pieces = [kv_line]
        for bit in at.ring_bits:
            kv_pieces = kv_pieces + [at.swap(piece, bit) for piece in kv_pieces]
        state, order = None, tuple(range(len(kv_pieces)))
    *context_low, context, stats = attend(place, q_line, kv_pieces, order, aug, state, True)
    if two_rows:
        ship, stats = lax.optimization_barrier((ship, stats))
        weights += [ship, at.swap(ship, 1)]
    else:
        full = [lax.all_gather(weight, "fsdp", axis=0, tiled=True) for weight in weights]
        far = [weight[weight.shape[0] // 2 :] for weight in full]
        weights = [weight[: weight.shape[0] // 2] for weight in full]
        ship = shipment(place, far)
        weights += [ship, at.swap(ship, 1)]
    contexts = at.groups(context_low)
    token_total = seg_rows * groups * at.ctx * at.fsdp
    factor = (2.0 * token_total / valid_count).reshape(1)
    output, grad_sum, g0, g1, g2, g3, act, hidden, normed, branch, attn, small = middle(
        place, factor, tokens, teacher, contexts, vectors, weights
    )
    if two_rows:
        half = all_pack.shape[0] // 2
        mine_pack = lax.dynamic_slice_in_dim(all_pack, at.bit(1) * half, half, 0)
    else:
        by_row = lax.all_gather(all_pack, "fsdp", axis=0, tiled=False)
        by_row = by_row.reshape(at.fsdp, head_splits, shard_rows, padded_cols)
        whole = by_row.transpose(1, 0, 2, 3).reshape(head_splits, width, padded_cols)
        near, far = whole[:, : width // 2], whole[:, width // 2 :]
        flat = lambda pack: pack.reshape(-1, padded_cols)
        mine = lax.dynamic_slice_in_dim(far, at.bit(1) * 2, 2, 0)
        packs = (flat(near), flat(mine), at.swap(flat(mine), 1))
    grads = at.groups([g0, g1, g2, g3])

    over = lambda bit: lambda block: at.swap(block, bit)
    order = Order(place)

    def add(total, shape, move, *others, parts=1):
        total.keep, gives = add_split(
            order.next(*others), total.keep.reshape(shape), total.got, parts
        )
        moved = [move(give) for give in gives]
        total.got = moved[0] if parts == 1 else moved
        order.did(total)

    heads, q_grads = [], []

    def back(*others, split=False):
        args = (len(heads), q_line, stats, context, grads, kv_pieces)
        if split:
            give, first = attend_back(order.next(*others), *args, (2, 3), 2, aug)
            far = Sum(give[1], at.swap(give[1], 1))
            own = Sum(give[0], at.swap(give[0], 1))
            order.did(far)
            keep, second = attend_back(order.next(), *args, (0, 1), 2, aug)
            own.keep, far.keep = keep
            q_grads.append([first, second])
        else:
            sums, first = attend_back(order.next(*others), *args, (0, 1, 2, 3), 4, aug)
            own, far = Sum(sums[0], at.swap(sums[2], 1)), Sum(sums[1], at.swap(sums[3], 1))
            q_grads.append([first])
        order.did(far)
        heads.append((own, far))

    def send_far(*used, needs=()):
        pairs = [array for head in used for array in (heads[head][1].keep, heads[head][1].got)]
        sums = add_pairs(order.next(*needs), *pairs)
        total = Sum(sums, at.swap(sums, 8))
        order.did(total)
        return total

    if at.fast:
        give_a, keep_a, give_b, keep_b = weight_grads(
            place, act, branch, normed, hidden, contexts, attn, small
        )
        give_a, give_b, *grads = lax.optimization_barrier((give_a, give_b, *grads))
        part_a, part_b = Sum(keep_a, at.swap(give_a, 1)), Sum(keep_b, at.swap(give_b, 1))
        shape_a, shape_b = (2, -1, 96, width), (2, -1, 128, width)
        def step(move_a, move_b, parts=1):
            add(part_a, shape_a, move_a, parts=parts)
            add(part_b, shape_b, move_b, parts=parts)

        back()
        step(at.across, over(2))
        back()
        firsts = send_far(0, 1)
        back(split=True)
        step(over(4), at.across, 2)
        lasts = send_far(2, needs=(firsts,))
        step(over(2), over(4))
        lay = lambda part, rows: (part.keep.reshape(2, rows, width), part.got.reshape(2, rows, width))
        both = add_merge(order.next(lasts), *lay(part_a, 96), *lay(part_b, 128))
        both, mine_pack = lax.optimization_barrier((both, mine_pack))
        both = Sum(both, at.swap(both, 8))
        mine_pack = at.across(mine_pack)
        packs = (all_pack, mine_pack, at.swap(mine_pack, 1))
        order.did(both)
        fars = [firsts.got, firsts.got, lasts.got[0]]
        kv_terms = [[own.keep, own.got, far] for (own, _), far in zip(heads, fars)]
        r0, r1, r2, r3, give0, give1, keep0, keep1 = project_back(
            order.next(), q_grads, kv_terms, blocks
        )
        qkv = Sum(keep1, at.swap(give1, 1))
        order.did(qkv)
        rows = at.groups([r0, r1, r2, r3])
        got0 = at.swap(give0, 1)
        (onward,) = add_pairs(order.next(), qkv.keep, qkv.got)
        onward = at.across(onward)
        rows, both.got = lax.optimization_barrier((rows, both.got))
        both.got = jnp.concatenate([both.got[1:], both.got[:1]])
        both = both.close()
        small = both[0, 216:].astype(wide_type)
        own_a, own_b = both[:, :96], both[:, 96:]
        own_a, own_b = Sum(own_a, at.swap(own_a, 4)), Sum(own_b, at.swap(own_b, 2))
        qkv = sum(part.astype(wide_type) for part in (keep0, got0, onward)).astype(low_type)
        qkv = Sum(qkv, at.swap(qkv, 8))

        def joined(own, bit):
            own.keep = jnp.stack([own.keep, own.got])
            own.got = at.swap(own.keep, bit)

        joined(own_a, 2)
        joined(own_b, 4)
        input_grad = input_back(place, grad_sum, rows, packs)
        own_b.got, input_grad = lax.optimization_barrier((own_b.got, input_grad))
        here = at.groups([qkv.close()] * head_splits)
        here = jnp.stack(here)
        there = at.swap(here, 1)
        mine = lambda bias, k: lax.dynamic_slice_in_dim(bias[k], at.row * shard_rows, shard_rows, 0)
        side = (small[:3, :shard_rows], small[:3, shard_rows:], small[3:5].reshape(-1), jnp.sum(small[5]))
        side, own_a.got = lax.optimization_barrier((side, own_a.got))
        left, right, inner_bias_grad, total_sq = side
        final_gain_grad, outer_bias_grad, attn_shift_grad = left
        final_shift_grad, attn_gain_grad, out_bias_grad = right
        joined(own_a, 1)
        joined(own_b, 1)
        outer_weight_grad, inner_weight_grad, out_weight_grad = unpack(
            place, own_a.keep, own_a.got, own_b.keep, own_b.got
        )
        query_weight_grad, key_weight_grad, value_weight_grad, bias = qkv_unpack(
            place, here, there, width
        )
        query_bias_grad, value_bias_grad = mine(bias, 0), mine(bias, 1)
    else:
        kv_terms = []
        every = tuple(range(len(kv_pieces)))
        for head in range(group_heads):
            (keep, give), q_grad = attend_back(
                place, head, q_line, stats, context, grads, kv_pieces, every, 2, aug
            )
            q_grads.append([q_grad])
            total = Sum(keep, at.swap(give, 1))
            for bit in at.ring_bits[-2::-1]:
                add(total, (2, -1, 128), over(bit))
            kv_terms.append([total.keep, total.got])
        r0, r1, r2, r3, *_ = project_back(place, q_grads, kv_terms, blocks)
        rows = at.groups([r0, r1, r2, r3])
        input_grad = input_back(place, grad_sum, rows, packs)
        all_rows = jnp.concatenate([r0, r1, r2, r3])
        line = jnp.concatenate(blocks)

        def summed(partial_sum):
            mine = lax.psum_scatter(partial_sum, "fsdp", scatter_dimension=0, tiled=True)
            return lax.psum(mine, "ctx")

        qkv = product(line, all_rows, weight_dims)
        qkv = jnp.concatenate([qkv, jnp.sum(all_rows, axis=0, dtype=wide_type)[None]])
        qkv = lax.dynamic_update_slice(
            jnp.zeros((width + 1, head_splits, pack_cols), wide_type), qkv[:, None], (0, at.group, 0)
        )
        kv = qkv[:, :, : 2 * group_cols].reshape(width + 1, H, 2, head_size)
        parts = [qkv[:, :, 2 * group_cols :], kv[:, :, 0], kv[:, :, 1]]
        parts = [part.reshape(width + 1, width) for part in parts]
        query_weight_grad, key_weight_grad, value_weight_grad = (
            summed(part[:width]) for part in parts
        )
        outer_weight_grad = summed(product(act, branch, weight_dims))
        inner_weight_grad = summed(product(normed, hidden, weight_dims))
        whole = jnp.zeros((width, width), wide_type)
        for k in range(head_splits):
            whole = lax.dynamic_update_slice_in_dim(
                whole, product(contexts[k], attn, weight_dims), (at.group ^ k) * group_cols, 0
            )
        out_weight_grad = summed(whole)
        sums = small[:, :3].reshape(2, 3, 2, width // 2).transpose(1, 2, 0, 3).reshape(6, width)
        sums = jnp.concatenate(
            [sums, parts[0][width:], parts[2][width:], small[:, 3:5].reshape(4, width), small[0, 5:6]]
        )
        sums = lax.psum(sums, ("ctx", "fsdp"))
        mine = lambda k: lax.dynamic_slice_in_dim(sums[k], at.row * shard_rows, shard_rows, 0)
        (
            final_gain_grad, final_shift_grad, outer_bias_grad, attn_gain_grad, attn_shift_grad,
            out_bias_grad, query_bias_grad, value_bias_grad,
        ) = map(mine, range(8))
        inner_bias_grad = lax.dynamic_slice_in_dim(
            sums[8:12].reshape(-1), at.row * ff_rows, ff_rows, 0
        )
        total_sq = jnp.sum(sums[12])
    distill_loss = total_sq / (width * valid_count)
    return (
        distill_loss,
        output.reshape(seg_rows, groups, width),
        input_grad.reshape(seg_rows, groups, width),
        query_weight_grad,
        query_bias_grad,
        key_weight_grad,
        value_weight_grad,
        value_bias_grad,
        out_weight_grad,
        out_bias_grad,
        attn_gain_grad,
        attn_shift_grad,
        inner_weight_grad,
        inner_bias_grad,
        outer_weight_grad,
        outer_bias_grad,
        final_gain_grad,
        final_shift_grad,
    )


def solution(mesh):
    states = P("ctx", "fsdp", None)
    matrix = P("fsdp", None)
    vector = P("fsdp")
    placed = (
        states, states, vector,
        matrix, vector, matrix, matrix, vector, matrix, vector, vector, vector,
        matrix, vector, matrix, vector, vector, vector,
    )
    return jax.shard_map(
        shards,
        mesh=mesh,
        in_specs=placed,
        out_specs=(P(), states, states) + placed[3:],
        check_vma=False,
    )
```

```python
from functools import partial
import math

import jax
import jax.numpy as jnp
from jax import lax
from jax.experimental import pallas as pl
from jax.experimental.pallas import tpu as pltpu
from jax.sharding import PartitionSpec as P

H = 12
head_size = 64
head_splits = 4
group_heads = H // head_splits
group_cols = group_heads * head_size
pack_cols = 3 * group_cols
padded_cols = 640
norm_eps = 1e-12
log_two = math.log(2.0)
masked_score = -1e30
low_type = jnp.bfloat16
wide_type = jnp.float32
score_scale = 1.0 / (log_two * math.sqrt(head_size))
some_vmem, most_vmem = 24 << 20, 58 << 20

plain_dims = (((1,), (0,)), ((), ()))
back_dims = (((1,), (1,)), ((), ()))
weight_dims = (((0,), (0,)), ((), ()))

in_smem = pl.BlockSpec(memory_space=pltpu.SMEM)
in_vmem = pl.BlockSpec(memory_space=pltpu.VMEM)
in_any = pl.BlockSpec(memory_space=pl.ANY)


def product(left_op, right_op, dims=plain_dims):
    return lax.dot_general(left_op, right_op, dims, preferred_element_type=wide_type)


def lanes_of(shape):
    return lax.broadcasted_iota(jnp.int32, shape, 1)


def compiled(name, vmem=some_vmem):
    return dict(
        name=name,
        cost_estimate=pl.CostEstimate(flops=1, bytes_accessed=1, transcendentals=0),
        compiler_params=pltpu.CompilerParams(vmem_limit_bytes=vmem),
    )


class Sum:
    def __init__(self, keep, got):
        self.keep, self.got = keep, got

    def close(self):
        return (self.keep.astype(wide_type) + self.got.astype(wide_type)).astype(low_type)


class Order:
    def __init__(self, place):
        self.place, self.last = place, []

    def next(self, *others):
        names = self.last + [(other, "got") for other in others]
        values = [getattr(owner, name) for owner, name in names]
        place, *values = lax.optimization_barrier((self.place, *values))
        for (owner, name), value in zip(names, values):
            setattr(owner, name, value)
        return place

    def did(self, owner, name="keep"):
        self.last = [(owner, name)]


def low_array(*shape):
    return jax.ShapeDtypeStruct(shape, low_type)


def wide_array(*shape):
    return jax.ShapeDtypeStruct(shape, wide_type)


def head_front(tile, head):
    begin = head // 2 * 128
    if begin + 128 <= tile.shape[1]:
        part = tile[:, begin : begin + 128]
        if head % 2:
            part = pltpu.roll(part, 64, 1)
    else:
        part = jnp.concatenate([tile[:, begin:], jnp.zeros_like(tile[:, begin:])], axis=1)
    return jnp.where(lanes_of(part.shape) < 64, part, 0.0)


def head_rear(tile, head):
    begin = head // 2 * 128
    if begin + 128 <= tile.shape[1]:
        part = tile[:, begin : begin + 128]
        if head % 2 == 0:
            part = pltpu.roll(part, 64, 1)
    else:
        part = jnp.concatenate([jnp.zeros_like(tile[:, begin:]), tile[:, begin:]], axis=1)
    return jnp.where(lanes_of(part.shape) >= 64, part, 0.0)


(at_row, at_core, at_x, at_z, at_group, at_ring, at_first, at_length, at_near, at_mine, at_other) = range(11)


def pack_kernel(place_ref, q_ref, k_ref, v_ref, all_ref, own_ref, half_ref):
    rows = q_ref.shape[0]
    for group in range(head_splits):
        part = pl.ds(group * rows, rows)
        for head in range(group_heads):
            begin = (group * group_heads + head) * head_size
            all_ref[part, head * 128 : head * 128 + 64] = k_ref[:, begin : begin + head_size]
            all_ref[part, head * 128 + 64 : head * 128 + 128] = v_ref[:, begin : begin + head_size]
        all_ref[part, 2 * group_cols : pack_cols] = q_ref[:, group * group_cols : (group + 1) * group_cols]
        all_ref[part, pack_cols:] = jnp.zeros((rows, padded_cols - pack_cols), low_type)
    start = place_ref[at_group] * rows
    own_ref[...] = all_ref[pl.ds(pl.multiple_of(start, rows), rows), :pack_cols]
    start = start + place_ref[at_mine] * (rows // 2)
    half_ref[...] = all_ref[pl.ds(pl.multiple_of(start, rows // 2), rows // 2), :pack_cols]


def pack_weights(place, query_weight, key_weight, value_weight):
    rows = query_weight.shape[0]
    return pl.pallas_call(
        pack_kernel,
        in_specs=[in_smem] + [in_vmem] * 3,
        out_specs=[in_vmem] * 3,
        out_shape=[
            low_array(head_splits * rows, padded_cols),
            low_array(rows, pack_cols),
            low_array(rows // 2, pack_cols),
        ],
        **compiled("pack_weights", most_vmem),
    )(place, query_weight, key_weight, value_weight)


def whole_vector(place_ref, own_ref, other_ref, begin, size):
    own = own_ref[:, begin : begin + size].astype(wide_type)
    other = other_ref[:, begin : begin + size].astype(wide_type)
    first = place_ref[at_near] == 0
    return jnp.concatenate([jnp.where(first, own, other), jnp.where(first, other, own)], axis=1)


def ship_kernel(place_ref, out_ref, inner_ref, outer_ref, ship_ref, sems):
    width = out_ref.shape[1]
    copies = []
    start = 0

    def send(ref, cols):
        nonlocal start
        half = ref.shape[0] // 2
        source = ref.at[pl.ds(pl.multiple_of(place_ref[at_mine] * half, half), half), cols]
        copies.append(
            pltpu.make_async_copy(source, ship_ref.at[pl.ds(start, half), :], sems.at[len(copies)])
        )
        copies[-1].start()
        start += half

    send(outer_ref, pl.ds(0, width))
    for k in range(0, inner_ref.shape[1], width):
        send(inner_ref, pl.ds(k, width))
    send(out_ref, pl.ds(0, width))
    for copy in copies:
        copy.wait()


def shipment(place, weights):
    width = weights[0].shape[1]
    chunks = weights[1].shape[1] // width
    rows = (weights[0].shape[0] + weights[1].shape[0] * chunks + weights[2].shape[0]) // 2
    return pl.pallas_call(
        ship_kernel,
        in_specs=[in_smem] + [in_any] * 3,
        out_specs=in_vmem,
        out_shape=low_array(rows, width),
        scratch_shapes=[pltpu.SemaphoreType.DMA((chunks + 2,))],
        **compiled("shipment", most_vmem),
    )(place, *weights)


def project_kernel(place_ref, x0, x1, x2, x3, own_ref, mine_ref, rest_ref, near_ref, far_ref, q_ref, kv_ref, other_ref):
    half = own_ref.shape[0]
    rows = x0.shape[0]
    near = pl.multiple_of(place_ref[at_near] * half, 128)
    far = pl.multiple_of((1 - place_ref[at_near]) * half, 128)
    kv_cols = 2 * group_cols
    for fetched, core in ((mine_ref, place_ref[at_mine]), (rest_ref, 1 - place_ref[at_mine])):
        other_ref[pl.ds(pl.multiple_of(core * (half // 2), half // 2), half // 2), :] = fetched[...]
    biases = [whole_vector(place_ref, near_ref, far_ref, k * half, half) for k in range(2)]
    q_bias, v_bias = [jnp.zeros((1, group_cols), wide_type)] * 2
    for group in range(head_splits):
        cols = slice(group * group_cols, (group + 1) * group_cols)
        q_bias = jnp.where(place_ref[at_group] == group, biases[0][:, cols], q_bias)
        v_bias = jnp.where(place_ref[at_group] == group, biases[1][:, cols], v_bias)
    kv_bias = []
    for head in range(group_heads):
        kv_bias += [jnp.zeros((1, head_size), wide_type), v_bias[:, head * 64 : head * 64 + 64]]
    bias = jnp.concatenate(kv_bias + [q_bias], axis=1)
    for k, x_ref in enumerate((x0, x1, x2, x3)):
        part = pl.ds(k * rows, rows)
        made = product(x_ref[:, pl.ds(near, half)], own_ref[...])
        made = made + product(x_ref[:, pl.ds(far, half)], other_ref[...]) + bias
        kv_ref[part, :] = made[:, :kv_cols].astype(low_type)
        q_ref[part, :] = (made[:, kv_cols:] * score_scale).astype(low_type)


def project(place, blocks, own, mine, rest, vectors):
    rows, width = blocks[0].shape
    line = rows * head_splits
    return pl.pallas_call(
        project_kernel,
        in_specs=[in_smem] + [in_vmem] * 9,
        out_specs=[in_vmem] * 2,
        out_shape=[low_array(line, group_cols), low_array(line, 2 * group_cols)],
        scratch_shapes=[pltpu.VMEM(own.shape, low_type)],
        **compiled("project", most_vmem),
    )(place, *blocks, own, mine, rest, *vectors)


def attend_kernel(starts, resumed, finished, place_ref, q_ref, *refs):
    pieces = len(starts)
    kv_refs, aug_ref = refs[:pieces], refs[pieces]
    refs = refs[pieces + 1 :]
    state_ref, out_refs = (refs[0], refs[1:]) if resumed else (None, refs)
    rows = q_ref.shape[0]
    joints = [[]]
    for k, kv_ref in enumerate(kv_refs):
        if sum(kv_refs[n].shape[0] for n in joints[-1]) + kv_ref.shape[0] > 2048:
            joints.append([])
        joints[-1].append(k)
    lane = lanes_of((rows, 128))
    q_aug = jnp.where(lane == 0, 1.0, 0.0).astype(low_type)
    stats = jnp.zeros((rows, 128), wide_type)
    q_wide = q_ref[...].astype(wide_type)
    outs = []
    for head in range(group_heads):
        cols = pl.ds(head * 128, 128)
        q_ext = jnp.concatenate([head_front(q_wide, head).astype(low_type), q_aug], axis=1)
        top = None
        if resumed:
            accum = state_ref[:, cols]
            total, top = accum[:, 0:1], accum[:, 1:2]
        for joint in joints:
            kv_ext = jnp.concatenate(
                [
                    jnp.concatenate(
                        [kv_refs[k][:, cols], aug_ref[pl.ds(starts[k], kv_refs[k].shape[0]), :]],
                        axis=1,
                    )
                    for k in joint
                ],
                axis=0,
            )
            scores = product(q_ext, kv_ext, back_dims)
            new_top = jnp.floor(jnp.max(scores, axis=1, keepdims=True))
            if top is not None:
                new_top = jnp.maximum(top, new_top)
            weights = jnp.exp2(scores - new_top).astype(low_type)
            part_sum = product(weights, kv_ext)
            part_total = part_sum[:, 129:130]
            if top is None:
                accum, total = part_sum[:, :128], part_total
            else:
                factor = jnp.exp2(top - new_top)
                accum, total = accum * factor + part_sum[:, :128], total * factor + part_total
            top = new_top
        if finished:
            outs.append(accum / total)
            stats = jnp.where(lane == head, top, stats)
            stats = jnp.where(lane == group_heads + head, total, stats)
        else:
            out_refs[0][:, cols] = jnp.where(lane == 0, total, jnp.where(lane == 1, top, accum))
    if not finished:
        return
    low_refs, wide_ref, stat_ref = out_refs[:head_splits], out_refs[-2], out_refs[-1]
    tiles = []
    for head in range(0, group_heads, 2):
        first = pltpu.roll(outs[head], 64, 1)
        if head + 1 < group_heads:
            tiles.append(jnp.where(lane < 64, first, outs[head + 1]))
        else:
            tiles.append(first[:, :64])
    context = jnp.concatenate(tiles, axis=1)
    wide_ref[...] = context
    stat_ref[...] = stats
    for k, low_ref in enumerate(low_refs):

        @pl.when(pl.program_id(0) == k)
        def _():
            low_ref[...] = context.astype(low_type)


def attend(place, q_line, kv_pieces, order, aug, state, finished):
    line = q_line.shape[0]
    tile = line // head_splits
    whole = lambda i: (0, 0)
    by_tile = lambda i: (i, 0)
    sizes = [piece.shape[0] for piece in kv_pieces]
    used = [kv_pieces[k] for k in order]
    starts = [sum(sizes[:k]) for k in order]
    states = [] if state is None else [state]
    state_cols = 128 * group_heads
    work = line * group_heads * used[0].shape[0] * len(used)
    if finished:
        out_specs = [pl.BlockSpec((tile, group_cols), whole)] * head_splits
        out_specs += [pl.BlockSpec((tile, group_cols), by_tile), pl.BlockSpec((tile, 128), by_tile)]
        out_shape = [low_array(tile, group_cols)] * head_splits
        out_shape += [wide_array(line, group_cols), wide_array(line, 128)]
    else:
        out_specs = pl.BlockSpec((tile, state_cols), by_tile)
        out_shape = wide_array(line, state_cols)
    return pl.pallas_call(
        partial(attend_kernel, starts, state is not None, finished),
        grid=(head_splits,),
        in_specs=[in_smem, pl.BlockSpec((tile, group_cols), by_tile)]
        + [pl.BlockSpec(piece.shape, whole) for piece in used]
        + [pl.BlockSpec(aug.shape, whole)]
        + [pl.BlockSpec((tile, state_cols), by_tile) for _ in states],
        out_specs=out_specs,
        out_shape=out_shape,
        **compiled("attend"),
    )(place, q_line, *used, aug, *states)


def split_three(number):
    first = number.astype(low_type).astype(wide_type)
    second = (number - first).astype(low_type).astype(wide_type)
    return first, second, number - first - second


def attend_back_kernel(head, pieces, first, outs, query_part, place_ref, q_ref, stat_ref, context_ref, g0, g1, g2, g3, *refs):
    kv_refs, aug_ref = refs[:pieces], refs[pieces]
    sum_refs = refs[pieces + 1 : pieces + 1 + outs]
    q_grad_ref, kv_all, q_ext, g_ext = refs[pieces + 1 + outs :]
    rows = q_ref.shape[0]
    query_rows = q_ref.shape[0]
    seg_rows = g0.shape[0]
    step = pl.program_id(0)

    @pl.when(step == 0)
    def _():
        q_grad_ref[...] = jnp.zeros_like(q_grad_ref)
        start = 0
        for kv_ref in kv_refs:
            kv_all[pl.ds(start, kv_ref.shape[0]), :] = kv_ref[...]
            start += kv_ref.shape[0]
        for k, grad_ref in enumerate((g0, g1, g2, g3)):
            part = pl.ds(k * seg_rows, seg_rows)
            lane = lanes_of((seg_rows, 128))
            stats = stat_ref[part, :]
            top = stats[:, head : head + 1]
            total = stats[:, group_heads + head : group_heads + head + 1]
            grad = head_rear(grad_ref[...].astype(wide_type), head)
            context = head_rear(context_ref[part, :], head)
            delta = jnp.sum(grad * context, axis=1, keepdims=True) / total
            q_more = jnp.where(lane == 0, 1.0, 0.0)
            g_more = jnp.zeros((seg_rows, 128), wide_type)
            for place, (of_top, of_delta) in enumerate(zip(split_three(top), split_three(delta))):
                q_more = jnp.where(lane == place + 1, -of_top, q_more)
                g_more = jnp.where(lane == place + 1, -of_delta, g_more)
            q_ext[part, :128] = head_front(q_ref[part, :].astype(wide_type), head).astype(low_type)
            q_ext[part, 128:] = q_more.astype(low_type)
            g_ext[part, :128] = (grad / total).astype(low_type)
            g_ext[part, 128:] = g_more.astype(low_type)

    kv_part = kv_all[pl.ds(pl.multiple_of(step * rows, rows), rows), :]
    aug_part = aug_ref[pl.ds(pl.multiple_of(first + step * rows, rows), rows), :]
    kv_ext = jnp.concatenate([kv_part, aug_part], axis=1)
    keys_turned = jnp.transpose(kv_part)[:64]
    accum = jnp.zeros((rows, 128), wide_type)
    for start in range(0, query_rows, query_part):
        part = pl.ds(start, query_part)
        q_part = q_ext[part, :]
        g_part = g_ext[part, :]
        weights = jnp.exp2(product(kv_ext, q_part, back_dims))
        along_values = product(kv_ext, g_part, back_dims)
        grad_scores = (weights * along_values).astype(low_type)
        accum = accum + product(weights.astype(low_type), g_part[:, :128])
        accum = accum + product(grad_scores, q_part[:, :128])
        q_grad_ref[:, part] += product(keys_turned, grad_scores)
    lane = lanes_of((rows, 128))
    made = (accum * jnp.where(lane < 64, log_two, 1.0)).astype(low_type)

    each = kv_all.shape[0] // rows // outs
    for k, sum_ref in enumerate(sum_refs):

        @pl.when(step // each == k)
        def _():
            sum_ref[...] = made


def attend_back(place, head, q_line, stats, context, grads, kv_pieces, order, outs, aug):
    line = q_line.shape[0]
    sizes = [piece.shape[0] for piece in kv_pieces]
    used = [kv_pieces[k] for k in order]
    length = sum(piece.shape[0] for piece in used)
    each = length // line // outs
    whole = lambda i: (0, 0)
    part_of = lambda k: lambda i: (jnp.clip(i - k * each, 0, each - 1), 0)
    *sums, q_grad = pl.pallas_call(
        partial(
            attend_back_kernel, head, len(used), sum(sizes[: order[0]]), outs, math.gcd(line, 512)
        ),
        grid=(length // line,),
        in_specs=[
            in_smem,
            pl.BlockSpec(q_line.shape, whole),
            pl.BlockSpec(stats.shape, whole),
            pl.BlockSpec(context.shape, whole),
        ]
        + [pl.BlockSpec(grad.shape, whole) for grad in grads]
        + [pl.BlockSpec((piece.shape[0], 128), lambda i: (0, head)) for piece in used]
        + [pl.BlockSpec(aug.shape, whole)],
        out_specs=[pl.BlockSpec((line, 128), part_of(k)) for k in range(outs)]
        + [pl.BlockSpec((head_size, line), whole)],
        out_shape=[low_array(line * each, 128)] * outs + [wide_array(head_size, line)],
        scratch_shapes=[
            pltpu.VMEM((length, 128), low_type),
            pltpu.VMEM((line, 256), low_type),
            pltpu.VMEM((line, 256), low_type),
        ],
        **compiled("attend_back"),
    )(place, q_line, stats, context, *grads, *used, aug)
    return sums, q_grad


def add_pairs_kernel(place_ref, *refs):
    out_ref = refs[-1]
    for k in range(out_ref.shape[0]):
        total = refs[2 * k][...].astype(wide_type) + refs[2 * k + 1][...].astype(wide_type)
        out_ref[k] = total.astype(low_type)


def add_pairs(place, *arrays):
    return pl.pallas_call(
        add_pairs_kernel,
        in_specs=[in_smem] + [in_vmem] * len(arrays),
        out_specs=in_vmem,
        out_shape=low_array(len(arrays) // 2, *arrays[0].shape),
        **compiled("add_pairs"),
    )(place, *arrays)


def add_merge_kernel(place_ref, keep_a, got_a, keep_b, got_b, out_ref):
    start = 0
    for kept, got in ((keep_a, got_a), (keep_b, got_b)):
        rows = kept.shape[1]
        total = kept[...].astype(wide_type) + got[...].astype(wide_type)
        out_ref[:, start : start + rows, :] = total.astype(low_type)
        start += rows


def add_merge(place, keep_a, got_a, keep_b, got_b):
    return pl.pallas_call(
        add_merge_kernel,
        in_specs=[in_smem] + [in_vmem] * 4,
        out_specs=in_vmem,
        out_shape=low_array(2, keep_a.shape[1] + keep_b.shape[1], keep_a.shape[2]),
        **compiled("add_merge"),
    )(place, keep_a, got_a, keep_b, got_b)


def norm_forward(hidden):
    centre = hidden - jnp.mean(hidden, axis=1, keepdims=True)
    inverse = lax.rsqrt(jnp.mean(centre * centre, axis=1, keepdims=True) + norm_eps)
    return centre * inverse, inverse


def norm_back(grad, normal, inverse):
    along = jnp.mean(grad * normal, axis=1, keepdims=True)
    return inverse * (grad - jnp.mean(grad, axis=1, keepdims=True) - normal * along)


def over_tokens(array):
    return jnp.sum(array, axis=0, keepdims=True)


def mid_kernel(place_ref, factor_ref, x_ref, teacher_ref, c0, c1, c2, c3, near_ref, far_ref, *refs):
    own_weights, shipments = refs[0:3], refs[3:5]
    (
        output_ref, sum_ref, d0, d1, d2, d3, act_ref, hidden_ref, normed_ref, branch_ref, attn_ref, small_ref,
        w_out, w_inner, w_outer, slope_ref, sems,
    ) = refs[5:]
    held = (w_out, w_inner, w_outer)
    near, mine = place_ref[at_near], place_ref[at_mine]
    copies = []
    width = x_ref.shape[1]

    def fetch(source, k, start, rows, cols=None):
        target = held[k].at[pl.ds(pl.multiple_of(start, rows), rows), :]
        if cols is not None:
            target = held[k].at[pl.ds(pl.multiple_of(start, rows), rows), cols]
        copies.append(pltpu.make_async_copy(source, target, sems.at[len(copies)]))
        copies[-1].start()

    halves = [weight.shape[0] // 2 for weight in own_weights]
    starts = [
        [(1 - near) * 2 * half + core * half for half in halves] for core in (mine, 1 - mine)
    ]
    out_half, inner_half, outer_half = halves
    chunks = own_weights[1].shape[1] // width
    base = outer_half + chunks * inner_half
    fetch(own_weights[0], 0, near * 2 * out_half, 2 * out_half)
    for ship, (out_start, _, _) in zip(shipments, starts):
        fetch(ship.at[pl.ds(base, out_half), :], 0, out_start, out_half)
    fetch(own_weights[1], 1, near * 2 * inner_half, 2 * inner_half)
    fetch(own_weights[2], 2, near * 2 * outer_half, 2 * outer_half)
    for ship, (_, inner_start, outer_start) in zip(shipments, starts):
        for k in range(chunks):
            source = ship.at[pl.ds(outer_half + k * inner_half, inner_half), :]
            fetch(source, 1, inner_start, inner_half, pl.ds(k * width, width))
        fetch(ship.at[pl.ds(0, outer_half), :], 2, outer_start, outer_half)
    rows = x_ref.shape[0]
    half = width // 2
    vector = lambda k, size: whole_vector(place_ref, near_ref, far_ref, k * half, size)
    b_out, g_attn, s_attn, b_outer, g_final, s_final = (vector(k, half) for k in range(2, 8))
    b_inner = vector(8, w_outer.shape[0] // 2)
    group = place_ref[at_group]
    of_group = lambda k: pl.ds(pl.multiple_of((group ^ k) * group_cols, group_cols), group_cols)

    for copy in copies[0:3]:
        copy.wait()
    hidden = x_ref[...].astype(wide_type) + b_out
    for k, c_ref in enumerate((c0, c1, c2, c3)):
        hidden = hidden + product(c_ref[...], w_out[of_group(k), :])
    attn_normal, attn_inverse = norm_forward(hidden)
    normed = attn_normal * g_attn + s_attn
    normed_low = normed.astype(low_type)
    normed_ref[...] = normed_low
    for copy in copies[3:]:
        copy.wait()
    branch = normed + b_outer
    for k in range(chunks):
        cols = pl.ds(k * width, width)
        pre = product(normed_low, w_inner[:, cols]) + b_inner[:, k * width : (k + 1) * width]
        bell = 0.5 * (1.0 + lax.erf(pre * math.sqrt(0.5)))
        slope_ref[:, cols] = bell + pre * jnp.exp(-0.5 * pre * pre) * (1.0 / math.sqrt(2.0 * math.pi))
        act = (pre * bell).astype(low_type)
        act_ref[:, cols] = act
        branch = branch + product(act, w_outer[cols, :])
    final_normal, final_inverse = norm_forward(branch)
    output = final_normal * g_final + s_final
    output_ref[:, 0, :] = output
    token = place_ref[at_first] + lax.broadcasted_iota(jnp.int32, (rows, 1), 0)
    valid = (token < place_ref[at_length]).astype(wide_type)
    mismatch = (output - teacher_ref[...].astype(wide_type)) * valid
    squares = over_tokens(mismatch * mismatch)
    grad_out = mismatch * factor_ref[0]
    final_gain_grad = over_tokens(grad_out * final_normal)
    final_shift_grad = over_tokens(grad_out)
    grad_mid = norm_back(grad_out * g_final, final_normal, final_inverse)
    grad_branch = grad_mid.astype(low_type)
    branch_ref[...] = grad_branch
    outer_bias_grad = over_tokens(grad_branch.astype(wide_type))
    grad_normed = grad_mid
    inner_bias_grad = []
    for k in range(chunks):
        cols = pl.ds(k * width, width)
        grad_act = product(grad_branch, w_outer[cols, :], back_dims)
        grad_hidden = (grad_act * slope_ref[:, cols]).astype(low_type)
        hidden_ref[:, cols] = grad_hidden
        inner_bias_grad.append(over_tokens(grad_hidden.astype(wide_type)))
        grad_normed = grad_normed + product(grad_hidden, w_inner[:, cols], back_dims)
    attn_gain_grad = over_tokens(grad_normed * attn_normal)
    attn_shift_grad = over_tokens(grad_normed)
    grad_sum = norm_back(grad_normed * g_attn, attn_normal, attn_inverse)
    sum_ref[...] = grad_sum
    grad_attn = grad_sum.astype(low_type)
    attn_ref[...] = grad_attn
    out_bias_grad = over_tokens(grad_attn.astype(wide_type))
    for k, d_ref in enumerate((d0, d1, d2, d3)):
        d_ref[...] = product(grad_attn, w_out[of_group(k), :], back_dims).astype(low_type)
    pairs = (
        (final_gain_grad, final_shift_grad),
        (outer_bias_grad, attn_gain_grad),
        (attn_shift_grad, out_bias_grad),
    )
    for side in range(2):
        cols = slice(side * half, side * half + half)
        lines = [jnp.concatenate([a[:, cols], b[:, cols]], axis=1) for a, b in pairs]
        lines += inner_bias_grad[side * 2 : side * 2 + 2] + [squares]
        lines.append(jnp.zeros((8 - len(lines), width), wide_type))
        small_ref[side] = jnp.concatenate(lines, axis=0)


def middle(place, factor, tokens, teacher, contexts, vectors, weights):
    rows, width = tokens.shape
    ff_width = weights[1].shape[1]
    return pl.pallas_call(
        mid_kernel,
        in_specs=[in_smem, in_smem] + [in_vmem] * 8 + [in_any] * 5,
        out_specs=[in_vmem] * 12,
        out_shape=[wide_array(rows, 1, width), wide_array(rows, width)]
        + [low_array(rows, group_cols)] * 4
        + [low_array(rows, ff_width)] * 2
        + [low_array(rows, width)] * 3
        + [wide_array(2, 8, width)],
        scratch_shapes=[
            pltpu.VMEM((width, width), low_type),
            pltpu.VMEM((width, ff_width), low_type),
            pltpu.VMEM((ff_width, width), low_type),
            pltpu.VMEM((rows, ff_width), wide_type),
            pltpu.SemaphoreType.DMA((5 + 2 * (1 + ff_width // width),)),
        ],
        **compiled("middle", most_vmem),
    )(place, factor, tokens, teacher, *contexts, *vectors, *weights)


def weight_kernel(
    place_ref, act_ref, branch_ref, normed_ref, hidden_ref, c0, c1, c2, c3, attn_ref, small_ref,
    give_a, keep_a, give_b, keep_b, out_grad,
):
    width = branch_ref.shape[1]
    half = width // 2
    group = place_ref[at_group]

    @pl.when((pl.program_id(0) == 0) & (pl.program_id(1) == 0))
    def _():
        for k, c_ref in enumerate((c0, c1, c2, c3)):
            part = pl.ds(pl.multiple_of((group ^ k) * group_cols, group_cols), group_cols)
            out_grad[part, :] = product(c_ref[...], attn_ref[...], weight_dims)

    row = place_ref[at_row] ^ pl.program_id(0)
    x = place_ref[at_x] ^ pl.program_id(1)
    for far, a_ref, b_ref in ((1, give_a, give_b), (0, keep_a, keep_b)):
        core = place_ref[at_core] ^ far
        begin = pl.multiple_of(((row * 2 + core) * 2 + x) * half, 128)
        outer = product(
            act_ref[:, pl.ds(begin, half)], branch_ref[...], weight_dims
        ).astype(low_type)
        inner = product(
            normed_ref[:, pl.ds(pl.multiple_of(row * half, 128), half)],
            hidden_ref[:, pl.ds(pl.multiple_of((core * 2 + x) * width, 128), width)],
            weight_dims,
        ).astype(low_type)
        base = row * half + core * (half // 2) + x * (half // 4)
        for z in range(4):
            apart = place_ref[at_z] ^ z
            low, high = pl.ds(apart & 1, 1), pl.ds(apart >> 1, 1)
            rows = slice(z * 96, z * 96 + 96)
            shaped = lambda block: block[None, None, None, None]
            a_ref[0:1, low, 0:1, high, :, :] = shaped(outer[rows])
            rest = out_grad[pl.ds(pl.multiple_of(base + z * 24, 8), 24), :]
            rest = jnp.concatenate([rest, small_ref[pl.ds(row, 1)][0]], axis=0).astype(low_type)
            b_ref[0:1, 0:1, low, high, :, :] = shaped(jnp.concatenate([inner[rows], rest], axis=0))


def weight_grads(place, act, branch, normed, hidden, contexts, attn, small):
    rows, width = branch.shape
    a_shape, b_shape = (2, 2, 2, 2, 96, width), (2, 2, 2, 2, 128, width)
    a_spec = pl.BlockSpec((1, 2, 1, 2, 96, width), lambda i, j: (i, 0, j, 0, 0, 0))
    b_spec = pl.BlockSpec((1, 1, 2, 2, 128, width), lambda i, j: (j, i, 0, 0, 0, 0))
    return pl.pallas_call(
        weight_kernel,
        grid=(2, 2),
        in_specs=[in_smem] + [in_vmem] * 10,
        out_specs=[a_spec, a_spec, b_spec, b_spec],
        out_shape=[low_array(*a_shape)] * 2 + [low_array(*b_shape)] * 2,
        scratch_shapes=[pltpu.VMEM((width, width), wide_type)],
        **compiled("weight_grads", most_vmem),
    )(place, act, branch, normed, hidden, *contexts, attn, small)


def add_split_kernel(gots, place_ref, kept_ref, *refs):
    got_refs, keep_ref, give_refs = refs[:gots], refs[gots], refs[gots + 1 :]
    got = [got_refs[0][0], got_refs[0][1]] if gots == 1 else [got_ref[...] for got_ref in got_refs]
    total = [
        (kept_ref[k].astype(wide_type) + got[k].astype(wide_type)).astype(low_type) for k in range(2)
    ]
    keep_ref[...] = total[0]
    rows = give_refs[0].shape[0]
    for k, give_ref in enumerate(give_refs):
        give_ref[...] = total[1][k * rows : (k + 1) * rows]


def add_split(place, kept, got, parts=1):
    cols = kept.shape[-1]
    shape = (2, kept.size // cols // 2, cols)
    if isinstance(got, list):
        gots = [array.reshape(shape[1:]) for array in got]
    else:
        gots = [got.reshape(shape)]
    keep, *gives = pl.pallas_call(
        partial(add_split_kernel, len(gots)),
        in_specs=[in_smem] + [in_vmem] * (1 + len(gots)),
        out_specs=[in_vmem] * (1 + parts),
        out_shape=[low_array(*shape[1:])] + [low_array(shape[1] // parts, cols)] * parts,
        **compiled("add_split"),
    )(place, kept.reshape(shape), *gots)
    gives = [give.reshape(kept.shape[1:]) if parts == 1 else give for give in gives]
    return keep.reshape(kept.shape[1:]), gives


def unpack_kernel(
    place_ref, own_a, got_a, own_b, got_b, outer_ref, inner_ref, out_ref, wide_a, wide_b, sems
):
    width = own_a.shape[-1]
    half = width // 2
    copies = []

    def send(source, target):
        copy = pltpu.make_async_copy(source, target, sems.at[len(copies)])
        copy.start()
        copies.append(copy)

    for k in range(16):
        core = place_ref[at_core] ^ (k // 8)
        x = place_ref[at_x] ^ (k // 4 % 2)
        z = place_ref[at_z] ^ (k // 2 % 2 + 2 * (k % 2))
        a_ref, b_ref = (got_a, got_b) if k // 8 else (own_a, own_b)
        wide_a[k] = a_ref[k // 4 % 2, k // 2 % 2, k % 2].astype(wide_type)
        start = pl.multiple_of((core * 2 + x) * half + z * 96, 32)
        send(wide_a.at[k], outer_ref.at[pl.ds(start, 96), :])
        wide_b[k] = b_ref[k // 2 % 2, k // 4 % 2, k % 2].astype(wide_type)
        cols = pl.ds(pl.multiple_of((core * 2 + x) * width, 128), width)
        send(wide_b.at[k, 0:96], inner_ref.at[pl.ds(pl.multiple_of(z * 96, 32), 96), cols])
        start = pl.multiple_of(core * (half // 2) + x * (half // 4) + z * 24, 8)
        send(wide_b.at[k, 96:120], out_ref.at[pl.ds(start, 24), :])
    for copy in copies:
        copy.wait()


def unpack(place, own_a, got_a, own_b, got_b):
    width = own_a.shape[-1]
    return pl.pallas_call(
        unpack_kernel,
        in_specs=[in_smem] + [in_vmem] * 4,
        out_specs=[in_any] * 3,
        out_shape=[
            wide_array(2 * width, width), wide_array(width // 2, 4 * width), wide_array(width // 2, width)
        ],
        scratch_shapes=[
            pltpu.VMEM((16, own_a.shape[-2], width), wide_type),
            pltpu.VMEM((16, own_b.shape[-2], width), wide_type),
            pltpu.SemaphoreType.DMA((48,)),
        ],
        **compiled("unpack"),
    )(place, own_a, got_a, own_b, got_b)


def rows_kernel(counts, terms, place_ref, *refs):
    heads, used = len(counts), sum(counts)
    q_grads, kv_terms = refs[:used], refs[used : used + sum(terms)]
    refs = refs[used + sum(terms) :]
    blocks = refs[:4]
    r0, r1, r2, r3, give0, give1, keep0, keep1, w_grad, all_rows = refs[4:]
    rows, width = blocks[0].shape
    kv_cols = 2 * group_cols
    for k in range(heads):
        total = 0.0
        for n in range(sum(terms[:k]), sum(terms[: k + 1])):
            term = kv_terms[n]
            total = total + (term[...] if len(term.shape) == 2 else term[k]).astype(wide_type)
        all_rows[:, k * 128 : k * 128 + 128] = total.astype(low_type)
    firsts = [sum(counts[:k]) for k in range(heads)]
    turned = [
        sum((ref[...] for ref in q_grads[first + 1 : first + count]), q_grads[first][...])
        for first, count in zip(firsts, counts)
    ]
    turned = jnp.concatenate(turned, axis=0) * 0.125
    all_rows[:, kv_cols:] = jnp.transpose(turned).astype(low_type)
    half = width // 2
    bias = jnp.zeros((1, pack_cols), wide_type)
    for k, r_ref in enumerate((r0, r1, r2, r3)):
        made = all_rows[pl.ds(k * rows, rows), :]
        r_ref[...] = made
        bias = bias + over_tokens(made.astype(wide_type))
        for side in range(2):
            part = product(blocks[k][:, side * half : side * half + half], made, weight_dims)
            if k:
                w_grad[side] += part
            else:
                w_grad[side] = part
    bias = jnp.concatenate([bias, jnp.zeros((15, pack_cols), wide_type)], axis=0)
    for far, piece_refs in ((1, (give0, give1)), (0, (keep0, keep1))):
        start = pl.multiple_of((place_ref[at_core] ^ far) * (half // 2), half // 2)
        for j in range(2):
            row = place_ref[at_row] ^ j
            block = w_grad[pl.ds(row, 1), pl.ds(start, half // 2), :][0]
            piece_refs[j][...] = jnp.concatenate([block, bias], axis=0).astype(low_type)


def project_back(place, q_grads, kv_terms, blocks):
    counts = [len(q_grad) for q_grad in q_grads]
    terms = [len(head) for head in kv_terms]
    every = [array for head in q_grads + kv_terms for array in head]
    rows, width = blocks[0].shape
    pieces = (width // 4 + 16, pack_cols)
    return pl.pallas_call(
        partial(rows_kernel, counts, terms),
        in_specs=[in_smem] + [in_vmem] * (len(every) + 4),
        out_specs=[in_vmem] * 8,
        out_shape=[low_array(rows, pack_cols)] * 4 + [low_array(*pieces)] * 4,
        scratch_shapes=[
            pltpu.VMEM((2, width // 2, pack_cols), wide_type),
            pltpu.VMEM((4 * rows, pack_cols), low_type),
        ],
        **compiled("project_back"),
    )(place, *every, *blocks)


def input_kernel(place_ref, sum_ref, r0, r1, r2, r3, own_ref, mine_ref, other_ref, grad_ref):
    half = own_ref.shape[0] // head_splits
    near = jnp.zeros((sum_ref.shape[0], half), wide_type)
    far = jnp.zeros((sum_ref.shape[0], half), wide_type)
    for k, r_ref in enumerate((r0, r1, r2, r3)):
        group = place_ref[at_group] ^ k
        near = near + product(r_ref[...], own_ref[pl.ds(pl.multiple_of(group * half, half), half), :pack_cols], back_dims)
        fetched = (group >> 1) == place_ref[at_mine]
        side = pl.ds(pl.multiple_of((group & 1) * half, half), half)
        weight = jnp.where(fetched, mine_ref[side, :pack_cols], other_ref[side, :pack_cols])
        far = far + product(r_ref[...], weight, back_dims)
    for part, begin in ((near, place_ref[at_near]), (far, 1 - place_ref[at_near])):
        cols = pl.ds(pl.multiple_of(begin * half, 128), half)
        grad_ref[:, 0, cols] = sum_ref[:, cols] + part


def input_back(place, grad_sum, rows, packs):
    return pl.pallas_call(
        input_kernel,
        in_specs=[in_smem] + [in_vmem] * 8,
        out_specs=in_vmem,
        out_shape=wide_array(grad_sum.shape[0], 1, grad_sum.shape[1]),
        **compiled("input_back"),
    )(place, grad_sum, *rows, *packs)


def qkv_unpack_kernel(place_ref, here_ref, there_ref, q_ref, k_ref, v_ref, bias_ref):
    side = q_ref.shape[0] // 2
    bias_ref[...] = jnp.zeros_like(bias_ref)
    for own in range(head_splits):

        @pl.when(place_ref[at_group] == own)
        def _():
            for n, piece in enumerate((here_ref, there_ref)):
                part = pl.ds(pl.multiple_of((place_ref[at_core] ^ n) * side, side), side)
                for k in range(head_splits):
                    first = (own ^ k) * group_cols
                    block = piece[k].astype(wide_type)
                    q_ref[part, first : first + group_cols] = block[:side, 2 * group_cols :]
                    for h in range(group_heads):
                        begin = first + h * head_size
                        keys = slice(h * 128, h * 128 + 64)
                        values = slice(h * 128 + 64, h * 128 + 128)
                        k_ref[part, begin : begin + head_size] = block[:side, keys]
                        v_ref[part, begin : begin + head_size] = block[:side, values]
                        if n == 0:
                            bias_ref[1:2, begin : begin + head_size] = block[side : side + 1, values]
                    if n == 0:
                        bias_ref[0:1, first : first + group_cols] = block[
                            side : side + 1, 2 * group_cols :
                        ]


def qkv_unpack(place, here, there, width):
    return pl.pallas_call(
        qkv_unpack_kernel,
        in_specs=[in_smem] + [in_vmem] * 2,
        out_specs=[in_vmem] * 4,
        out_shape=[wide_array(width // 2, width)] * 3 + [wide_array(8, width)],
        **compiled("qkv_unpack"),
    )(place, here, there)


class Layout:
    def __init__(self):
        self.ctx = lax.axis_size("ctx")
        self.fsdp = lax.axis_size("fsdp")
        self.me = lax.axis_index("ctx")
        self.row = lax.axis_index("fsdp")
        self.fast = self.ctx == 16 and self.fsdp == 2
        group_bits = (2, 4) if self.fast else (self.ctx // 4, self.ctx // 2)
        bits = [1 << k for k in reversed(range(self.ctx.bit_length() - 1))]
        self.ring_bits = [bit for bit in bits if bit not in group_bits]
        self.group = self.bit(group_bits[0]) + 2 * self.bit(group_bits[1])
        self.group_codes = [0, group_bits[0], group_bits[1], group_bits[0] | group_bits[1]]
        self.ring_codes = [0]
        for bit in self.ring_bits:
            self.ring_codes = self.ring_codes + [code | bit for code in self.ring_codes]

    def bit(self, bit):
        return (self.me // bit) % 2

    def swap(self, block, code):
        return lax.ppermute(block, "ctx", [(i, i ^ code) for i in range(self.ctx)])

    def groups(self, blocks):
        return [blocks[0]] + [self.swap(blocks[k], self.group_codes[k]) for k in range(1, 4)]

    def across(self, block):
        return lax.ppermute(block, "fsdp", [(0, 1), (1, 0)])


def shards(
    layer_input,
    teacher_states,
    seq_lengths,
    query_weight,
    query_bias,
    key_weight,
    value_weight,
    value_bias,
    out_weight,
    out_bias,
    attn_gain,
    attn_shift,
    inner_weight,
    inner_bias,
    outer_weight,
    outer_bias,
    final_gain,
    final_shift,
):
    at = Layout()
    seg_rows, groups, width = layer_input.shape
    shard_rows = query_weight.shape[0]
    ff_rows = outer_weight.shape[0]
    ff_width = inner_weight.shape[1]
    tokens = layer_input.reshape(seg_rows, width)
    teacher = teacher_states.reshape(seg_rows, width)
    two_rows = at.fsdp == 2
    place = jnp.stack(
        [
            at.row, at.bit(1), at.bit(2), at.bit(4) + 2 * at.bit(8), at.group, at.bit(8),
            at.me * seg_rows, seq_lengths[0],
            at.row if two_rows else 0, at.bit(1), 0,
        ]
    ).astype(jnp.int32)

    blocks = at.groups([tokens] * 4)
    all_pack, own_pack, half_pack = pack_weights(place, query_weight, key_weight, value_weight)
    if two_rows:
        mine_part = at.across(half_pack)
    else:
        full = lax.all_gather(own_pack, "fsdp", axis=0, tiled=True)
        own_pack, far = full[: width // 2], full[width // 2 :]
        mine_part = lax.dynamic_slice_in_dim(far, at.bit(1) * (width // 4), width // 4, 0)
    rest_part = at.swap(mine_part, 1)
    vectors = (
        query_bias, value_bias, out_bias, attn_gain, attn_shift,
        outer_bias, final_gain, final_shift, inner_bias,
    )
    if two_rows:
        *vectors, own_pack = lax.optimization_barrier((*vectors, own_pack))
        own_vectors = jnp.concatenate(vectors).reshape(1, -1)
        vectors = (own_vectors, at.across(own_vectors))
    else:
        whole = lambda vector: lax.all_gather(vector, "fsdp", axis=0, tiled=True).reshape(2, -1)
        both = jnp.concatenate([whole(vector) for vector in vectors], axis=1)
        vectors = (both[:1], both[1:])
    own_count = jnp.sum(seq_lengths).astype(wide_type)
    weights = [out_weight, inner_weight, outer_weight]
    if two_rows:
        valid_count = own_count + at.across(own_count.reshape(1))[0]
        ship, rest_part, vectors, blocks, valid_count = lax.optimization_barrier(
            (shipment(place, weights), rest_part, vectors, blocks, valid_count)
        )
        ship = at.across(ship)
    q_line, kv_line = project(place, blocks, own_pack, mine_part, rest_part, vectors)
    if not two_rows:
        valid_count = lax.psum(own_count, "fsdp")

    source = jnp.stack(
        [at.me ^ (ring | group) for ring in at.ring_codes for group in at.group_codes]
    )
    position = (source[:, None] * seg_rows + jnp.arange(seg_rows)[None, :]).reshape(-1, 1)
    lane = lax.broadcasted_iota(jnp.int32, (position.shape[0], 128), 1)
    mask = jnp.where(position < seq_lengths[0], 0.0, masked_score)
    aug = jnp.where(lane == 0, mask, jnp.where(lane < 4, 1.0, 0.0)).astype(low_type)

    if at.fast:
        near = at.swap(kv_line, 1)
        far = at.swap(kv_line, 8)
        state = attend(place, q_line, [kv_line, far, near, far], (0, 2), aug, None, False)
        far, state = lax.optimization_barrier((far, state))
        kv_pieces = [kv_line, far, near, at.swap(far, 1)]
        order = (1, 3)
    else:
        kv_pieces = [kv_line]
        for bit in at.ring_bits:
            kv_pieces = kv_pieces + [at.swap(piece, bit) for piece in kv_pieces]
        state, order = None, tuple(range(len(kv_pieces)))
    *context_low, context, stats = attend(place, q_line, kv_pieces, order, aug, state, True)
    if two_rows:
        ship, stats = lax.optimization_barrier((ship, stats))
        weights += [ship, at.swap(ship, 1)]
    else:
        full = [lax.all_gather(weight, "fsdp", axis=0, tiled=True) for weight in weights]
        far = [weight[weight.shape[0] // 2 :] for weight in full]
        weights = [weight[: weight.shape[0] // 2] for weight in full]
        ship = shipment(place, far)
        weights += [ship, at.swap(ship, 1)]
    contexts = at.groups(context_low)
    token_total = seg_rows * groups * at.ctx * at.fsdp
    factor = (2.0 * token_total / valid_count).reshape(1)
    output, grad_sum, g0, g1, g2, g3, act, hidden, normed, branch, attn, small = middle(
        place, factor, tokens, teacher, contexts, vectors, weights
    )
    if two_rows:
        half = all_pack.shape[0] // 2
        mine_pack = lax.dynamic_slice_in_dim(all_pack, at.bit(1) * half, half, 0)
    else:
        by_row = lax.all_gather(all_pack, "fsdp", axis=0, tiled=False)
        by_row = by_row.reshape(at.fsdp, head_splits, shard_rows, padded_cols)
        whole = by_row.transpose(1, 0, 2, 3).reshape(head_splits, width, padded_cols)
        near, far = whole[:, : width // 2], whole[:, width // 2 :]
        flat = lambda pack: pack.reshape(-1, padded_cols)
        mine = lax.dynamic_slice_in_dim(far, at.bit(1) * 2, 2, 0)
        packs = (flat(near), flat(mine), at.swap(flat(mine), 1))
    grads = at.groups([g0, g1, g2, g3])

    over = lambda bit: lambda block: at.swap(block, bit)
    order = Order(place)

    def add(total, shape, move, *others, parts=1):
        total.keep, gives = add_split(
            order.next(*others), total.keep.reshape(shape), total.got, parts
        )
        moved = [move(give) for give in gives]
        total.got = moved[0] if parts == 1 else moved
        order.did(total)

    heads, q_grads = [], []

    def back(*others, split=False):
        args = (len(heads), q_line, stats, context, grads, kv_pieces)
        if split:
            give, first = attend_back(order.next(*others), *args, (2, 3), 2, aug)
            far = Sum(give[1], at.swap(give[1], 1))
            own = Sum(give[0], at.swap(give[0], 1))
            order.did(far)
            keep, second = attend_back(order.next(), *args, (0, 1), 2, aug)
            own.keep, far.keep = keep
            q_grads.append([first, second])
        else:
            sums, first = attend_back(order.next(*others), *args, (0, 1, 2, 3), 4, aug)
            own, far = Sum(sums[0], at.swap(sums[2], 1)), Sum(sums[1], at.swap(sums[3], 1))
            q_grads.append([first])
        order.did(far)
        heads.append((own, far))

    def send_far(*used, needs=()):
        pairs = [array for head in used for array in (heads[head][1].keep, heads[head][1].got)]
        sums = add_pairs(order.next(*needs), *pairs)
        total = Sum(sums, at.swap(sums, 8))
        order.did(total)
        return total

    if at.fast:
        give_a, keep_a, give_b, keep_b = weight_grads(
            place, act, branch, normed, hidden, contexts, attn, small
        )
        give_a, give_b, *grads = lax.optimization_barrier((give_a, give_b, *grads))
        part_a, part_b = Sum(keep_a, at.swap(give_a, 1)), Sum(keep_b, at.swap(give_b, 1))
        shape_a, shape_b = (2, -1, 96, width), (2, -1, 128, width)
        def step(move_a, move_b, parts=1):
            add(part_a, shape_a, move_a, parts=parts)
            add(part_b, shape_b, move_b, parts=parts)

        back()
        step(at.across, over(2))
        back()
        firsts = send_far(0, 1)
        back(split=True)
        step(over(4), at.across, 2)
        lasts = send_far(2, needs=(firsts,))
        step(over(2), over(4))
        lay = lambda part, rows: (part.keep.reshape(2, rows, width), part.got.reshape(2, rows, width))
        both = add_merge(order.next(lasts), *lay(part_a, 96), *lay(part_b, 128))
        both, mine_pack = lax.optimization_barrier((both, mine_pack))
        both = Sum(both, at.swap(both, 8))
        mine_pack = at.across(mine_pack)
        packs = (all_pack, mine_pack, at.swap(mine_pack, 1))
        order.did(both)
        fars = [firsts.got, firsts.got, lasts.got[0]]
        kv_terms = [[own.keep, own.got, far] for (own, _), far in zip(heads, fars)]
        r0, r1, r2, r3, give0, give1, keep0, keep1 = project_back(
            order.next(), q_grads, kv_terms, blocks
        )
        qkv = Sum(keep1, at.swap(give1, 1))
        order.did(qkv)
        rows = at.groups([r0, r1, r2, r3])
        got0 = at.swap(give0, 1)
        (onward,) = add_pairs(order.next(), qkv.keep, qkv.got)
        onward = at.across(onward)
        rows, both.got = lax.optimization_barrier((rows, both.got))
        both.got = jnp.concatenate([both.got[1:], both.got[:1]])
        both = both.close()
        small = both[0, 216:].astype(wide_type)
        own_a, own_b = both[:, :96], both[:, 96:]
        own_a, own_b = Sum(own_a, at.swap(own_a, 4)), Sum(own_b, at.swap(own_b, 2))
        qkv = sum(part.astype(wide_type) for part in (keep0, got0, onward)).astype(low_type)
        qkv = Sum(qkv, at.swap(qkv, 8))

        def joined(own, bit):
            own.keep = jnp.stack([own.keep, own.got])
            own.got = at.swap(own.keep, bit)

        joined(own_a, 2)
        joined(own_b, 4)
        input_grad = input_back(place, grad_sum, rows, packs)
        own_b.got, input_grad = lax.optimization_barrier((own_b.got, input_grad))
        here = at.groups([qkv.close()] * head_splits)
        here = jnp.stack(here)
        there = at.swap(here, 1)
        mine = lambda bias, k: lax.dynamic_slice_in_dim(bias[k], at.row * shard_rows, shard_rows, 0)
        side = (small[:3, :shard_rows], small[:3, shard_rows:], small[3:5].reshape(-1), jnp.sum(small[5]))
        side, own_a.got = lax.optimization_barrier((side, own_a.got))
        left, right, inner_bias_grad, total_sq = side
        final_gain_grad, outer_bias_grad, attn_shift_grad = left
        final_shift_grad, attn_gain_grad, out_bias_grad = right
        joined(own_a, 1)
        joined(own_b, 1)
        outer_weight_grad, inner_weight_grad, out_weight_grad = unpack(
            place, own_a.keep, own_a.got, own_b.keep, own_b.got
        )
        query_weight_grad, key_weight_grad, value_weight_grad, bias = qkv_unpack(
            place, here, there, width
        )
        query_bias_grad, value_bias_grad = mine(bias, 0), mine(bias, 1)
    else:
        kv_terms = []
        every = tuple(range(len(kv_pieces)))
        for head in range(group_heads):
            (keep, give), q_grad = attend_back(
                place, head, q_line, stats, context, grads, kv_pieces, every, 2, aug
            )
            q_grads.append([q_grad])
            total = Sum(keep, at.swap(give, 1))
            for bit in at.ring_bits[-2::-1]:
                add(total, (2, -1, 128), over(bit))
            kv_terms.append([total.keep, total.got])
        r0, r1, r2, r3, *_ = project_back(place, q_grads, kv_terms, blocks)
        rows = at.groups([r0, r1, r2, r3])
        input_grad = input_back(place, grad_sum, rows, packs)
        all_rows = jnp.concatenate([r0, r1, r2, r3])
        line = jnp.concatenate(blocks)

        def summed(partial_sum):
            mine = lax.psum_scatter(partial_sum, "fsdp", scatter_dimension=0, tiled=True)
            return lax.psum(mine, "ctx")

        qkv = product(line, all_rows, weight_dims)
        qkv = jnp.concatenate([qkv, jnp.sum(all_rows, axis=0, dtype=wide_type)[None]])
        qkv = lax.dynamic_update_slice(
            jnp.zeros((width + 1, head_splits, pack_cols), wide_type), qkv[:, None], (0, at.group, 0)
        )
        kv = qkv[:, :, : 2 * group_cols].reshape(width + 1, H, 2, head_size)
        parts = [qkv[:, :, 2 * group_cols :], kv[:, :, 0], kv[:, :, 1]]
        parts = [part.reshape(width + 1, width) for part in parts]
        query_weight_grad, key_weight_grad, value_weight_grad = (
            summed(part[:width]) for part in parts
        )
        outer_weight_grad = summed(product(act, branch, weight_dims))
        inner_weight_grad = summed(product(normed, hidden, weight_dims))
        whole = jnp.zeros((width, width), wide_type)
        for k in range(head_splits):
            whole = lax.dynamic_update_slice_in_dim(
                whole, product(contexts[k], attn, weight_dims), (at.group ^ k) * group_cols, 0
            )
        out_weight_grad = summed(whole)
        sums = small[:, :3].reshape(2, 3, 2, width // 2).transpose(1, 2, 0, 3).reshape(6, width)
        sums = jnp.concatenate(
            [sums, parts[0][width:], parts[2][width:], small[:, 3:5].reshape(4, width), small[0, 5:6]]
        )
        sums = lax.psum(sums, ("ctx", "fsdp"))
        mine = lambda k: lax.dynamic_slice_in_dim(sums[k], at.row * shard_rows, shard_rows, 0)
        (
            final_gain_grad, final_shift_grad, outer_bias_grad, attn_gain_grad, attn_shift_grad,
            out_bias_grad, query_bias_grad, value_bias_grad,
        ) = map(mine, range(8))
        inner_bias_grad = lax.dynamic_slice_in_dim(
            sums[8:12].reshape(-1), at.row * ff_rows, ff_rows, 0
        )
        total_sq = jnp.sum(sums[12])
    distill_loss = total_sq / (width * valid_count)
    return (
        distill_loss,
        output.reshape(seg_rows, groups, width),
        input_grad.reshape(seg_rows, groups, width),
        query_weight_grad,
        query_bias_grad,
        key_weight_grad,
        value_weight_grad,
        value_bias_grad,
        out_weight_grad,
        out_bias_grad,
        attn_gain_grad,
        attn_shift_grad,
        inner_weight_grad,
        inner_bias_grad,
        outer_weight_grad,
        outer_bias_grad,
        final_gain_grad,
        final_shift_grad,
    )


def solution(mesh):
    states = P("ctx", "fsdp", None)
    matrix = P("fsdp", None)
    vector = P("fsdp")
    placed = (
        states, states, vector,
        matrix, vector, matrix, matrix, vector, matrix, vector, vector, vector,
        matrix, vector, matrix, vector, vector, vector,
    )
    return jax.shard_map(
        shards,
        mesh=mesh,
        in_specs=placed,
        out_specs=(P(), states, states) + placed[3:],
        check_vma=False,
    )
```
